32 devices in a mesh: grp: 2 (over y), slab: 8 (over z, x), col: 2 (over core).
Axes of the slice: x: 2, y: 2, z: 4, core: 2. Of those that a mesh axis runs over, the one named last changes fastest.
Arguments:
- states: float32 [4, 64, 128, 1024], P(None, ('grp', 'slab'), 'col'), parts along dimension 1, may hold values from 0 to 1.4, as said below
- cond: float32 [6, 16, 32, 256], P(None, ('grp', 'slab'), 'col'), parts along dimension 1, may hold values from -0.025 to 0.15, as said below
- tension: float32 [32, 64, 512], P(('grp', 'slab'), 'col'), parts along dimension 0, may hold values from 0 to 1
- fiber: int32 [16, 32, 256], P(('grp', 'slab'), 'col'), parts along dimension 0, may hold values from 0 to 63
- disp: float32 [3, 16, 32, 256], P(None, ('grp', 'slab'), 'col'), parts along dimension 1, may hold values from -0.12 to 0.12
Outputs:
- states_next: float32 [4, 64, 128, 1024], P(None, ('grp', 'slab'), 'col'), parts along dimension 1
- tension_next: float32 [32, 64, 512], P(('grp', 'slab'), 'col'), parts along dimension 0
- disp_next: float32 [3, 16, 32, 256], P(None, ('grp', 'slab'), 'col'), parts along dimension 1
- cond_next: float32 [6, 16, 32, 256], P(None, ('grp', 'slab'), 'col'), parts along dimension 1
The draws below stay inside these ranges and needn't reach their ends.
There are 2 independent parts, one for each index of `grp`. The reference program is written for one: setup_inputs(seed, part) draws one part's arguments, and reference() takes and returns one part's arrays. A program takes and returns all parts, laid end to end along the dimension named above; each array names one. Nothing has to cross between parts.
Inputs may be any that keep to these rules, and one draw needn't show every extreme that they name: `states`: component 0 lies in 0 to 1.4, components 1 to 3 in 0 to 1. `cond`: components 0 to 2 lie in 0.05 to 0.15, components 3 to 5 in -0.025 to 0.025.
All inputs are finite; a program needn't handle non-finite values.
Results may differ from the reference program's by a relative error of at most 0.0003.
Values sent between devices are 32-bit elements; how exact they have to be, the bound alone decides.
No kernel may reach another device: no remote copies, remote signals or barrier semaphores. Data moves between devices by JAX's collectives and lax.ppermute only.
A program may use at most 192 MiB of HBM per device.

```python
import jax
import jax.numpy as jnp
from jax import lax

NX = 1024
SUB = 4
MECH_STEPS = 2
NFIB = 64
NZ = 32
NY = 128
TZ = 16
TY = 64
TX = 512
MZ = 8
MY = 32
MX = 256


def draw_states(key, part):
    keys = jax.random.split(key, 1)
    rough = jax.random.uniform(keys[0], (4, NZ, NY, NX), jnp.float32)
    scales = jnp.array([1.4, 1.0, 1.0, 1.0], jnp.float32).reshape(4, 1, 1, 1)
    return rough * scales


def draw_cond(key, part):
    keys = jax.random.split(key, 2)
    diagonal = jax.random.uniform(keys[0], (3, MZ, MY, MX), jnp.float32, 0.05, 0.15)
    cross = jax.random.uniform(keys[1], (3, MZ, MY, MX), jnp.float32, -0.025, 0.025)
    return jnp.concatenate([diagonal, cross], 0)


def set_ends(drawn, own_key, least, top_value):
    place = [jax.random.randint(jax.random.fold_in(own_key, axis), (), 0, length) for axis, length in enumerate(drawn.shape)]
    main_axis = drawn.shape.index(max(drawn.shape))
    beside = place[:main_axis] + [(place[main_axis] + 1) % drawn.shape[main_axis]] + place[main_axis + 1:]
    return drawn.at[tuple(place)].set(least).at[tuple(beside)].set(top_value)


def block_levels(own_key, dims, cuts, low, top_value):
    def one(dim, blocks):
        heights = jax.random.uniform(jax.random.fold_in(jax.random.fold_in(own_key, 6), dim), (blocks,), jnp.float32, low / len(cuts), top_value / len(cuts))
        return jnp.repeat(jnp.exp(heights), dims[dim] // blocks).reshape((-1,) + (1,) * (len(dims) - dim - 1))

    level = one(*cuts[0])
    for cut in cuts[1:]:
        level = level * one(*cut)
    return level


def gaussian(stream_key, shape, scale, most, shards=(), kind=jnp.bfloat16):
    drawn = jax.random.normal(stream_key, shape, jnp.float32) * scale
    if len(shards) > 0:
        drawn = block_levels(stream_key, shape, shards, -0.22, 0.18) * drawn
    return jnp.clip(drawn, min=-most, max=most).astype(kind)


def setup_inputs(seed: int = 0, part: int = 0) -> dict:
    key_of = jax.random.split(jax.random.key(seed), 6)
    own_keys = jax.random.split(jax.random.fold_in(key_of[5], part), 6)
    states = draw_states(jax.random.fold_in(jax.random.fold_in(key_of[5], part), 71), part)
    cond = draw_cond(jax.random.fold_in(jax.random.fold_in(key_of[5], part), 71), part)
    tension = jnp.clip(1.0 * jax.random.uniform(own_keys[2], (TZ, TY, TX), jnp.float32) ** block_levels(own_keys[2], (TZ, TY, TX), ((0, 8), (1, 2)), -0.2, 0.2), 0.0, 1.0)
    fiber = set_ends(jax.random.randint(own_keys[3], (MZ, MY, MX), 0, NFIB), jax.random.fold_in(own_keys[3], 1), 0, NFIB - 1).astype(jnp.int32)
    disp = gaussian(own_keys[4], (3, MZ, MY, MX), 0.03, 0.12, ((1, 8), (2, 2)), jnp.float32)
    return dict(states=states, cond=cond, tension=tension, fiber=fiber, disp=disp)


SHARP = 50.0
STEP_TIME = 0.05
LAME_FIRST = 1.0
SHEAR = 0.5
ACTIVE_GAIN = 0.5
MECH_RATE = 0.15
SIGMA_LONG = 0.16
SIGMA_TRANS = 0.04
SMOOTH_WEIGHTS = (0.125, 0.75, 0.125)
SLOPE_WEIGHTS = (-0.5, 0.0, 0.5)
PAIRS = ((0, 0), (1, 1), (2, 2), (0, 1), (0, 2), (1, 2))


def switch(value):
    return 0.5 * (1.0 + jnp.tanh(SHARP * value))


def ionic_rates(volt, gate_v, gate_w, gate_s):
    high_v = switch(volt - 0.3)
    high_w = switch(volt - 0.13)
    high_o = switch(volt - 0.006)
    tau_vminus = (1.0 - high_o) * 60.0 + high_o * 1150.0
    tau_wminus = 60.0 + (15.0 - 60.0) * 0.5 * (1.0 + jnp.tanh(65.0 * (volt - 0.03)))
    tau_soft = 30.0181 + (0.9957 - 30.0181) * 0.5 * (1.0 + jnp.tanh(2.0458 * (volt - 0.65)))
    tau_slow = (1.0 - high_w) * 2.7342 + high_w * 16.0
    tau_open = (1.0 - high_o) * 400.0 + high_o * 6.0
    v_inf = 1.0 - high_o
    w_inf = (1.0 - high_o) * (1.0 - volt / 0.07) + high_o * 0.94
    fast_current = -gate_v * high_v * (volt - 0.3) * (1.55 - volt) / 0.11
    outward = volt * (1.0 - high_w) / tau_open + high_w / tau_soft
    slow_current = -high_w * gate_w * gate_s / 1.8875
    rate_v = (1.0 - high_v) * (v_inf - gate_v) / tau_vminus - high_v * gate_v / 1.4506
    rate_w = (1.0 - high_w) * (w_inf - gate_w) / tau_wminus - high_w * gate_w / 200.0
    rate_s = (0.5 * (1.0 + jnp.tanh(2.0994 * (volt - 0.9087))) - gate_s) / tau_slow
    return -(fast_current + outward + slow_current), rate_v, rate_w, rate_s


def diffusion(padded, coeff):
    centre = padded[1:-1, 1:-1, 1:-1]
    along_z = padded[2:, 1:-1, 1:-1] + padded[:-2, 1:-1, 1:-1] - 2.0 * centre
    along_y = padded[1:-1, 2:, 1:-1] + padded[1:-1, :-2, 1:-1] - 2.0 * centre
    along_x = padded[1:-1, 1:-1, 2:] + padded[1:-1, 1:-1, :-2] - 2.0 * centre
    cross_zy = 0.25 * (padded[2:, 2:, 1:-1] - padded[2:, :-2, 1:-1] - padded[:-2, 2:, 1:-1] + padded[:-2, :-2, 1:-1])
    cross_zx = 0.25 * (padded[2:, 1:-1, 2:] - padded[2:, 1:-1, :-2] - padded[:-2, 1:-1, 2:] + padded[:-2, 1:-1, :-2])
    cross_yx = 0.25 * (padded[1:-1, 2:, 2:] - padded[1:-1, 2:, :-2] - padded[1:-1, :-2, 2:] + padded[1:-1, :-2, :-2])
    return (coeff[0] * along_z + coeff[1] * along_y + coeff[2] * along_x
            + 2.0 * (coeff[3] * cross_zy + coeff[4] * cross_zx + coeff[5] * cross_yx))


def excite_step(padded, volt, gate_v, gate_w, gate_s, coeff):
    ion, rate_v, rate_w, rate_s = ionic_rates(volt, gate_v, gate_w, gate_s)
    new_volt = volt + diffusion(padded, coeff) + STEP_TIME * ion
    return new_volt, gate_v + STEP_TIME * rate_v, gate_w + STEP_TIME * rate_w, gate_s + STEP_TIME * rate_s


def upsample(cond):
    return jnp.repeat(jnp.repeat(jnp.repeat(cond, 4, axis=1), 4, axis=2), 4, axis=3)


def coarsen(field):
    shaped = field.reshape(field.shape[0] // 2, 2, field.shape[1] // 2, 2, field.shape[2] // 2, 2)
    return jnp.mean(shaped, axis=(1, 3, 5))


def fiber_dir(fiber):
    block_index = fiber.astype(jnp.float32)
    theta = -1.0 + 2.0 * block_index / (NFIB - 1)
    tilt = 0.3 * jnp.sin(3.0 * block_index)
    return jnp.stack([jnp.sin(tilt), jnp.cos(tilt) * jnp.sin(theta), jnp.cos(tilt) * jnp.cos(theta)])


def along(field, axis_pos, weights):
    count = field.shape[axis_pos] - 2
    total = weights[0] * lax.slice_in_dim(field, 0, count, axis=axis_pos)
    total = total + weights[1] * lax.slice_in_dim(field, 1, count + 1, axis=axis_pos)
    return total + weights[2] * lax.slice_in_dim(field, 2, count + 2, axis=axis_pos)


def spline_op(padded, direction):
    result = padded
    for dim_pos in range(3):
        result = along(result, dim_pos + 1, SLOPE_WEIGHTS if dim_pos == direction else SMOOTH_WEIGHTS)
    return result


def deformation(padded_disp):
    grads = [spline_op(padded_disp, direction) for direction in range(3)]
    return [[grads[col_pos][row_pos] + (1.0 if row_pos == col_pos else 0.0) for col_pos in range(3)] for row_pos in range(3)]


def first_piola(deform, active, fdir):
    right = [[deform[0][a_pos] * deform[0][b_pos] + deform[1][a_pos] * deform[1][b_pos] + deform[2][a_pos] * deform[2][b_pos]
              for b_pos in range(3)] for a_pos in range(3)]
    strain = [[0.5 * (right[a_pos][b_pos] - (1.0 if a_pos == b_pos else 0.0)) for b_pos in range(3)] for a_pos in range(3)]
    trace_e = strain[0][0] + strain[1][1] + strain[2][2]
    second = []
    for a_pos in range(3):
        row_list = []
        for b_pos in range(3):
            entry = 2.0 * SHEAR * strain[a_pos][b_pos] + ACTIVE_GAIN * active * fdir[a_pos] * fdir[b_pos]
            if a_pos == b_pos:
                entry = LAME_FIRST * trace_e + entry
            row_list.append(entry)
        second.append(row_list)
    pieces = []
    for a_pos in range(3):
        for i_pos in range(3):
            pieces.append(deform[i_pos][0] * second[0][a_pos] + deform[i_pos][1] * second[1][a_pos] + deform[i_pos][2] * second[2][a_pos])
    return jnp.stack(pieces)


def forces(padded_piola):
    total = spline_op(padded_piola[0:3], 0)
    total = total + spline_op(padded_piola[3:6], 1)
    return total + spline_op(padded_piola[6:9], 2)


def metric(deform, fdir):
    det_f = (deform[0][0] * (deform[1][1] * deform[2][2] - deform[1][2] * deform[2][1])
             - deform[0][1] * (deform[1][0] * deform[2][2] - deform[1][2] * deform[2][0])
             + deform[0][2] * (deform[1][0] * deform[2][1] - deform[1][1] * deform[2][0]))
    inverse = [[None, None, None] for row_pos in range(3)]
    for i_pos in range(3):
        for j_pos in range(3):
            cofac = (deform[(i_pos + 1) % 3][(j_pos + 1) % 3] * deform[(i_pos + 2) % 3][(j_pos + 2) % 3]
                     - deform[(i_pos + 1) % 3][(j_pos + 2) % 3] * deform[(i_pos + 2) % 3][(j_pos + 1) % 3])
            inverse[j_pos][i_pos] = cofac / det_f
    along_fiber = [inverse[a_pos][0] * fdir[0] + inverse[a_pos][1] * fdir[1] + inverse[a_pos][2] * fdir[2] for a_pos in range(3)]
    comps = []
    for a_pos, b_pos in PAIRS:
        inv_metric = inverse[a_pos][0] * inverse[b_pos][0] + inverse[a_pos][1] * inverse[b_pos][1] + inverse[a_pos][2] * inverse[b_pos][2]
        comps.append(SIGMA_TRANS * inv_metric + (SIGMA_LONG - SIGMA_TRANS) * along_fiber[a_pos] * along_fiber[b_pos])
    return jnp.stack(comps)


def mechanics(disp, active, fdir, extend):
    for turn_index in range(MECH_STEPS):
        deform = deformation(extend(disp))
        piola = first_piola(deform, active, fdir)
        disp = disp + MECH_RATE * forces(extend(piola))
    deform = deformation(extend(disp))
    return disp, metric(deform, fdir)


def pad_space(field):
    return jnp.pad(field, ((0, 0), (1, 1), (1, 1), (1, 1)))


def reference(states, cond, tension, fiber, disp):
    volt, gate_v, gate_w, gate_s = states[0], states[1], states[2], states[3]
    coeff = upsample(cond)
    for turn_index in range(SUB):
        padded = jnp.pad(volt, 1)
        volt, gate_v, gate_w, gate_s = excite_step(padded, volt, gate_v, gate_w, gate_s, coeff)
    states_next = jnp.stack([volt, gate_v, gate_w, gate_s])
    tension_next = tension + 0.5 * (coarsen(volt) - tension)
    active = coarsen(tension_next)
    fdir = fiber_dir(fiber)
    disp_next, cond_next = mechanics(disp, active, fdir, pad_space)
    return states_next, tension_next, disp_next, cond_next
```

```python
import functools

import jax
import jax.numpy as jnp
from jax import lax
from jax.experimental import pallas as pl
from jax.experimental.pallas import tpu as pltpu
from jax.sharding import PartitionSpec as P

SUB = 4
MECH_STEPS = 2
NFIB = 64

STEP_TIME = 0.05
LAME_FIRST = 1.0
SHEAR = 0.5
ACTIVE_GAIN = 0.5
MECH_RATE = 0.15
SIGMA_LONG = 0.16
SIGMA_TRANS = 0.04
PAIRS = ((0, 0), (1, 1), (2, 2), (0, 1), (0, 2), (1, 2))

C_ZZ, C_ZY, C_ZXR, C_ZXL, C_MID, C_YY, C_XXR, C_YXR, C_XXL, C_YXL = range(10)

HIGHEST = lax.Precision.HIGHEST
LIMIT = 40 * 1024 * 1024


def params(**kwargs):
    return pltpu.CompilerParams(vmem_limit_bytes=LIMIT, **kwargs)


def cost(flops, nbytes, trans=0):
    return pl.CostEstimate(flops=flops, bytes_accessed=nbytes, transcendentals=trans)


def row_iota():
    return lax.broadcasted_iota(jnp.int32, (8, 1024), 0)


def next_row(cur, nxt, sub):
    return pltpu.roll(jnp.where(sub == 0, nxt, cur), 7, 0)


def prev_row(cur, prv, sub):
    return pltpu.roll(jnp.where(sub == 7, prv, cur), 1, 0)


def left(val):
    return pltpu.roll(val, val.shape[-1] - 1, val.ndim - 1)


def right(val):
    return pltpu.roll(val, 1, val.ndim - 1)


def edge_masks(tile, side, own):
    before = jnp.where((tile == 0) & (side == 0), 0.0, 1.0)
    after = jnp.where((tile == own - 1) & (side == 1), 0.0, 1.0)
    return before, after


def ring_neighbours(tile, tiles):
    before = jnp.where(tile == 0, tiles - 1, tile - 1)
    after = jnp.where(tile == tiles - 1, 0, tile + 1)
    return before, after


def coeff_kernel(cond_ref, out_ref):
    six, rows, width = cond_ref.shape
    fine = 4 * width
    mech = lax.broadcasted_iota(jnp.int32, (width, fine), 0)
    cell = lax.broadcasted_iota(jnp.int32, (width, fine), 1)
    tiles = rows // 2
    sub = lax.broadcasted_iota(jnp.int32, (8, fine), 0)

    def spread(comps, shift):
        pick = jnp.where(mech == ((cell + shift) >> 2), 1.0, 0.0)
        flat = jnp.concatenate([cond_ref[comp] for comp in comps], axis=0)
        wide = jnp.dot(flat, pick, precision=HIGHEST, preferred_element_type=jnp.float32)
        return [wide[pos * rows : (pos + 1) * rows] for pos in range(len(comps))]

    def store(index, wide):
        for tile in range(tiles):
            upper = jnp.broadcast_to(wide[2 * tile : 2 * tile + 1], (8, fine))
            lower = jnp.broadcast_to(wide[2 * tile + 1 : 2 * tile + 2], (8, fine))
            out_ref[index, tile] = jnp.where(sub < 4, upper, lower)

    zz, yy, xx, zy = spread((0, 1, 2, 3), 0)
    store(C_ZZ, zz)
    store(C_YY, yy)
    store(C_MID, -2.0 * (zz + yy + xx))
    store(C_ZY, 0.5 * zy)
    xx, zx, yx = spread((2, 4, 5), -1)
    store(C_XXR, xx)
    store(C_ZXR, 0.5 * zx)
    store(C_YXR, 0.5 * yx)
    xx, zx, yx = spread((2, 4, 5), 1)
    store(C_XXL, xx)
    store(C_ZXL, 0.5 * zx)
    store(C_YXL, 0.5 * yx)


def fine_coeffs(cond_rows):
    six, rows, width = cond_rows.shape
    return pl.pallas_call(
        coeff_kernel,
        out_shape=jax.ShapeDtypeStruct((10, rows // 2, 8, 4 * width), jnp.float32),
        compiler_params=params(),
        cost_estimate=cost(2_000_000, 3_200_000),
        name="coeffs",
    )(cond_rows)


def inverse(val):
    guess = pl.reciprocal(val, approx=True)
    return guess * (2.0 - val * guess)


def ionic(u, v, w, s):
    t_v = jnp.tanh(50.0 * u - 15.0)
    t_w = jnp.tanh(50.0 * u - 6.5)
    t_o = jnp.tanh(50.0 * u - 0.3)
    t_m = jnp.tanh(65.0 * u - 65.0 * 0.03)
    t_f = jnp.tanh(2.0458 * u - 2.0458 * 0.65)
    t_s = jnp.tanh(2.0994 * u - 2.0994 * 0.9087)
    hv = 0.5 + 0.5 * t_v
    hw = 0.5 + 0.5 * t_w
    ho = 0.5 + 0.5 * t_o
    nv = 1.0 - hv
    nw = 1.0 - hw
    no = 1.0 - ho
    r_vm = inverse(605.0 + 545.0 * t_o)
    r_wm = inverse(37.5 - 22.5 * t_m)
    half_so = 0.5 * (30.0181 - 0.9957)
    r_so = inverse((30.0181 - half_so) - half_so * t_f)
    r_s = inverse(9.3671 + 6.6329 * t_w)
    r_o = inverse(203.0 - 197.0 * t_o)
    w_inf = no * (1.0 - u * (1.0 / 0.07)) + 0.94 * ho
    hvv = hv * v
    hww = hw * w
    fast = hvv * ((u - 0.3) * (1.55 - u)) * (STEP_TIME / 0.11)
    out = (u * nw) * r_o + hw * r_so
    slow = hww * s * (STEP_TIME / 1.8875)
    u_add = fast + slow - STEP_TIME * out
    v_new = v + (nv * (no - v)) * (STEP_TIME * r_vm) - hvv * (STEP_TIME / 1.4506)
    w_new = w + (nw * (w_inf - w)) * (STEP_TIME * r_wm) - hww * (STEP_TIME / 200.0)
    s_new = s + ((0.5 + 0.5 * t_s) - s) * (STEP_TIME * r_s)
    return u_add, v_new, w_new, s_new


def local_kernel(last, tiles, per_block, side_ref, lo_ref, mid_ref, hi_ref, gate_ref, coeff_ref, *outs):
    side = side_ref[0]
    sub = row_iota()
    own = tiles - 1
    refs = [lambda t: lo_ref[t], lambda t: mid_ref[0, t], lambda t: mid_ref[1, t], lambda t: hi_ref[t]]
    planes = len(refs)

    def one(local_tile, carry):
        tile = pl.program_id(0) * per_block + local_tile
        before, after = ring_neighbours(tile, tiles)
        mask_before, mask_after = edge_masks(tile, side, own)
        cur = [ref(tile) for ref in refs]
        prv = [ref(before) * mask_before for ref in refs]
        nxt = [ref(after) * mask_after for ref in refs]

        def coeff(index):
            return coeff_ref[index, local_tile]

        for plane in range(planes):
            u = cur[plane]

            def slope(field):
                if plane == 0:
                    return field[1]
                if plane == planes - 1:
                    return -field[plane - 1]
                return field[plane + 1] - field[plane - 1]

            if plane == 0:
                around = cur[1]
            elif plane == planes - 1:
                around = cur[plane - 1]
            else:
                around = cur[plane + 1] + cur[plane - 1]
            wide = slope(cur)
            u_next = next_row(u, nxt[plane], sub)
            u_prev = prev_row(u, prv[plane], sub)
            w_next = next_row(wide, slope(nxt), sub)
            w_prev = prev_row(wide, slope(prv), sub)
            tall = u_next - u_prev
            diff = coeff(C_MID) * u + coeff(C_ZZ) * around
            diff += coeff(C_YY) * (u_next + u_prev) + coeff(C_ZY) * (w_next - w_prev)
            diff += left(coeff(C_XXR) * u + coeff(C_ZXR) * wide + coeff(C_YXR) * tall)
            diff += right(coeff(C_XXL) * u - coeff(C_ZXL) * wide - coeff(C_YXL) * tall)
            base = u + diff
            chunk = 256
            for start in range(0, 1024, chunk):
                lanes = slice(start, start + chunk)
                u_add, v_new, w_new, s_new = ionic(
                    u[:, lanes],
                    gate_ref[0, plane, local_tile, :, lanes],
                    gate_ref[1, plane, local_tile, :, lanes],
                    gate_ref[2, plane, local_tile, :, lanes],
                )
                u_new = base[:, lanes] + u_add
                if last:
                    outs[0][0, plane, local_tile, :, lanes] = u_new
                    outs[0][1, plane, local_tile, :, lanes] = v_new
                    outs[0][2, plane, local_tile, :, lanes] = w_new
                    outs[0][3, plane, local_tile, :, lanes] = s_new
                else:
                    if plane == 0:
                        outs[0][local_tile, :, lanes] = u_new
                    elif plane == planes - 1:
                        outs[2][local_tile, :, lanes] = u_new
                    else:
                        outs[1][plane - 1, local_tile, :, lanes] = u_new
                    outs[3][0, plane, local_tile, :, lanes] = v_new
                    outs[3][1, plane, local_tile, :, lanes] = w_new
                    outs[3][2, plane, local_tile, :, lanes] = s_new
        return carry

    lax.fori_loop(0, per_block, one, 0)


def local_step(side, lo, mid, hi, gates, coeffs, last):
    tiles, _, width = lo.shape
    per_block = 2 if last else 3
    blocks = (tiles - 1) // per_block if last else tiles // per_block
    whole3 = pl.BlockSpec((tiles, 8, width), lambda i: (0, 0, 0))
    whole4 = pl.BlockSpec((2, tiles, 8, width), lambda i: (0, 0, 0, 0))
    in_specs = [
        pl.BlockSpec(memory_space=pltpu.SMEM),
        whole3,
        whole4,
        whole3,
        pl.BlockSpec((3, 4, per_block, 8, width), lambda i: (0, 0, i, 0, 0)),
        pl.BlockSpec((10, per_block, 8, width), lambda i: (0, i, 0, 0)),
    ]
    if last:
        out_shape = jax.ShapeDtypeStruct((4, 4, tiles - 1, 8, width), jnp.float32)
        out_specs = pl.BlockSpec((4, 4, per_block, 8, width), lambda i: (0, 0, i, 0, 0))
    else:
        out_shape = [
            jax.ShapeDtypeStruct(lo.shape, jnp.float32),
            jax.ShapeDtypeStruct(mid.shape, jnp.float32),
            jax.ShapeDtypeStruct(hi.shape, jnp.float32),
            jax.ShapeDtypeStruct(gates.shape, jnp.float32),
        ]
        out_specs = [
            pl.BlockSpec((per_block, 8, width), lambda i: (i, 0, 0)),
            pl.BlockSpec((2, per_block, 8, width), lambda i: (0, i, 0, 0)),
            pl.BlockSpec((per_block, 8, width), lambda i: (i, 0, 0)),
            pl.BlockSpec((3, 4, per_block, 8, width), lambda i: (0, 0, i, 0, 0)),
        ]
    cells = 4 * tiles * 8 * width
    return pl.pallas_call(
        functools.partial(local_kernel, last, tiles, per_block),
        grid=(blocks,),
        in_specs=in_specs,
        out_specs=out_specs,
        out_shape=out_shape,
        compiler_params=params(),
        cost_estimate=cost(150 * cells, 40 * cells, 11 * cells),
        name="local_last" if last else "local",
    )(side, lo, mid, hi, gates, coeffs)


def halo_terms(halo_ref, coeff_ref, tile, tiles, side, sub, sign):
    before, after = ring_neighbours(tile, tiles)
    mask_before, mask_after = edge_masks(tile, side, tiles - 1)
    cur = halo_ref[tile]
    up = next_row(cur, halo_ref[after] * mask_after, sub)
    down = prev_row(cur, halo_ref[before] * mask_before, sub)
    cross = coeff_ref[C_ZY, tile] * (up - down)
    cross += left(coeff_ref[C_ZXR, tile] * cur) - right(coeff_ref[C_ZXL, tile] * cur)
    total = coeff_ref[C_ZZ, tile] * cur
    return total + cross if sign > 0 else total - cross


def halo_kernel(tiles, side_ref, lo_ref, hi_ref, below_ref, above_ref, coeff_ref, lo_out, hi_out):
    side = side_ref[0]
    sub = row_iota()

    def one(tile, carry):
        lo_out[tile] = lo_ref[tile] + halo_terms(below_ref, coeff_ref, tile, tiles, side, sub, -1)
        hi_out[tile] = hi_ref[tile] + halo_terms(above_ref, coeff_ref, tile, tiles, side, sub, 1)
        return carry

    lax.fori_loop(0, tiles, one, 0)


def halo_step(side, lo, hi, below, above, coeffs):
    tiles, _, width = lo.shape
    whole = pl.BlockSpec((tiles, 8, width), lambda i: (0, 0, 0))
    cells = 2 * tiles * 8 * width
    return pl.pallas_call(
        functools.partial(halo_kernel, tiles),
        grid=(1,),
        in_specs=[pl.BlockSpec(memory_space=pltpu.SMEM)]
        + [whole] * 4
        + [pl.BlockSpec((4, tiles, 8, width), lambda i: (0, 0, 0, 0))],
        out_specs=[whole, whole],
        out_shape=[jax.ShapeDtypeStruct(lo.shape, jnp.float32)] * 2,
        compiler_params=params(),
        cost_estimate=cost(15 * cells, 20 * cells),
        name="halo",
    )(side, lo, hi, below, above, coeffs)


def pair_matrix(width, scale):
    fine = lax.broadcasted_iota(jnp.int32, (width, width // 2), 0)
    coarse = lax.broadcasted_iota(jnp.int32, (width, width // 2), 1)
    return jnp.where((fine >> 1) == coarse, scale, 0.0)


def row_pairs(count, scale):
    coarse = lax.broadcasted_iota(jnp.int32, (count // 2, count), 0)
    fine = lax.broadcasted_iota(jnp.int32, (count // 2, count), 1)
    return jnp.where((fine >> 1) == coarse, scale, 0.0)


def dot(a, b):
    return jnp.dot(a, b, precision=HIGHEST, preferred_element_type=jnp.float32)


def pooled(field):
    rows, lanes = field.shape
    few = dot(row_pairs(rows, 0.5), field)
    pick = pair_matrix(256, 0.5)
    return jnp.concatenate([dot(few[:, at : at + 256], pick) for at in range(0, lanes, 256)], axis=1)


def finish_kernel(tiles, side_ref, part_ref, below_ref, above_ref, coeff_ref, tension_ref, out_ref, tension_out, active_out):
    side = side_ref[0]
    sub = row_iota()
    own = tiles - 1
    planes = part_ref.shape[1]

    def one(tile, carry):
        out_ref[0, 0, tile] = part_ref[0, 0, tile] + halo_terms(below_ref, coeff_ref, tile, tiles, side, sub, -1)
        for plane in range(1, planes - 1):
            out_ref[0, plane, tile] = part_ref[0, plane, tile]
        out_ref[0, planes - 1, tile] = part_ref[0, planes - 1, tile] + halo_terms(
            above_ref, coeff_ref, tile, tiles, side, sub, 1
        )
        return carry

    lax.fori_loop(0, own, one, 0)
    width = part_ref.shape[-1]
    total = None
    for layer in range(planes // 2):
        both = 0.5 * (out_ref[0, 2 * layer] + out_ref[0, 2 * layer + 1])
        mean = pooled(both.reshape(own * 8, width))
        old = tension_ref[layer]
        new = old + 0.5 * (mean - old)
        tension_out[layer] = new
        total = new if total is None else total + new
    active_out[...] = pooled(0.5 * total)


def finish_step(side, part, below, above, coeffs, tension):
    tiles, _, width = below.shape
    own = tiles - 1
    planes = part.shape[1]
    halo_spec = pl.BlockSpec((tiles, 8, width), lambda i: (0, 0, 0))
    u_spec = pl.BlockSpec((1, planes, own, 8, width), lambda i: (0, 0, 0, 0, 0))
    tension_spec = pl.BlockSpec(tension.shape, lambda i: (0, 0, 0))
    active_shape = (own * 2, width // 4)
    cells = planes * own * 8 * width
    return pl.pallas_call(
        functools.partial(finish_kernel, tiles),
        grid=(1,),
        in_specs=[
            pl.BlockSpec(memory_space=pltpu.SMEM),
            u_spec,
            halo_spec,
            halo_spec,
            pl.BlockSpec((4, tiles, 8, width), lambda i: (0, 0, 0, 0)),
            tension_spec,
        ],
        out_specs=[u_spec, tension_spec, pl.BlockSpec(active_shape, lambda i: (0, 0))],
        out_shape=[
            jax.ShapeDtypeStruct(part.shape, jnp.float32),
            jax.ShapeDtypeStruct(tension.shape, jnp.float32),
            jax.ShapeDtypeStruct(active_shape, jnp.float32),
        ],
        input_output_aliases={1: 0},
        compiler_params=params(),
        cost_estimate=cost(20 * cells, 20 * cells),
        name="finish",
    )(side, part, below, above, coeffs, tension)


REACH = 4
ROWS = 24


class Weights:
    def __init__(self, side, own, width):
        row = lax.broadcasted_iota(jnp.int32, (ROWS, width), 0)
        lane = lax.broadcasted_iota(jnp.int32, (ROWS, width), 1)
        self.next_y = jnp.where((row == own - 1) & (side == 1), 0.0, 1.0)
        self.prev_y = jnp.where((row == 0) & (side == 0), 0.0, 1.0)
        self.next_x = jnp.where(lane == width - 1, 0.0, 1.0)
        self.prev_x = jnp.where(lane == 0, 0.0, 1.0)


def up_y(val):
    return pltpu.roll(val, ROWS - 1, 0)


def down_y(val):
    return pltpu.roll(val, 1, 0)


def slope_z(below, mid, above):
    return 0.5 * (above - below)


def smooth_z(below, mid, above):
    return 0.75 * mid + 0.125 * (above + below)


def gradients(below, mid, above, k):
    slope = slope_z(below, mid, above)
    smooth = smooth_z(below, mid, above)
    slope_s = 0.75 * slope + 0.125 * (up_y(slope) * k.next_y + down_y(slope) * k.prev_y)
    ahead = up_y(smooth) * k.next_y
    behind = down_y(smooth) * k.prev_y
    smooth_s = 0.75 * smooth + 0.125 * (ahead + behind)
    smooth_d = 0.5 * (ahead - behind)

    def smooth_x(val):
        return 0.75 * val + 0.125 * (left(val) * k.next_x + right(val) * k.prev_x)

    return (
        smooth_x(slope_s),
        smooth_x(smooth_d),
        0.5 * (left(smooth_s) * k.next_x - right(smooth_s) * k.prev_x),
    )


def force(below, mid, above, k):
    p_z = slope_z(below[0], mid[0], above[0])
    p_y = smooth_z(below[1], mid[1], above[1])
    p_x = smooth_z(below[2], mid[2], above[2])
    small, half = 0.125 * p_z, 0.5 * p_y
    both = 0.75 * p_z + up_y(small + half) * k.next_y + down_y(small - half) * k.prev_y
    p_x = 0.75 * p_x + 0.125 * (up_y(p_x) * k.next_y + down_y(p_x) * k.prev_y)
    small, half = 0.125 * both, 0.5 * p_x
    return 0.75 * both + left(small + half) * k.next_x + right(small - half) * k.prev_x


def deformation(below, mid, above, k):
    deform = []
    for comp in range(3):
        row = list(gradients(below[comp], mid[comp], above[comp], k))
        row[comp] = row[comp] + 1.0
        deform.append(row)
    return deform


def passive_stress(deform):
    right_c = {}
    for a_pos, b_pos in PAIRS:
        right_c[a_pos, b_pos] = sum(deform[i_pos][a_pos] * deform[i_pos][b_pos] for i_pos in range(3))
    strain = {}
    for a_pos, b_pos in PAIRS:
        strain[a_pos, b_pos] = 0.5 * (right_c[a_pos, b_pos] - (1.0 if a_pos == b_pos else 0.0))
    trace = strain[0, 0] + strain[1, 1] + strain[2, 2]
    second = {}
    for a_pos, b_pos in PAIRS:
        entry = (2.0 * SHEAR) * strain[a_pos, b_pos]
        if a_pos == b_pos:
            entry = entry + LAME_FIRST * trace
        second[a_pos, b_pos] = entry
        second[b_pos, a_pos] = entry
    return second


def times(deform, second):
    return [
        [sum(deform[i_pos][b_pos] * second[b_pos, a_pos] for b_pos in range(3)) for a_pos in range(3)]
        for i_pos in range(3)
    ]


def metric(deform, fdir):
    def cofactor(i_pos, j_pos):
        i_next, i_last = (i_pos + 1) % 3, (i_pos + 2) % 3
        j_next, j_last = (j_pos + 1) % 3, (j_pos + 2) % 3
        return deform[i_next][j_next] * deform[i_last][j_last] - deform[i_next][j_last] * deform[i_last][j_next]

    cof = [[cofactor(i_pos, j_pos) for j_pos in range(3)] for i_pos in range(3)]
    det = deform[0][0] * cof[0][0] + deform[0][1] * cof[0][1] + deform[0][2] * cof[0][2]
    scale = 1.0 / det
    inv = [[cof[i_pos][j_pos] * scale for i_pos in range(3)] for j_pos in range(3)]
    along = [sum(inv[a_pos][i_pos] * fdir[i_pos] for i_pos in range(3)) for a_pos in range(3)]
    comps = []
    for a_pos, b_pos in PAIRS:
        inner = sum(inv[a_pos][i_pos] * inv[b_pos][i_pos] for i_pos in range(3))
        comps.append(SIGMA_TRANS * inner + (SIGMA_LONG - SIGMA_TRANS) * along[a_pos] * along[b_pos])
    return comps


def window_plane(ref, comp, place, offset):
    slab, side, slabs = place
    spot = jnp.clip(slab + offset, 0, slabs - 1)
    own = ref[spot, side, comp]
    first = pl.multiple_of(8 * side, 8)
    strip = ref[spot, 1 - side, comp, pl.ds(first, 8), :]
    return jnp.concatenate([own, strip], axis=0)


def inside(place, offset):
    slab, _, slabs = place
    spot = slab + offset
    return jnp.where((spot >= 0) & (spot < slabs), 1.0, 0.0)


def passive_kernel(place_ref, field_ref, disp_out, stress_out, pull_out, fdir_out):
    slabs, _, _, own, width = field_ref.shape
    place = (place_ref[0], place_ref[1], slabs)
    k = Weights(place[1], own, width)

    def disp_at(offset):
        factor = inside(place, offset)
        return [window_plane(field_ref, comp, place, offset) * factor for comp in range(3)]

    def one(step, carry):
        offset = step - REACH
        below, mid, above = (disp_at(offset - 1), disp_at(offset), disp_at(offset + 1))
        factor = inside(place, offset)
        deform = deformation(below, mid, above, k)
        stress = times(deform, passive_stress(deform))
        fdir = [window_plane(field_ref, 3 + comp, place, offset) for comp in range(3)]
        for i_pos in range(3):
            pull = (ACTIVE_GAIN * factor) * sum(deform[i_pos][b_pos] * fdir[b_pos] for b_pos in range(3))
            for a_pos in range(3):
                stress_out[3 * i_pos + a_pos, step] = stress[i_pos][a_pos] * factor
                pull_out[3 * i_pos + a_pos, step] = pull * fdir[a_pos]
            disp_out[i_pos, step] = mid[i_pos]
            fdir_out[i_pos, step] = fdir[i_pos]
        return carry

    lax.fori_loop(0, 2 * REACH + 1, one, 0)


def passive_step(place, field):
    slabs, _, _, own, width = field.shape
    planes = 2 * REACH + 1
    shapes = [(3, planes), (9, planes), (9, planes), (3, planes)]
    return pl.pallas_call(
        passive_kernel,
        in_specs=[pl.BlockSpec(memory_space=pltpu.SMEM), pl.BlockSpec(memory_space=pltpu.VMEM)],
        out_shape=[jax.ShapeDtypeStruct((a, b, ROWS, width), jnp.float32) for a, b in shapes],
        compiler_params=params(),
        cost_estimate=cost(400 * planes * ROWS * width, 5_000_000),
        name="passive",
    )(place, field)


def mechanics_kernel(place_ref, active_ref, disp_ref, stress_ref, pull_ref, fdir_ref, disp_out, cond_out, d_one, p_two):
    slabs, _, own, width = active_ref.shape
    slab, side = place_ref[0], place_ref[1]
    place = (slab, side, slabs)
    k = Weights(side, own, width)

    def active_at(step):
        spot = jnp.clip(slab + step - REACH, 0, slabs - 1)
        first = pl.multiple_of(8 * side, 8)
        return jnp.concatenate([active_ref[spot, side], active_ref[spot, 1 - side, pl.ds(first, 8), :]], axis=0)

    def first_force(step, carry):
        act = [active_at(step + shift) for shift in (-1, 0, 1)]
        factor = inside(place, step - REACH)
        for i_pos in range(3):
            stress = [
                [stress_ref[3 * i_pos + a_pos, step + shift] + act[shift + 1] * pull_ref[3 * i_pos + a_pos, step + shift] for a_pos in range(3)]
                for shift in (-1, 0, 1)
            ]
            moved = disp_ref[i_pos, step] + MECH_RATE * force(stress[0], stress[1], stress[2], k)
            d_one[i_pos, step] = moved * factor
        return carry

    lax.fori_loop(1, 2 * REACH, first_force, 0)

    def second_stress(step, carry):
        planes = [[d_one[comp, step + shift] for comp in range(3)] for shift in (-1, 0, 1)]
        deform = deformation(planes[0], planes[1], planes[2], k)
        second = passive_stress(deform)
        fdir = [fdir_ref[comp, step] for comp in range(3)]
        gain = ACTIVE_GAIN * active_at(step)
        for a_pos, b_pos in PAIRS:
            entry = second[a_pos, b_pos] + gain * fdir[a_pos] * fdir[b_pos]
            second[a_pos, b_pos] = entry
            second[b_pos, a_pos] = entry
        stress = times(deform, second)
        factor = inside(place, step - REACH)
        for i_pos in range(3):
            for a_pos in range(3):
                p_two[3 * i_pos + a_pos, step] = stress[i_pos][a_pos] * factor
        return carry

    lax.fori_loop(2, 2 * REACH - 1, second_stress, 0)

    last = []
    for step in (REACH - 1, REACH, REACH + 1):
        factor = inside(place, step - REACH)
        row = []
        for i_pos in range(3):
            stress = [[p_two[3 * i_pos + a_pos, step + shift] for a_pos in range(3)] for shift in (-1, 0, 1)]
            moved = d_one[i_pos, step] + MECH_RATE * force(stress[0], stress[1], stress[2], k)
            row.append(moved * factor)
        last.append(row)
    deform = deformation(last[0], last[1], last[2], k)
    comps = metric(deform, [fdir_ref[comp, REACH] for comp in range(3)])
    for i_pos in range(3):
        disp_out[i_pos, 0] = last[1][i_pos][:own]
    for pos, comp in enumerate(comps):
        cond_out[pos, 0] = comp[:own]


def mechanics_step(place, active, window):
    slabs, _, own, width = active.shape
    planes = 2 * REACH + 1
    vmem = pl.BlockSpec(memory_space=pltpu.VMEM)
    return pl.pallas_call(
        mechanics_kernel,
        in_specs=[pl.BlockSpec(memory_space=pltpu.SMEM)] + [vmem] * 5,
        out_shape=[
            jax.ShapeDtypeStruct((3, 1, own, width), jnp.float32),
            jax.ShapeDtypeStruct((6, 1, own, width), jnp.float32),
        ],
        scratch_shapes=[
            pltpu.VMEM((3, planes, ROWS, width), jnp.float32),
            pltpu.VMEM((9, planes, ROWS, width), jnp.float32),
        ],
        compiler_params=params(),
        cost_estimate=cost(400 * planes * ROWS * width, 5_000_000),
        name="mechanics",
    )(place, active, *window)


def fiber_dir(fiber):
    block_index = fiber.astype(jnp.float32)
    theta = -1.0 + 2.0 * block_index / (NFIB - 1)
    tilt = 0.3 * jnp.sin(3.0 * block_index)
    return jnp.stack([jnp.sin(tilt), jnp.cos(tilt) * jnp.sin(theta), jnp.cos(tilt) * jnp.cos(theta)])


def on_device(states, cond, tension, fiber, disp):
    slabs = lax.axis_size("slab")
    slab, col = lax.axis_index("slab"), lax.axis_index("col")
    _, planes, rows, width = states.shape
    own = rows // 8
    up = [(i, i + 1) for i in range(slabs - 1)]
    down = [(i + 1, i) for i in range(slabs - 1)]
    up_cross = [(2 * i + c, 2 * i + 3 - c) for i in range(slabs - 1) for c in range(2)]
    down_cross = [(dst, src) for src, dst in up_cross]
    swap = [(0, 1), (1, 0)]
    side = col.astype(jnp.int32).reshape(1)
    place = jnp.stack([slab, col]).astype(jnp.int32)

    tiled = states.reshape(4, planes, own, 8, width)
    below_own = lax.ppermute(tiled[0, planes - 1], "slab", up)
    above_own = lax.ppermute(tiled[0, 0], "slab", down)

    facing = jnp.where(col == 0, tiled[:, :, own - 1], tiled[:, :, 0])
    cond_facing = jnp.where(col == 0, cond[:, 0, -2:], cond[:, 0, :2])
    strip = lax.ppermute(facing, "col", swap)
    cond_strip = lax.ppermute(cond_facing, "col", swap)
    below_strip = lax.ppermute(facing[0, planes - 1], ("slab", "col"), up_cross)
    above_strip = lax.ppermute(facing[0, 0], ("slab", "col"), down_cross)

    field = jnp.concatenate([disp[:, 0], fiber_dir(fiber)[:, 0]], axis=0)
    field = lax.all_gather(field, ("slab", "col")).reshape((slabs, 2) + field.shape)

    coeffs = fine_coeffs(jnp.concatenate([cond[:, 0], cond_strip], axis=1))
    wide = jnp.concatenate([tiled, strip[:, :, None]], axis=2)
    lo, mid, hi, gates = wide[0, 0], wide[0, 1:-1], wide[0, -1], wide[1:]
    below = jnp.concatenate([below_own, below_strip[None]], axis=0)
    above = jnp.concatenate([above_own, above_strip[None]], axis=0)
    window = None
    for turn_index in range(SUB):
        last = turn_index == SUB - 1
        result = local_step(side, lo, mid, hi, gates, coeffs, last)
        if turn_index == 1:
            window = passive_step(place, field)
        if last:
            part = result
        else:
            lo, mid, hi, gates = result
            lo, hi = halo_step(side, lo, hi, below, above, coeffs)
            below = lax.ppermute(hi, "slab", up)
            above = lax.ppermute(lo, "slab", down)
    states_next, tension_next, active = finish_step(side, part, below, above, coeffs, tension)
    active = lax.all_gather(active, ("slab", "col")).reshape((slabs, 2) + active.shape)
    disp_next, cond_next = mechanics_step(place, active, window)
    return (states_next.reshape(states.shape), tension_next, disp_next, cond_next)


def solution(mesh):
    in_specs = (
        P(None, ("grp", "slab"), "col", None),
        P(None, ("grp", "slab"), "col", None),
        P(("grp", "slab"), "col", None),
        P(("grp", "slab"), "col", None),
        P(None, ("grp", "slab"), "col", None),
    )
    out_specs = (
        P(None, ("grp", "slab"), "col", None),
        P(("grp", "slab"), "col", None),
        P(None, ("grp", "slab"), "col", None),
        P(None, ("grp", "slab"), "col", None),
    )
    return jax.shard_map(
        on_device, mesh=mesh, in_specs=in_specs, out_specs=out_specs, check_vma=False
    )
```

```python
import functools

import jax
import jax.numpy as jnp
from jax import lax
from jax.experimental import pallas as pl
from jax.experimental.pallas import tpu as pltpu
from jax.sharding import PartitionSpec as P

SUB = 4
MECH_STEPS = 2
NFIB = 64

STEP_TIME = 0.05
LAME_FIRST = 1.0
SHEAR = 0.5
ACTIVE_GAIN = 0.5
MECH_RATE = 0.15
SIGMA_LONG = 0.16
SIGMA_TRANS = 0.04
PAIRS = ((0, 0), (1, 1), (2, 2), (0, 1), (0, 2), (1, 2))

C_ZZ, C_ZY, C_ZXR, C_ZXL, C_MID, C_YY, C_XXR, C_YXR, C_XXL, C_YXL = range(10)

SLAB, SIDE, FLIP, FAR = range(4)

HIGHEST = lax.Precision.HIGHEST
LIMIT = 40 * 1024 * 1024


def params(**kwargs):
    return pltpu.CompilerParams(vmem_limit_bytes=LIMIT, **kwargs)


def cost(flops, nbytes, trans=0):
    return pl.CostEstimate(flops=flops, bytes_accessed=nbytes, transcendentals=trans)


def row_iota():
    return lax.broadcasted_iota(jnp.int32, (8, 1024), 0)


def next_row(cur, nxt, sub):
    return pltpu.roll(jnp.where(sub == 0, nxt, cur), 7, 0)


def prev_row(cur, prv, sub):
    return pltpu.roll(jnp.where(sub == 7, prv, cur), 1, 0)


def left(val):
    return pltpu.roll(val, val.shape[-1] - 1, val.ndim - 1)


def right(val):
    return pltpu.roll(val, 1, val.ndim - 1)


def edge_masks(tile, side, own):
    before = jnp.where((tile == 0) & (side == 0), 0.0, 1.0)
    after = jnp.where((tile == own - 1) & (side == 1), 0.0, 1.0)
    return before, after


def ring_neighbours(tile, tiles):
    before = jnp.where(tile == 0, tiles - 1, tile - 1)
    after = jnp.where(tile == tiles - 1, 0, tile + 1)
    return before, after


def coeff_kernel(info_ref, cond_ref, out_ref):
    six, rows, width = cond_ref.shape
    turn = jnp.where(info_ref[FLIP] == 1, -0.5, 0.5)
    fine = 4 * width
    mech = lax.broadcasted_iota(jnp.int32, (width, fine), 0)
    cell = lax.broadcasted_iota(jnp.int32, (width, fine), 1)
    tiles = rows // 2
    sub = lax.broadcasted_iota(jnp.int32, (8, fine), 0)

    def spread(comps, shift):
        pick = jnp.where(mech == ((cell + shift) >> 2), 1.0, 0.0)
        flat = jnp.concatenate([cond_ref[comp] for comp in comps], axis=0)
        wide = jnp.dot(flat, pick, precision=HIGHEST, preferred_element_type=jnp.float32)
        return [wide[pos * rows : (pos + 1) * rows] for pos in range(len(comps))]

    def store(index, wide):
        for tile in range(tiles):
            upper = jnp.broadcast_to(wide[2 * tile : 2 * tile + 1], (8, fine))
            lower = jnp.broadcast_to(wide[2 * tile + 1 : 2 * tile + 2], (8, fine))
            out_ref[index, tile] = jnp.where(sub < 4, upper, lower)

    zz, yy, xx, zy = spread((0, 1, 2, 3), 0)
    store(C_ZZ, zz)
    store(C_YY, yy)
    store(C_MID, -2.0 * (zz + yy + xx))
    store(C_ZY, turn * zy)
    xx, zx, yx = spread((2, 4, 5), -1)
    store(C_XXR, xx)
    store(C_ZXR, turn * zx)
    store(C_YXR, 0.5 * yx)
    xx, zx, yx = spread((2, 4, 5), 1)
    store(C_XXL, xx)
    store(C_ZXL, turn * zx)
    store(C_YXL, 0.5 * yx)


def fine_coeffs(info, cond_rows):
    six, rows, width = cond_rows.shape
    return pl.pallas_call(
        coeff_kernel,
        in_specs=[pl.BlockSpec(memory_space=pltpu.SMEM), pl.BlockSpec(memory_space=pltpu.VMEM)],
        out_shape=jax.ShapeDtypeStruct((10, rows // 2, 8, 4 * width), jnp.float32),
        compiler_params=params(),
        cost_estimate=cost(2_000_000, 3_200_000),
        name="coeffs",
    )(info, cond_rows)


def inverse(val):
    guess = pl.reciprocal(val, approx=True)
    return guess * (2.0 - val * guess)


def ionic(u, v, w, s):
    t_v = jnp.tanh(50.0 * u - 15.0)
    t_w = jnp.tanh(50.0 * u - 6.5)
    t_o = jnp.tanh(50.0 * u - 0.3)
    t_m = jnp.tanh(65.0 * u - 65.0 * 0.03)
    t_f = jnp.tanh(2.0458 * u - 2.0458 * 0.65)
    t_s = jnp.tanh(2.0994 * u - 2.0994 * 0.9087)
    hv = 0.5 + 0.5 * t_v
    hw = 0.5 + 0.5 * t_w
    ho = 0.5 + 0.5 * t_o
    nv = 1.0 - hv
    nw = 1.0 - hw
    no = 1.0 - ho
    r_vm = inverse(605.0 + 545.0 * t_o)
    r_wm = inverse(37.5 - 22.5 * t_m)
    half_so = 0.5 * (30.0181 - 0.9957)
    r_so = inverse((30.0181 - half_so) - half_so * t_f)
    r_s = inverse(9.3671 + 6.6329 * t_w)
    r_o = inverse(203.0 - 197.0 * t_o)
    w_inf = no * (1.0 - u * (1.0 / 0.07)) + 0.94 * ho
    hvv = hv * v
    hww = hw * w
    fast = hvv * ((u - 0.3) * (1.55 - u)) * (STEP_TIME / 0.11)
    out = (u * nw) * r_o + hw * r_so
    slow = hww * s * (STEP_TIME / 1.8875)
    u_add = fast + slow - STEP_TIME * out
    v_new = v + (nv * (no - v)) * (STEP_TIME * r_vm) - hvv * (STEP_TIME / 1.4506)
    w_new = w + (nw * (w_inf - w)) * (STEP_TIME * r_wm) - hww * (STEP_TIME / 200.0)
    s_new = s + ((0.5 + 0.5 * t_s) - s) * (STEP_TIME * r_s)
    return u_add, v_new, w_new, s_new


def local_kernel(first, last, tiles, per_block, info_ref, *refs):
    side, flip = info_ref[SIDE], info_ref[FLIP]
    sub = row_iota()
    own = tiles - 1
    planes = 4
    place = [plane + flip * (planes - 1 - 2 * plane) for plane in range(planes)]
    if first:
        u_ref, gate_ref, coeff_ref, *outs = refs
        reads = [lambda t, p=p: u_ref[p, t] for p in place]
        gate_place = place
    else:
        far_ref, mid_ref, near_ref, gate_ref, coeff_ref, *outs = refs
        reads = [lambda t: far_ref[t], lambda t: mid_ref[0, t], lambda t: mid_ref[1, t], lambda t: near_ref[t]]
        gate_place = list(range(planes))

    def one(local_tile, carry):
        tile = pl.program_id(0) * per_block + local_tile
        before, after = ring_neighbours(tile, tiles)
        mask_before, mask_after = edge_masks(tile, side, own)
        cur = [read(tile) for read in reads]
        prv = [read(before) * mask_before for read in reads]
        nxt = [read(after) * mask_after for read in reads]

        def coeff(index):
            return coeff_ref[index, local_tile]

        for plane in range(planes):
            u = cur[plane]

            def slope(field):
                if plane == 0:
                    return field[1]
                if plane == planes - 1:
                    return -field[plane - 1]
                return field[plane + 1] - field[plane - 1]

            if plane == 0:
                around = cur[1]
            elif plane == planes - 1:
                around = cur[plane - 1]
            else:
                around = cur[plane + 1] + cur[plane - 1]
            wide = slope(cur)
            u_next = next_row(u, nxt[plane], sub)
            u_prev = prev_row(u, prv[plane], sub)
            w_next = next_row(wide, slope(nxt), sub)
            w_prev = prev_row(wide, slope(prv), sub)
            tall = u_next - u_prev
            diff = coeff(C_MID) * u + coeff(C_ZZ) * around
            diff += coeff(C_YY) * (u_next + u_prev) + coeff(C_ZY) * (w_next - w_prev)
            diff += left(coeff(C_XXR) * u + coeff(C_ZXR) * wide + coeff(C_YXR) * tall)
            diff += right(coeff(C_XXL) * u - coeff(C_ZXL) * wide - coeff(C_YXL) * tall)
            base = u + diff
            chunk = 256
            for start in range(0, 1024, chunk):
                lanes = slice(start, start + chunk)
                gates = [gate_ref[g, gate_place[plane], local_tile, :, lanes] for g in range(3)]
                u_add, v_new, w_new, s_new = ionic(u[:, lanes], *gates)
                u_new = base[:, lanes] + u_add
                if last:
                    for comp, value in enumerate((u_new, v_new, w_new, s_new)):
                        outs[0][comp, place[plane], local_tile, :, lanes] = value
                else:
                    if plane == 0:
                        outs[0][local_tile, :, lanes] = u_new
                    elif plane == planes - 1:
                        outs[2][local_tile, :, lanes] = u_new
                    else:
                        outs[1][plane - 1, local_tile, :, lanes] = u_new
                    for comp, value in enumerate((v_new, w_new, s_new)):
                        outs[3][comp, plane, local_tile, :, lanes] = value
        return carry

    lax.fori_loop(0, per_block, one, 0)


def local_step(info, u_parts, gates, coeffs, last):
    first = len(u_parts) == 1
    _, planes, tiles, _, width = gates.shape
    per_block = 2 if last else 3
    blocks = (tiles - 1) // per_block if last else tiles // per_block
    plane_shape, mid_shape = (tiles, 8, width), (planes - 2, tiles, 8, width)
    in_specs = [pl.BlockSpec(memory_space=pltpu.SMEM)]
    in_specs += [pl.BlockSpec(part.shape, lambda i, n=part.ndim: (0,) * n) for part in u_parts]
    in_specs += [
        pl.BlockSpec((3, planes, per_block, 8, width), lambda i: (0, 0, i, 0, 0)),
        pl.BlockSpec((10, per_block, 8, width), lambda i: (0, i, 0, 0)),
    ]
    if last:
        out_shape = jax.ShapeDtypeStruct((4, planes, tiles - 1, 8, width), jnp.float32)
        out_specs = pl.BlockSpec((4, planes, per_block, 8, width), lambda i: (0, 0, i, 0, 0))
    else:
        out_shape = [
            jax.ShapeDtypeStruct(plane_shape, jnp.float32),
            jax.ShapeDtypeStruct(mid_shape, jnp.float32),
            jax.ShapeDtypeStruct(plane_shape, jnp.float32),
            jax.ShapeDtypeStruct(gates.shape, jnp.float32),
        ]
        out_specs = [
            pl.BlockSpec((per_block, 8, width), lambda i: (i, 0, 0)),
            pl.BlockSpec((planes - 2, per_block, 8, width), lambda i: (0, i, 0, 0)),
            pl.BlockSpec((per_block, 8, width), lambda i: (i, 0, 0)),
            pl.BlockSpec((3, planes, per_block, 8, width), lambda i: (0, 0, i, 0, 0)),
        ]
    cells = planes * tiles * 8 * width
    return pl.pallas_call(
        functools.partial(local_kernel, first, last, tiles, per_block),
        grid=(blocks,),
        in_specs=in_specs,
        out_specs=out_specs,
        out_shape=out_shape,
        compiler_params=params(),
        cost_estimate=cost(150 * cells, 40 * cells, 11 * cells),
        name="local_first" if first else "local_last" if last else "local",
    )(info, *u_parts, gates, coeffs)


def halo_terms(halo_ref, coeff_ref, tile, tiles, side, sub, sign):
    before, after = ring_neighbours(tile, tiles)
    mask_before, mask_after = edge_masks(tile, side, tiles - 1)
    cur = halo_ref[tile]
    up = next_row(cur, halo_ref[after] * mask_after, sub)
    down = prev_row(cur, halo_ref[before] * mask_before, sub)
    cross = coeff_ref[C_ZY, tile] * (up - down)
    cross += left(coeff_ref[C_ZXR, tile] * cur) - right(coeff_ref[C_ZXL, tile] * cur)
    total = coeff_ref[C_ZZ, tile] * cur
    return total + cross if sign > 0 else total - cross


def halo_kernel(tiles, info_ref, far_ref, near_ref, beyond_ref, pair_ref, coeff_ref, far_out, near_out):
    side = info_ref[SIDE]
    exists = info_ref[FAR].astype(jnp.float32)
    sub = row_iota()

    def one(tile, carry):
        near_out[tile] = near_ref[tile] + halo_terms(pair_ref, coeff_ref, tile, tiles, side, sub, 1)
        far_out[tile] = far_ref[tile] + exists * halo_terms(beyond_ref, coeff_ref, tile, tiles, side, sub, -1)
        return carry

    lax.fori_loop(0, tiles, one, 0)


def halo_step(info, far, near, beyond, pair, coeffs):
    tiles, _, width = far.shape
    whole = pl.BlockSpec((tiles, 8, width), lambda i: (0, 0, 0))
    cells = 2 * tiles * 8 * width
    return pl.pallas_call(
        functools.partial(halo_kernel, tiles),
        grid=(1,),
        in_specs=[pl.BlockSpec(memory_space=pltpu.SMEM)]
        + [whole] * 4
        + [pl.BlockSpec((4, tiles, 8, width), lambda i: (0, 0, 0, 0))],
        out_specs=[whole, whole],
        out_shape=[jax.ShapeDtypeStruct(far.shape, jnp.float32)] * 2,
        compiler_params=params(),
        cost_estimate=cost(15 * cells, 20 * cells),
        name="halo",
    )(info, far, near, beyond, pair, coeffs)


def pair_matrix(width, scale):
    fine = lax.broadcasted_iota(jnp.int32, (width, width // 2), 0)
    coarse = lax.broadcasted_iota(jnp.int32, (width, width // 2), 1)
    return jnp.where((fine >> 1) == coarse, scale, 0.0)


def row_pairs(count, scale):
    coarse = lax.broadcasted_iota(jnp.int32, (count // 2, count), 0)
    fine = lax.broadcasted_iota(jnp.int32, (count // 2, count), 1)
    return jnp.where((fine >> 1) == coarse, scale, 0.0)


def dot(a, b):
    return jnp.dot(a, b, precision=HIGHEST, preferred_element_type=jnp.float32)


def pooled(field):
    rows, lanes = field.shape
    few = dot(row_pairs(rows, 0.5), field)
    pick = pair_matrix(256, 0.5)
    return jnp.concatenate([dot(few[:, at : at + 256], pick) for at in range(0, lanes, 256)], axis=1)


def finish_kernel(tiles, info_ref, part_ref, beyond_ref, pair_ref, coeff_ref, tension_ref, out_ref, tension_out, active_out, facing_out):
    side, flip = info_ref[SIDE], info_ref[FLIP]
    exists = info_ref[FAR].astype(jnp.float32)
    sub = row_iota()
    own = tiles - 1
    planes = part_ref.shape[1]
    far, near = flip * (planes - 1), (1 - flip) * (planes - 1)

    def one(tile, carry):
        out_ref[0, near, tile] = part_ref[0, near, tile] + halo_terms(pair_ref, coeff_ref, tile, tiles, side, sub, 1)
        for plane in range(1, planes - 1):
            out_ref[0, plane, tile] = part_ref[0, plane, tile]
        out_ref[0, far, tile] = part_ref[0, far, tile] + exists * halo_terms(
            beyond_ref, coeff_ref, tile, tiles, side, sub, -1
        )
        return carry

    lax.fori_loop(0, own, one, 0)
    width = part_ref.shape[-1]
    total = None
    for layer in range(planes // 2):
        both = 0.5 * (out_ref[0, 2 * layer] + out_ref[0, 2 * layer + 1])
        mean = pooled(both.reshape(own * 8, width))
        old = tension_ref[layer]
        new = old + 0.5 * (mean - old)
        tension_out[layer] = new
        total = new if total is None else total + new
    active_out[...] = pooled(0.5 * total)
    facing_out[...] = active_out[pl.ds(pl.multiple_of(8 * (1 - side), 8), 8), :]


def finish_step(info, part, beyond, pair, coeffs, tension):
    tiles, _, width = pair.shape
    own = tiles - 1
    planes = part.shape[1]
    halo_spec = pl.BlockSpec((tiles, 8, width), lambda i: (0, 0, 0))
    u_spec = pl.BlockSpec((1, planes, own, 8, width), lambda i: (0, 0, 0, 0, 0))
    tension_spec = pl.BlockSpec(tension.shape, lambda i: (0, 0, 0))
    active_shape = (own * 2, width // 4)
    cells = planes * own * 8 * width
    return pl.pallas_call(
        functools.partial(finish_kernel, tiles),
        grid=(1,),
        in_specs=[
            pl.BlockSpec(memory_space=pltpu.SMEM),
            u_spec,
            halo_spec,
            halo_spec,
            pl.BlockSpec((4, tiles, 8, width), lambda i: (0, 0, 0, 0)),
            tension_spec,
        ],
        out_specs=[u_spec, tension_spec, pl.BlockSpec(active_shape, lambda i: (0, 0)), pl.BlockSpec((8, width // 4), lambda i: (0, 0))],
        out_shape=[
            jax.ShapeDtypeStruct(part.shape, jnp.float32),
            jax.ShapeDtypeStruct(tension.shape, jnp.float32),
            jax.ShapeDtypeStruct(active_shape, jnp.float32),
            jax.ShapeDtypeStruct((8, width // 4), jnp.float32),
        ],
        input_output_aliases={1: 0},
        compiler_params=params(),
        cost_estimate=cost(20 * cells, 20 * cells),
        name="finish",
    )(info, part, beyond, pair, coeffs, tension)


REACH = 4
ROWS = 24


class Weights:
    def __init__(self, side, own, width):
        row = lax.broadcasted_iota(jnp.int32, (ROWS, width), 0)
        lane = lax.broadcasted_iota(jnp.int32, (ROWS, width), 1)
        self.next_y = jnp.where((row == own - 1) & (side == 1), 0.0, 1.0)
        self.prev_y = jnp.where((row == 0) & (side == 0), 0.0, 1.0)
        self.next_x = jnp.where(lane == width - 1, 0.0, 1.0)
        self.prev_x = jnp.where(lane == 0, 0.0, 1.0)


def up_y(val):
    return pltpu.roll(val, ROWS - 1, 0)


def down_y(val):
    return pltpu.roll(val, 1, 0)


def slope_z(below, mid, above):
    return 0.5 * (above - below)


def smooth_z(below, mid, above):
    return 0.75 * mid + 0.125 * (above + below)


def gradients(below, mid, above, k):
    slope = slope_z(below, mid, above)
    smooth = smooth_z(below, mid, above)
    slope_s = 0.75 * slope + 0.125 * (up_y(slope) * k.next_y + down_y(slope) * k.prev_y)
    ahead = up_y(smooth) * k.next_y
    behind = down_y(smooth) * k.prev_y
    smooth_s = 0.75 * smooth + 0.125 * (ahead + behind)
    smooth_d = 0.5 * (ahead - behind)

    def smooth_x(val):
        return 0.75 * val + 0.125 * (left(val) * k.next_x + right(val) * k.prev_x)

    return (
        smooth_x(slope_s),
        smooth_x(smooth_d),
        0.5 * (left(smooth_s) * k.next_x - right(smooth_s) * k.prev_x),
    )


def force(below, mid, above, k):
    p_z = slope_z(below[0], mid[0], above[0])
    p_y = smooth_z(below[1], mid[1], above[1])
    p_x = smooth_z(below[2], mid[2], above[2])
    small, half = 0.125 * p_z, 0.5 * p_y
    both = 0.75 * p_z + up_y(small + half) * k.next_y + down_y(small - half) * k.prev_y
    p_x = 0.75 * p_x + 0.125 * (up_y(p_x) * k.next_y + down_y(p_x) * k.prev_y)
    small, half = 0.125 * both, 0.5 * p_x
    return 0.75 * both + left(small + half) * k.next_x + right(small - half) * k.prev_x


def deformation(below, mid, above, k):
    deform = []
    for comp in range(3):
        row = list(gradients(below[comp], mid[comp], above[comp], k))
        row[comp] = row[comp] + 1.0
        deform.append(row)
    return deform


def passive_stress(deform):
    right_c = {}
    for a_pos, b_pos in PAIRS:
        right_c[a_pos, b_pos] = sum(deform[i_pos][a_pos] * deform[i_pos][b_pos] for i_pos in range(3))
    strain = {}
    for a_pos, b_pos in PAIRS:
        strain[a_pos, b_pos] = 0.5 * (right_c[a_pos, b_pos] - (1.0 if a_pos == b_pos else 0.0))
    trace = strain[0, 0] + strain[1, 1] + strain[2, 2]
    second = {}
    for a_pos, b_pos in PAIRS:
        entry = (2.0 * SHEAR) * strain[a_pos, b_pos]
        if a_pos == b_pos:
            entry = entry + LAME_FIRST * trace
        second[a_pos, b_pos] = entry
        second[b_pos, a_pos] = entry
    return second


def times(deform, second):
    return [
        [sum(deform[i_pos][b_pos] * second[b_pos, a_pos] for b_pos in range(3)) for a_pos in range(3)]
        for i_pos in range(3)
    ]


def metric(deform, fdir):
    def cofactor(i_pos, j_pos):
        i_next, i_last = (i_pos + 1) % 3, (i_pos + 2) % 3
        j_next, j_last = (j_pos + 1) % 3, (j_pos + 2) % 3
        return deform[i_next][j_next] * deform[i_last][j_last] - deform[i_next][j_last] * deform[i_last][j_next]

    cof = [[cofactor(i_pos, j_pos) for j_pos in range(3)] for i_pos in range(3)]
    det = deform[0][0] * cof[0][0] + deform[0][1] * cof[0][1] + deform[0][2] * cof[0][2]
    scale = 1.0 / det
    inv = [[cof[i_pos][j_pos] * scale for i_pos in range(3)] for j_pos in range(3)]
    along = [sum(inv[a_pos][i_pos] * fdir[i_pos] for i_pos in range(3)) for a_pos in range(3)]
    comps = []
    for a_pos, b_pos in PAIRS:
        inner = sum(inv[a_pos][i_pos] * inv[b_pos][i_pos] for i_pos in range(3))
        comps.append(SIGMA_TRANS * inner + (SIGMA_LONG - SIGMA_TRANS) * along[a_pos] * along[b_pos])
    return comps


def inside(slab, slabs, offset):
    spot = slab + offset
    return jnp.where((spot >= 0) & (spot < slabs), 1.0, 0.0)


def gather_planes(field, slabs, reach):
    planes = {0: field}
    for offset in range(1, reach + 1):
        for shift in (offset % slabs, -offset % slabs):
            if shift not in planes:
                perm = [((i + shift) % slabs, i) for i in range(slabs)]
                planes[shift] = lax.ppermute(field, "slab", perm)
    return planes


def fiber_table():
    index = jnp.arange(128, dtype=jnp.float32)
    theta = -1.0 + 2.0 * index / (NFIB - 1)
    tilt = 0.3 * jnp.sin(3.0 * index)
    return jnp.stack([jnp.sin(tilt), jnp.cos(tilt) * jnp.sin(theta), jnp.cos(tilt) * jnp.cos(theta)])


def facing_kernel(info_ref, *refs):
    out_ref = refs[-1]
    first = pl.multiple_of(8 * (1 - info_ref[SIDE]), 8)
    for pos, ref in enumerate(refs[:-1]):
        for comp in range(ref.shape[0]):
            out_ref[pos, comp] = ref[comp, pl.ds(first, 8), :]


def facing_rows(info, fields):
    comps, _, width = fields[0].shape
    vmem = pl.BlockSpec(memory_space=pltpu.VMEM)
    return pl.pallas_call(
        facing_kernel,
        in_specs=[pl.BlockSpec(memory_space=pltpu.SMEM)] + [vmem] * len(fields),
        out_shape=jax.ShapeDtypeStruct((len(fields), comps, 8, width), jnp.float32),
        compiler_params=params(),
        cost_estimate=cost(0, 600_000),
        name="facing",
    )(info, *fields)


def passive_kernel(slabs, shifts, info_ref, table_ref, strip_ref, *refs):
    own_refs, (disp_out, stress_out, pull_out, disp_all) = refs[:-4], refs[-4:]
    slab = info_ref[SLAB]
    own, width = own_refs[0].shape[-2:]
    k = Weights(info_ref[SIDE], own, width)
    reach = REACH + 1

    def plane(comp, offset):
        spot = shifts.index(offset % slabs)
        return jnp.concatenate([own_refs[spot][comp], strip_ref[spot, comp]], axis=0)

    for offset in range(-reach, reach + 1):
        factor = inside(slab, slabs, offset)
        for comp in range(3):
            disp_all[comp, offset + reach] = plane(comp, offset) * factor

    tables = [jnp.broadcast_to(table_ref[comp : comp + 1], (8, 128)) for comp in range(3)]

    def direction(index, comp):
        index = index.astype(jnp.int32)
        rows = []
        for top in range(0, ROWS, 8):
            parts = [
                jnp.take_along_axis(tables[comp], index[top : top + 8, at : at + 128], axis=1, mode="promise_in_bounds")
                for at in range(0, width, 128)
            ]
            rows.append(jnp.concatenate(parts, axis=1))
        return jnp.concatenate(rows, axis=0)

    for step in range(2 * REACH + 1):
        offset = step - REACH
        below, mid, above = ([disp_all[comp, step + shift] for comp in range(3)] for shift in range(3))
        factor = inside(slab, slabs, offset)
        deform = deformation(below, mid, above, k)
        stress = times(deform, passive_stress(deform))
        index = plane(3, offset)
        fdir = [direction(index, comp) for comp in range(3)]
        for i_pos in range(3):
            pull = (ACTIVE_GAIN * factor) * sum(deform[i_pos][b_pos] * fdir[b_pos] for b_pos in range(3))
            for a_pos in range(3):
                stress_out[3 * i_pos + a_pos, step] = stress[i_pos][a_pos] * factor
                pull_out[3 * i_pos + a_pos, step] = pull * fdir[a_pos]
            disp_out[i_pos, step] = mid[i_pos]
            disp_out[3 + i_pos, step] = fdir[i_pos]


def passive_step(info, slabs, fields, strips):
    shifts = sorted(fields)
    width = strips.shape[-1]
    planes = 2 * REACH + 1
    shapes = [(6, planes), (9, planes), (9, planes)]
    vmem = pl.BlockSpec(memory_space=pltpu.VMEM)
    return pl.pallas_call(
        functools.partial(passive_kernel, slabs, shifts),
        in_specs=[pl.BlockSpec(memory_space=pltpu.SMEM)] + [vmem] * (2 + len(shifts)),
        out_shape=[jax.ShapeDtypeStruct((a, b, ROWS, width), jnp.float32) for a, b in shapes],
        scratch_shapes=[pltpu.VMEM((3, planes + 2, ROWS, width), jnp.float32)],
        compiler_params=params(),
        cost_estimate=cost(400 * planes * ROWS * width, 5_000_000),
        name="passive",
    )(info, fiber_table(), strips, *[fields[shift] for shift in shifts])


def mechanics_kernel(slabs, shifts, info_ref, disp_ref, stress_ref, pull_ref, *rest):
    active_refs, (disp_out, cond_out, d_one, p_two) = rest[:-4], rest[-4:]
    slab, side = info_ref[SLAB], info_ref[SIDE]
    own, width = disp_out.shape[-2:]
    k = Weights(side, own, width)

    def active_at(step):
        return active_refs[shifts.index((step - REACH) % slabs)][...]

    for step in range(1, 2 * REACH):
        act = [active_at(step + shift) for shift in (-1, 0, 1)]
        factor = inside(slab, slabs, step - REACH)
        for i_pos in range(3):
            stress = [
                [stress_ref[3 * i_pos + a_pos, step + shift] + act[shift + 1] * pull_ref[3 * i_pos + a_pos, step + shift] for a_pos in range(3)]
                for shift in (-1, 0, 1)
            ]
            moved = disp_ref[i_pos, step] + MECH_RATE * force(stress[0], stress[1], stress[2], k)
            d_one[i_pos, step] = moved * factor

    for step in range(2, 2 * REACH - 1):
        planes = [[d_one[comp, step + shift] for comp in range(3)] for shift in (-1, 0, 1)]
        deform = deformation(planes[0], planes[1], planes[2], k)
        second = passive_stress(deform)
        fdir = [disp_ref[3 + comp, step] for comp in range(3)]
        gain = ACTIVE_GAIN * active_at(step)
        for a_pos, b_pos in PAIRS:
            entry = second[a_pos, b_pos] + gain * fdir[a_pos] * fdir[b_pos]
            second[a_pos, b_pos] = entry
            second[b_pos, a_pos] = entry
        stress = times(deform, second)
        factor = inside(slab, slabs, step - REACH)
        for i_pos in range(3):
            for a_pos in range(3):
                p_two[3 * i_pos + a_pos, step] = stress[i_pos][a_pos] * factor

    last = []
    for step in (REACH - 1, REACH, REACH + 1):
        factor = inside(slab, slabs, step - REACH)
        row = []
        for i_pos in range(3):
            stress = [[p_two[3 * i_pos + a_pos, step + shift] for a_pos in range(3)] for shift in (-1, 0, 1)]
            moved = d_one[i_pos, step] + MECH_RATE * force(stress[0], stress[1], stress[2], k)
            row.append(moved * factor)
        last.append(row)
    deform = deformation(last[0], last[1], last[2], k)
    comps = metric(deform, [disp_ref[3 + comp, REACH] for comp in range(3)])
    for i_pos in range(3):
        disp_out[i_pos, 0] = last[1][i_pos][:own]
    for pos, comp in enumerate(comps):
        cond_out[pos, 0] = comp[:own]


def mechanics_step(info, slabs, own, active, window):
    shifts = sorted(active)
    width = active[0].shape[-1]
    planes = 2 * REACH + 1
    vmem = pl.BlockSpec(memory_space=pltpu.VMEM)
    return pl.pallas_call(
        functools.partial(mechanics_kernel, slabs, shifts),
        in_specs=[pl.BlockSpec(memory_space=pltpu.SMEM)] + [vmem] * (3 + len(shifts)),
        out_shape=[
            jax.ShapeDtypeStruct((3, 1, own, width), jnp.float32),
            jax.ShapeDtypeStruct((6, 1, own, width), jnp.float32),
        ],
        scratch_shapes=[
            pltpu.VMEM((3, planes, ROWS, width), jnp.float32),
            pltpu.VMEM((9, planes, ROWS, width), jnp.float32),
        ],
        compiler_params=params(),
        cost_estimate=cost(400 * planes * ROWS * width, 5_000_000),
        name="mechanics",
    )(info, *window, *[active[shift] for shift in shifts])


def on_device(states, cond, tension, fiber, disp):
    slabs = lax.axis_size("slab")
    slab, col = lax.axis_index("slab"), lax.axis_index("col")
    _, planes, rows, width = states.shape
    own = rows // 8
    flip = slab % 2
    far_exists = (slab > 0) & (slab < slabs - 1)
    info = jnp.stack([slab, col, flip, far_exists]).astype(jnp.int32)

    partner = {i: i ^ 1 for i in range(slabs)}
    other = {i: i if i in (0, slabs - 1) else ((i + 1) ^ 1) - 1 for i in range(slabs)}
    to_pair = list(partner.items())
    to_other = list(other.items())
    cross_pair = [(2 * i + c, 2 * j + 1 - c) for i, j in to_pair for c in range(2)]
    cross_other = [(2 * i + c, 2 * j + 1 - c) for i, j in to_other for c in range(2)]
    swap = [(0, 1), (1, 0)]

    tiled = states.reshape(4, planes, own, 8, width)
    far_z, near_z = flip * (planes - 1), (1 - flip) * (planes - 1)
    near = lax.dynamic_index_in_dim(tiled[0], near_z, 0, keepdims=False)
    far = lax.dynamic_index_in_dim(tiled[0], far_z, 0, keepdims=False)
    pair_own = lax.ppermute(near, "slab", to_pair)
    beyond_own = lax.ppermute(far, "slab", to_other)

    cond_strip = lax.ppermute(jnp.where(col == 0, cond[:, 0, -2:], cond[:, 0, :2]), "col", swap)
    facing = jnp.where(col == 0, tiled[:, :, own - 1], tiled[:, :, 0])
    strip = lax.ppermute(facing, "col", swap)
    facing_near = jnp.where(col == 0, near[own - 1], near[0])
    facing_far = jnp.where(col == 0, far[own - 1], far[0])
    pair_strip = lax.ppermute(facing_near, ("slab", "col"), cross_pair)
    beyond_strip = lax.ppermute(facing_far, ("slab", "col"), cross_other)

    field = jnp.concatenate([disp[:, 0], fiber.astype(jnp.float32)], axis=0)
    fields = gather_planes(field, slabs, REACH + 1)
    strips = lax.ppermute(facing_rows(info, [fields[shift] for shift in sorted(fields)]), "col", swap)

    coeffs = fine_coeffs(info, jnp.concatenate([cond[:, 0], cond_strip], axis=1))
    whole = jnp.concatenate([tiled, strip[:, :, None]], axis=2)
    u_parts, gates = (whole[0],), whole[1:]
    pair = jnp.concatenate([pair_own, pair_strip[None]], axis=0)
    beyond = jnp.concatenate([beyond_own, beyond_strip[None]], axis=0)
    window = None
    for turn_index in range(SUB):
        last = turn_index == SUB - 1
        result = local_step(info, u_parts, gates, coeffs, last)
        if turn_index == 1:
            window = passive_step(info, slabs, fields, strips)
        if last:
            part = result
        else:
            far, mid, near, gates = result
            far, near = halo_step(info, far, near, beyond, pair, coeffs)
            pair = lax.ppermute(near, "slab", to_pair)
            beyond = lax.ppermute(far, "slab", to_other)
            u_parts = (far, mid, near)
    states_next, tension_next, active, facing = finish_step(info, part, beyond, pair, coeffs, tension)
    active_strip = lax.ppermute(facing, "col", swap)
    active = gather_planes(jnp.concatenate([active, active_strip], axis=0), slabs, REACH)
    disp_next, cond_next = mechanics_step(info, slabs, disp.shape[2], active, window)
    return (states_next.reshape(states.shape), tension_next, disp_next, cond_next)


def solution(mesh):
    in_specs = (
        P(None, ("grp", "slab"), "col", None),
        P(None, ("grp", "slab"), "col", None),
        P(("grp", "slab"), "col", None),
        P(("grp", "slab"), "col", None),
        P(None, ("grp", "slab"), "col", None),
    )
    out_specs = (
        P(None, ("grp", "slab"), "col", None),
        P(("grp", "slab"), "col", None),
        P(None, ("grp", "slab"), "col", None),
        P(None, ("grp", "slab"), "col", None),
    )
    return jax.shard_map(
        on_device, mesh=mesh, in_specs=in_specs, out_specs=out_specs, check_vma=False
    )
```

```python
import functools

import jax
import jax.numpy as jnp
from jax import lax
from jax.experimental import pallas as pl
from jax.experimental.pallas import tpu as pltpu
from jax.sharding import PartitionSpec as P

SUB = 4
MECH_STEPS = 2
NFIB = 64

STEP_TIME = 0.05
LAME_FIRST = 1.0
SHEAR = 0.5
ACTIVE_GAIN = 0.5
MECH_RATE = 0.15
SIGMA_LONG = 0.16
SIGMA_TRANS = 0.04
PAIRS = ((0, 0), (1, 1), (2, 2), (0, 1), (0, 2), (1, 2))

C_ZZ, C_ZY, C_ZXR, C_ZXL, C_MID, C_YY, C_XXR, C_YXR, C_XXL, C_YXL = range(10)

SLAB, SIDE, FLIP, FAR = range(4)

HIGHEST = lax.Precision.HIGHEST
LIMIT = 40 * 1024 * 1024


def params(**kwargs):
    return pltpu.CompilerParams(vmem_limit_bytes=LIMIT, **kwargs)


def cost(flops, nbytes, trans=0):
    return pl.CostEstimate(flops=flops, bytes_accessed=nbytes, transcendentals=trans)


def row_iota():
    return lax.broadcasted_iota(jnp.int32, (8, 1024), 0)


def next_row(cur, nxt, sub):
    return pltpu.roll(jnp.where(sub == 0, nxt, cur), 7, 0)


def prev_row(cur, prv, sub):
    return pltpu.roll(jnp.where(sub == 7, prv, cur), 1, 0)


def left(val):
    return pltpu.roll(val, val.shape[-1] - 1, val.ndim - 1)


def right(val):
    return pltpu.roll(val, 1, val.ndim - 1)


def edge_masks(tile, side, own):
    before = jnp.where((tile == 0) & (side == 0), 0.0, 1.0)
    after = jnp.where((tile == own - 1) & (side == 1), 0.0, 1.0)
    return before, after


def ring_neighbours(tile, tiles):
    before = jnp.where(tile == 0, tiles - 1, tile - 1)
    after = jnp.where(tile == tiles - 1, 0, tile + 1)
    return before, after


def coeff_kernel(info_ref, cond_ref, strip_ref, out_ref):
    rows, width = cond_ref.shape[-2:]
    turn = jnp.where(info_ref[FLIP] == 1, -0.5, 0.5)
    upper_side = info_ref[SIDE] == 0
    fine = 4 * width
    mech = lax.broadcasted_iota(jnp.int32, (width, fine), 0)
    cell = lax.broadcasted_iota(jnp.int32, (width, fine), 1)
    own = rows // 2
    block = rows + 8
    sub = lax.broadcasted_iota(jnp.int32, (8, fine), 0)

    def spread(comps, shift):
        pick = jnp.where(mech == ((cell + shift) >> 2), 1.0, 0.0)
        flat = jnp.concatenate([part for comp in comps for part in (cond_ref[comp, 0], strip_ref[comp])], axis=0)
        wide = jnp.dot(flat, pick, precision=HIGHEST, preferred_element_type=jnp.float32)
        return [wide[pos * block : (pos + 1) * block] for pos in range(len(comps))]

    def both(first, second):
        return jnp.where(sub < 4, jnp.broadcast_to(first, (8, fine)), jnp.broadcast_to(second, (8, fine)))

    def store(index, wide):
        for tile in range(own):
            out_ref[index, tile] = both(wide[2 * tile : 2 * tile + 1], wide[2 * tile + 1 : 2 * tile + 2])
        head = both(wide[rows : rows + 1], wide[rows + 1 : rows + 2])
        tail = both(wide[block - 2 : block - 1], wide[block - 1 : block])
        out_ref[index, own] = jnp.where(upper_side, head, tail)

    zz, yy, xx, zy = spread((0, 1, 2, 3), 0)
    store(C_ZZ, zz)
    store(C_YY, yy)
    store(C_MID, 1.0 - 2.0 * (zz + yy + xx))
    store(C_ZY, turn * zy)
    xx, zx, yx = spread((2, 4, 5), -1)
    store(C_XXR, xx)
    store(C_ZXR, turn * zx)
    store(C_YXR, 0.5 * yx)
    xx, zx, yx = spread((2, 4, 5), 1)
    store(C_XXL, xx)
    store(C_ZXL, turn * zx)
    store(C_YXL, 0.5 * yx)


def fine_coeffs(info, cond, strip):
    rows, width = cond.shape[-2:]
    vmem = pl.BlockSpec(memory_space=pltpu.VMEM)
    return pl.pallas_call(
        coeff_kernel,
        in_specs=[pl.BlockSpec(memory_space=pltpu.SMEM), vmem, vmem],
        out_shape=jax.ShapeDtypeStruct((10, rows // 2 + 1, 8, 4 * width), jnp.float32),
        compiler_params=params(),
        cost_estimate=cost(2_000_000, 3_200_000),
        name="coeffs",
    )(info, cond, strip)


def pack_kernel(info_ref, states_ref, cond_ref, far_ref, near_ref, facing_ref, far_rows, near_rows, cond_rows, sems):
    side, flip = info_ref[SIDE], info_ref[FLIP]
    planes, own = states_ref.shape[1:3]
    far, near = flip * (planes - 1), (1 - flip) * (planes - 1)
    edge = (1 - side) * (own - 1)
    half = pl.multiple_of(8 * (1 - side), 8)
    moves = [
        (states_ref.at[0, far], far_ref),
        (states_ref.at[0, near], near_ref),
        (states_ref.at[0, far, edge], far_rows),
        (states_ref.at[0, near, edge], near_rows),
        (states_ref.at[:, :, edge], facing_ref),
        (cond_ref.at[:, 0, pl.ds(half, 8), :], cond_rows),
    ]
    copies = [pltpu.make_async_copy(src, dst, sems.at[pos]) for pos, (src, dst) in enumerate(moves)]
    for copy in copies:
        copy.start()
    for copy in copies:
        copy.wait()


def pack(info, tiled, cond):
    comps, planes, own, _, width = tiled.shape
    shapes = [(own, 8, width), (own, 8, width), (comps, planes, 8, width), (8, width), (8, width)]
    shapes.append((cond.shape[0], 8, cond.shape[-1]))
    return pl.pallas_call(
        pack_kernel,
        in_specs=[pl.BlockSpec(memory_space=pltpu.SMEM)] + [pl.BlockSpec(memory_space=pltpu.HBM)] * 2,
        out_specs=[pl.BlockSpec(memory_space=pltpu.VMEM)] * len(shapes),
        out_shape=[jax.ShapeDtypeStruct(shape, jnp.float32) for shape in shapes],
        scratch_shapes=[pltpu.SemaphoreType.DMA((len(shapes),))],
        compiler_params=params(),
        cost_estimate=cost(0, 2_500_000),
        name="pack",
    )(info, tiled, cond)


def fraction(val):
    return pl.reciprocal(val, approx=True)


def ionic(u, v, w, s):
    dt = STEP_TIME
    steep = 50.0 * u
    t_v = jnp.tanh(steep - 15.0)
    t_w = jnp.tanh(steep - 6.5)
    t_o = jnp.tanh(steep - 0.3)
    t_m = jnp.tanh(65.0 * u - 65.0 * 0.03)
    t_f = jnp.tanh(2.0458 * u - 2.0458 * 0.65)
    t_s = jnp.tanh(2.0994 * u - 2.0994 * 0.9087)
    hv, nv = 1.0 + t_v, 1.0 - t_v
    hw, nw = 1.0 + t_w, 1.0 - t_w
    no = 0.5 - 0.5 * t_o
    half_so = 0.5 * (30.0181 - 0.9957)
    r_vm = fraction(2.0 / dt * 605.0 + (2.0 / dt * 545.0) * t_o)
    r_wm = fraction(2.0 / dt * 37.5 - (2.0 / dt * 22.5) * t_m)
    r_so = fraction(2.0 / dt * (30.0181 - half_so) - (2.0 / dt * half_so) * t_f)
    r_s = fraction(9.3671 / dt + (6.6329 / dt) * t_w)
    r_o = fraction(2.0 / dt * 203.0 - (2.0 / dt * 197.0) * t_o)
    w_inf = 0.94 + no * (0.06 - u * (1.0 / 0.07))
    hvv = hv * v
    hww = hw * w
    fast = hvv * ((u - 0.3) * (0.5 * dt / 0.11 * 1.55 - (0.5 * dt / 0.11) * u))
    out = (u * nw) * r_o + hw * r_so
    slow = hww * (s * (0.5 * dt / 1.8875))
    v_new = v + (nv * (no - v)) * r_vm - hvv * (0.5 * dt / 1.4506)
    w_new = w + (nw * (w_inf - w)) * r_wm - hww * (0.5 * dt / 200.0)
    s_new = s + ((0.5 + 0.5 * t_s) - s) * r_s
    return fast + slow - out, v_new, w_new, s_new


FAR_HALF, NEAR_HALF = -1, 1


def half_place(info_ref, half):
    flip = info_ref[FLIP]
    return (flip, flip) if half == FAR_HALF else (1 - flip, 1 - flip)


def half_kernel(kind, half, tiles, per_block, info_ref, *refs):
    side = info_ref[SIDE]
    sub = row_iota()
    own = tiles - 1
    index, outer = half_place(info_ref, half)
    if kind == "first":
        whole_ref, coeff_ref, outer_out, inner_out, gate_out = refs
        spots = [2 * index + outer, 2 * index + 1 - outer, 2 - index]
        reads = [lambda t, z=z: whole_ref[0, z, t] for z in spots]
    elif kind == "middle":
        *u_refs, gate_ref, coeff_ref, outer_out, inner_out, gate_out = refs
        reads = [lambda t, ref=ref: ref[t] for ref in u_refs]
    else:
        *u_refs, gate_ref, coeff_ref = refs[:5]
        out_ref = refs[-1]
        reads = [lambda t, ref=ref: ref[t] for ref in u_refs]
        place = [outer, 1 - outer]

    def one(local_tile, carry):
        tile = local_tile if kind != "last" else pl.program_id(0) * per_block + local_tile
        before, after = ring_neighbours(tile, tiles)
        mask_before, mask_after = edge_masks(tile, side, own)
        cur = [read(tile) for read in reads]
        prv = [read(before) * mask_before for read in reads]
        nxt = [read(after) * mask_after for read in reads]

        def coeff(index):
            return coeff_ref[index, local_tile]

        for plane in range(2):
            u = cur[plane]
            if plane == 0:
                around = cur[1]
                wide, wide_nxt, wide_prv = cur[1], nxt[1], prv[1]
            else:
                around = cur[0] + cur[2]
                wide, wide_nxt, wide_prv = cur[2] - cur[0], nxt[2] - nxt[0], prv[2] - prv[0]
            u_next = next_row(u, nxt[plane], sub)
            u_prev = prev_row(u, prv[plane], sub)
            tilt = coeff(C_ZY) * (next_row(wide, wide_nxt, sub) - prev_row(wide, wide_prv, sub))
            tall = u_next - u_prev
            to_left = coeff(C_XXR) * u + coeff(C_YXR) * tall
            to_right = coeff(C_XXL) * u - coeff(C_YXL) * tall
            if half == FAR_HALF:
                to_left += coeff(C_ZXR) * wide
                to_right -= coeff(C_ZXL) * wide
            else:
                to_left -= coeff(C_ZXR) * wide
                to_right += coeff(C_ZXL) * wide
            base = coeff(C_MID) * u + coeff(C_ZZ) * around + coeff(C_YY) * (u_next + u_prev)
            base = base + tilt if half == FAR_HALF else base - tilt
            base += left(to_left) + right(to_right)
            chunk = 256
            for start in range(0, 1024, chunk):
                lanes = slice(start, start + chunk)
                if kind == "first":
                    gates = [whole_ref[1 + g, spots[plane], tile, :, lanes] for g in range(3)]
                else:
                    gates = [gate_ref[g, plane, local_tile, :, lanes] for g in range(3)]
                u_add, *gates = ionic(u[:, lanes], *gates)
                u_new = base[:, lanes] + u_add
                if kind == "last":
                    for comp, value in enumerate([u_new] + gates):
                        out_ref[comp, place[plane], local_tile, :, lanes] = value
                else:
                    (outer_out, inner_out)[plane][tile, :, lanes] = u_new
                    for comp, value in enumerate(gates):
                        gate_out[comp, plane, tile, :, lanes] = value
        return carry

    lax.fori_loop(0, per_block, one, 0)


def half_costs(tiles, width):
    cells = 2 * tiles * 8 * width
    return cost(100 * cells, 40 * cells, 11 * cells)


def half_step(kind, half, info, arrays, coeffs):
    _, tiles, _, width = coeffs.shape
    vmem = pl.BlockSpec(memory_space=pltpu.VMEM)
    plane = jax.ShapeDtypeStruct((tiles, 8, width), jnp.float32)
    return pl.pallas_call(
        functools.partial(half_kernel, kind, half, tiles, tiles),
        in_specs=[pl.BlockSpec(memory_space=pltpu.SMEM)] + [vmem] * (len(arrays) + 1),
        out_specs=[vmem] * 3,
        out_shape=[plane, plane, jax.ShapeDtypeStruct((3, 2, tiles, 8, width), jnp.float32)],
        compiler_params=params(),
        cost_estimate=half_costs(tiles, width),
        name=kind + ("_far" if half == FAR_HALF else "_near"),
    )(info, *arrays, coeffs)


def half_last(half, info, arrays, coeffs, states=None):
    _, tiles, _, width = coeffs.shape
    per_block = 2
    whole = pl.BlockSpec((tiles, 8, width), lambda i, info: (0, 0, 0))
    in_specs = [whole] * 3 + [
        pl.BlockSpec((3, 2, per_block, 8, width), lambda i, info: (0, 0, i, 0, 0)),
        pl.BlockSpec((10, per_block, 8, width), lambda i, info: (0, i, 0, 0)),
    ]
    operands = [*arrays, coeffs]
    aliases = {}
    if states is not None:
        in_specs.append(pl.BlockSpec(memory_space=pl.ANY))
        operands.append(states)
        aliases = {len(operands): 0}
    return pl.pallas_call(
        functools.partial(half_kernel, "last", half, tiles, per_block),
        grid_spec=pltpu.PrefetchScalarGridSpec(
            num_scalar_prefetch=1,
            grid=((tiles - 1) // per_block,),
            in_specs=in_specs,
            out_specs=pl.BlockSpec((4, 2, per_block, 8, width), lambda i, info: (0, half_place(info, half)[0], i, 0, 0)),
        ),
        out_shape=jax.ShapeDtypeStruct((4, 4, tiles - 1, 8, width), jnp.float32),
        input_output_aliases=aliases,
        compiler_params=params(),
        cost_estimate=half_costs(tiles, width),
        name="last" + ("_far" if half == FAR_HALF else "_near"),
    )(info, *operands)


def halo_terms(halo_ref, coeff_ref, tile, tiles, side, sub, half):
    before, after = ring_neighbours(tile, tiles)
    mask_before, mask_after = edge_masks(tile, side, tiles - 1)
    cur = halo_ref[tile]
    up = next_row(cur, halo_ref[after] * mask_after, sub)
    down = prev_row(cur, halo_ref[before] * mask_before, sub)
    cross = coeff_ref[C_ZY, tile] * (up - down)
    cross += left(coeff_ref[C_ZXR, tile] * cur) - right(coeff_ref[C_ZXL, tile] * cur)
    total = coeff_ref[C_ZZ, tile] * cur
    return total - cross if half == FAR_HALF else total + cross


def halo_kernel(half, tiles, info_ref, outer_ref, halo_ref, coeff_ref, out_ref):
    side = info_ref[SIDE]
    sub = row_iota()

    def one(tile, carry):
        out_ref[tile] = outer_ref[tile] + halo_terms(halo_ref, coeff_ref, tile, tiles, side, sub, half)
        return carry

    def kept(tile, carry):
        out_ref[tile] = outer_ref[tile]
        return carry

    if half == NEAR_HALF:
        lax.fori_loop(0, tiles, one, 0)
    else:
        exists = info_ref[FAR] == 1

        @pl.when(exists)
        def _():
            lax.fori_loop(0, tiles, one, 0)

        @pl.when(jnp.logical_not(exists))
        def _():
            lax.fori_loop(0, tiles, kept, 0)


def halo_step(half, info, outer, halo, coeffs):
    tiles, _, width = outer.shape
    vmem = pl.BlockSpec(memory_space=pltpu.VMEM)
    cells = tiles * 8 * width
    return pl.pallas_call(
        functools.partial(halo_kernel, half, tiles),
        in_specs=[pl.BlockSpec(memory_space=pltpu.SMEM)] + [vmem] * 3,
        out_specs=vmem,
        out_shape=jax.ShapeDtypeStruct(outer.shape, jnp.float32),
        compiler_params=params(),
        cost_estimate=cost(15 * cells, 20 * cells),
        name="halo" + ("_far" if half == FAR_HALF else "_near"),
    )(info, outer, halo, coeffs)


def pair_matrix(width, scale):
    fine = lax.broadcasted_iota(jnp.int32, (width, width // 2), 0)
    coarse = lax.broadcasted_iota(jnp.int32, (width, width // 2), 1)
    return jnp.where((fine >> 1) == coarse, scale, 0.0)


def row_pairs(count, scale):
    coarse = lax.broadcasted_iota(jnp.int32, (count // 2, count), 0)
    fine = lax.broadcasted_iota(jnp.int32, (count // 2, count), 1)
    return jnp.where((fine >> 1) == coarse, scale, 0.0)


def dot(a, b):
    return jnp.dot(a, b, precision=HIGHEST, preferred_element_type=jnp.float32)


def pooled(field):
    rows, lanes = field.shape
    few = dot(row_pairs(rows, 0.5), field)
    pick = pair_matrix(256, 0.5)
    return jnp.concatenate([dot(few[:, at : at + 256], pick) for at in range(0, lanes, 256)], axis=1)


def finish_kernel(half, tiles, info_ref, part_ref, halo_ref, coeff_ref, tension_ref, *refs):
    if half == FAR_HALF:
        out_ref, tension_out, active_out = refs
    else:
        active_ref, _, out_ref, tension_out, active_out, facing_out = refs
    side = info_ref[SIDE]
    sub = row_iota()
    own = tiles - 1
    _, outer = half_place(info_ref, half)
    out_ref[0, 1 - outer] = part_ref[0, 1 - outer]

    def one(tile, carry):
        out_ref[0, outer, tile] = part_ref[0, outer, tile] + halo_terms(halo_ref, coeff_ref, tile, tiles, side, sub, half)
        return carry

    if half == NEAR_HALF:
        lax.fori_loop(0, own, one, 0)
    else:
        exists = info_ref[FAR] == 1

        @pl.when(exists)
        def _():
            lax.fori_loop(0, own, one, 0)

        @pl.when(jnp.logical_not(exists))
        def _():
            out_ref[0, outer] = part_ref[0, outer]

    both = 0.5 * (out_ref[0, 0] + out_ref[0, 1])
    mean = pooled(both.reshape(own * 8, both.shape[-1]))
    old = tension_ref[0]
    new = old + 0.5 * (mean - old)
    tension_out[0] = new
    if half == FAR_HALF:
        active_out[...] = pooled(0.5 * new)
    else:
        active_out[...] = active_ref[...] + pooled(0.5 * new)
        facing_out[...] = active_out[pl.ds(pl.multiple_of(8 * (1 - side), 8), 8), :]


def finish_half(half, info, part, halo, coeffs, tension, active=None, tension_next=None):
    tiles, _, width = halo.shape
    own = tiles - 1
    active_shape = (own * 2, width // 4)
    z_half = lambda info: half_place(info, half)[0]
    u_spec = pl.BlockSpec((1, 2, own, 8, width), lambda i, info: (0, z_half(info), 0, 0, 0))
    tension_spec = pl.BlockSpec((1,) + tension.shape[1:], lambda i, info: (z_half(info), 0, 0))
    active_spec = pl.BlockSpec(active_shape, lambda i, info: (0, 0))
    in_specs = [
        u_spec,
        pl.BlockSpec((tiles, 8, width), lambda i, info: (0, 0, 0)),
        pl.BlockSpec((4, tiles, 8, width), lambda i, info: (0, 0, 0, 0)),
        tension_spec,
    ]
    operands = [part, halo, coeffs, tension]
    out_specs = [u_spec, tension_spec, active_spec]
    out_shape = [
        jax.ShapeDtypeStruct(part.shape, jnp.float32),
        jax.ShapeDtypeStruct(tension.shape, jnp.float32),
        jax.ShapeDtypeStruct(active_shape, jnp.float32),
    ]
    aliases = {1: 0}
    if half == NEAR_HALF:
        in_specs += [active_spec, pl.BlockSpec(memory_space=pl.ANY)]
        operands += [active, tension_next]
        aliases[len(operands)] = 1
        out_specs.append(pl.BlockSpec((8, width // 4), lambda i, info: (0, 0)))
        out_shape.append(jax.ShapeDtypeStruct((8, width // 4), jnp.float32))
    cells = 2 * own * 8 * width
    return pl.pallas_call(
        functools.partial(finish_kernel, half, tiles),
        grid_spec=pltpu.PrefetchScalarGridSpec(num_scalar_prefetch=1, grid=(1,), in_specs=in_specs, out_specs=out_specs),
        out_shape=out_shape,
        input_output_aliases=aliases,
        compiler_params=params(),
        cost_estimate=cost(20 * cells, 20 * cells),
        name="finish" + ("_far" if half == FAR_HALF else "_near"),
    )(info, *operands)


REACH = 4
ROWS = 24


class Weights:
    def __init__(self, side, own, width):
        row = lax.broadcasted_iota(jnp.int32, (ROWS, width), 0)
        lane = lax.broadcasted_iota(jnp.int32, (ROWS, width), 1)
        self.next_y = jnp.where((row == own - 1) & (side == 1), 0.0, 1.0)
        self.prev_y = jnp.where((row == 0) & (side == 0), 0.0, 1.0)
        self.next_x = jnp.where(lane == width - 1, 0.0, 1.0)
        self.prev_x = jnp.where(lane == 0, 0.0, 1.0)


def up_y(val):
    return pltpu.roll(val, ROWS - 1, 0)


def down_y(val):
    return pltpu.roll(val, 1, 0)


def slope_z(below, mid, above):
    return 0.5 * (above - below)


def smooth_z(below, mid, above):
    return 0.75 * mid + 0.125 * (above + below)


def gradients(below, mid, above, k):
    slope = slope_z(below, mid, above)
    smooth = smooth_z(below, mid, above)
    slope_s = 0.75 * slope + 0.125 * (up_y(slope) * k.next_y + down_y(slope) * k.prev_y)
    ahead = up_y(smooth) * k.next_y
    behind = down_y(smooth) * k.prev_y
    smooth_s = 0.75 * smooth + 0.125 * (ahead + behind)
    smooth_d = 0.5 * (ahead - behind)

    def smooth_x(val):
        return 0.75 * val + 0.125 * (left(val) * k.next_x + right(val) * k.prev_x)

    return (
        smooth_x(slope_s),
        smooth_x(smooth_d),
        0.5 * (left(smooth_s) * k.next_x - right(smooth_s) * k.prev_x),
    )


def force(below, mid, above, k):
    p_z = slope_z(below[0], mid[0], above[0])
    p_y = smooth_z(below[1], mid[1], above[1])
    p_x = smooth_z(below[2], mid[2], above[2])
    small, half = 0.125 * p_z, 0.5 * p_y
    both = 0.75 * p_z + up_y(small + half) * k.next_y + down_y(small - half) * k.prev_y
    p_x = 0.75 * p_x + 0.125 * (up_y(p_x) * k.next_y + down_y(p_x) * k.prev_y)
    small, half = 0.125 * both, 0.5 * p_x
    return 0.75 * both + left(small + half) * k.next_x + right(small - half) * k.prev_x


def deformation(below, mid, above, k):
    deform = []
    for comp in range(3):
        row = list(gradients(below[comp], mid[comp], above[comp], k))
        row[comp] = row[comp] + 1.0
        deform.append(row)
    return deform


def passive_stress(deform):
    right_c = {}
    for a_pos, b_pos in PAIRS:
        right_c[a_pos, b_pos] = sum(deform[i_pos][a_pos] * deform[i_pos][b_pos] for i_pos in range(3))
    strain = {}
    for a_pos, b_pos in PAIRS:
        strain[a_pos, b_pos] = 0.5 * (right_c[a_pos, b_pos] - (1.0 if a_pos == b_pos else 0.0))
    trace = strain[0, 0] + strain[1, 1] + strain[2, 2]
    second = {}
    for a_pos, b_pos in PAIRS:
        entry = (2.0 * SHEAR) * strain[a_pos, b_pos]
        if a_pos == b_pos:
            entry = entry + LAME_FIRST * trace
        second[a_pos, b_pos] = entry
        second[b_pos, a_pos] = entry
    return second


def times(deform, second):
    return [
        [sum(deform[i_pos][b_pos] * second[b_pos, a_pos] for b_pos in range(3)) for a_pos in range(3)]
        for i_pos in range(3)
    ]


def metric(deform, fdir):
    def cofactor(i_pos, j_pos):
        i_next, i_last = (i_pos + 1) % 3, (i_pos + 2) % 3
        j_next, j_last = (j_pos + 1) % 3, (j_pos + 2) % 3
        return deform[i_next][j_next] * deform[i_last][j_last] - deform[i_next][j_last] * deform[i_last][j_next]

    cof = [[cofactor(i_pos, j_pos) for j_pos in range(3)] for i_pos in range(3)]
    det = deform[0][0] * cof[0][0] + deform[0][1] * cof[0][1] + deform[0][2] * cof[0][2]
    scale = 1.0 / det
    inv = [[cof[i_pos][j_pos] * scale for i_pos in range(3)] for j_pos in range(3)]
    along = [sum(inv[a_pos][i_pos] * fdir[i_pos] for i_pos in range(3)) for a_pos in range(3)]
    comps = []
    for a_pos, b_pos in PAIRS:
        inner = sum(inv[a_pos][i_pos] * inv[b_pos][i_pos] for i_pos in range(3))
        comps.append(SIGMA_TRANS * inner + (SIGMA_LONG - SIGMA_TRANS) * along[a_pos] * along[b_pos])
    return comps


def inside(slab, slabs, offset):
    spot = slab + offset
    return jnp.where((spot >= 0) & (spot < slabs), 1.0, 0.0)


class Planes:
    def __init__(self, field, slabs, reach):
        self.slabs, self.reach = slabs, reach
        self.parts = [field[None]]
        self.doubling = slabs in (1, 2, 4, 8)
        self.step = 1

    def round(self):
        if self.doubling:
            if self.step < self.slabs:
                held = jnp.concatenate(self.parts, axis=0) if len(self.parts) > 1 else self.parts[0]
                perm = [(i, i ^ self.step) for i in range(self.slabs)]
                self.parts.append(lax.ppermute(held, "slab", perm))
                self.step *= 2
        elif self.step == 1:
            for shift in self.shifts()[1:]:
                perm = [((i + shift) % self.slabs, i) for i in range(self.slabs)]
                self.parts.append(lax.ppermute(self.parts[0], "slab", perm))
            self.step = 0

    def shifts(self):
        return sorted({offset % self.slabs for offset in range(-self.reach, self.reach + 1)})

    def spot(self, slab, offset):
        if self.doubling:
            return slab ^ jnp.clip(slab + offset, 0, self.slabs - 1)
        return self.shifts().index(offset % self.slabs)


def fiber_table():
    index = jnp.arange(128, dtype=jnp.float32)
    theta = -1.0 + 2.0 * index / (NFIB - 1)
    tilt = 0.3 * jnp.sin(3.0 * index)
    return jnp.stack([jnp.sin(tilt), jnp.cos(tilt) * jnp.sin(theta), jnp.cos(tilt) * jnp.cos(theta)])


def facing_kernel(info_ref, *refs):
    out_ref = refs[-1]
    first = pl.multiple_of(8 * (1 - info_ref[SIDE]), 8)
    at = 0
    for ref in refs[:-1]:
        for pos in range(ref.shape[0]):
            for comp in range(ref.shape[1]):
                out_ref[at, comp] = ref[pos, comp, pl.ds(first, 8), :]
            at += 1


def facing_rows(info, fields):
    _, comps, _, width = fields[0].shape
    count = sum(field.shape[0] for field in fields)
    vmem = pl.BlockSpec(memory_space=pltpu.VMEM)
    return pl.pallas_call(
        facing_kernel,
        in_specs=[pl.BlockSpec(memory_space=pltpu.SMEM)] + [vmem] * len(fields),
        out_shape=jax.ShapeDtypeStruct((count, comps, 8, width), jnp.float32),
        compiler_params=params(),
        cost_estimate=cost(0, 600_000),
        name="facing",
    )(info, *fields)


def passive_kernel(planes, info_ref, table_ref, strip_ref, *refs):
    own_refs, (disp_out, stress_out, pull_out, disp_all, field) = refs[:-5], refs[-5:]
    slab, slabs = info_ref[SLAB], planes.slabs
    own, width = own_refs[0].shape[-2:]
    k = Weights(info_ref[SIDE], own, width)
    reach = REACH + 1

    at = 0
    for ref in own_refs:
        for pos in range(ref.shape[0]):
            for comp in range(ref.shape[1]):
                field[at, comp, :own] = ref[pos, comp]
                field[at, comp, own:] = strip_ref[at, comp]
            at += 1

    def plane(comp, offset):
        return field[planes.spot(slab, offset), comp]

    for offset in range(-reach, reach + 1):
        factor = inside(slab, slabs, offset)
        for comp in range(3):
            disp_all[comp, offset + reach] = plane(comp, offset) * factor

    tables = [jnp.broadcast_to(table_ref[comp : comp + 1], (8, 128)) for comp in range(3)]

    def direction(index, comp):
        index = index.astype(jnp.int32)
        rows = []
        for top in range(0, ROWS, 8):
            parts = [
                jnp.take_along_axis(tables[comp], index[top : top + 8, at : at + 128], axis=1, mode="promise_in_bounds")
                for at in range(0, width, 128)
            ]
            rows.append(jnp.concatenate(parts, axis=1))
        return jnp.concatenate(rows, axis=0)

    for step in range(2 * REACH + 1):
        offset = step - REACH
        below, mid, above = ([disp_all[comp, step + shift] for comp in range(3)] for shift in range(3))
        factor = inside(slab, slabs, offset)
        deform = deformation(below, mid, above, k)
        stress = times(deform, passive_stress(deform))
        index = plane(3, offset)
        fdir = [direction(index, comp) for comp in range(3)]
        for i_pos in range(3):
            pull = (ACTIVE_GAIN * factor) * sum(deform[i_pos][b_pos] * fdir[b_pos] for b_pos in range(3))
            for a_pos in range(3):
                stress_out[3 * i_pos + a_pos, step] = stress[i_pos][a_pos] * factor
                pull_out[3 * i_pos + a_pos, step] = pull * fdir[a_pos]
            disp_out[i_pos, step] = mid[i_pos]
            disp_out[3 + i_pos, step] = fdir[i_pos]


def passive_step(info, planes, strips):
    width = strips.shape[-1]
    count = 2 * REACH + 1
    shapes = [(6, count), (9, count), (9, count)]
    vmem = pl.BlockSpec(memory_space=pltpu.VMEM)
    return pl.pallas_call(
        functools.partial(passive_kernel, planes),
        in_specs=[pl.BlockSpec(memory_space=pltpu.SMEM)] + [vmem] * (2 + len(planes.parts)),
        out_shape=[jax.ShapeDtypeStruct((a, b, ROWS, width), jnp.float32) for a, b in shapes],
        scratch_shapes=[
            pltpu.VMEM((3, count + 2, ROWS, width), jnp.float32),
            pltpu.VMEM(strips.shape[:2] + (ROWS, width), jnp.float32),
        ],
        compiler_params=params(),
        cost_estimate=cost(400 * count * ROWS * width, 5_000_000),
        name="passive",
    )(info, fiber_table(), strips, *planes.parts)


def mechanics_kernel(planes, info_ref, disp_ref, stress_ref, pull_ref, *rest):
    active_refs, (disp_out, cond_out, d_one, p_two, active) = rest[:-5], rest[-5:]
    slab, side, slabs = info_ref[SLAB], info_ref[SIDE], planes.slabs
    own, width = disp_out.shape[-2:]
    k = Weights(side, own, width)

    at = 0
    for ref in active_refs:
        active[at : at + ref.shape[0]] = ref[...]
        at += ref.shape[0]

    def active_at(step):
        return active[planes.spot(slab, step - REACH)]

    for step in range(1, 2 * REACH):
        act = [active_at(step + shift) for shift in (-1, 0, 1)]
        factor = inside(slab, slabs, step - REACH)
        for i_pos in range(3):
            stress = [
                [stress_ref[3 * i_pos + a_pos, step + shift] + act[shift + 1] * pull_ref[3 * i_pos + a_pos, step + shift] for a_pos in range(3)]
                for shift in (-1, 0, 1)
            ]
            moved = disp_ref[i_pos, step] + MECH_RATE * force(stress[0], stress[1], stress[2], k)
            d_one[i_pos, step] = moved * factor

    for step in range(2, 2 * REACH - 1):
        disp = [[d_one[comp, step + shift] for comp in range(3)] for shift in (-1, 0, 1)]
        deform = deformation(disp[0], disp[1], disp[2], k)
        second = passive_stress(deform)
        fdir = [disp_ref[3 + comp, step] for comp in range(3)]
        gain = ACTIVE_GAIN * active_at(step)
        for a_pos, b_pos in PAIRS:
            entry = second[a_pos, b_pos] + gain * fdir[a_pos] * fdir[b_pos]
            second[a_pos, b_pos] = entry
            second[b_pos, a_pos] = entry
        stress = times(deform, second)
        factor = inside(slab, slabs, step - REACH)
        for i_pos in range(3):
            for a_pos in range(3):
                p_two[3 * i_pos + a_pos, step] = stress[i_pos][a_pos] * factor

    last = []
    for step in (REACH - 1, REACH, REACH + 1):
        factor = inside(slab, slabs, step - REACH)
        row = []
        for i_pos in range(3):
            stress = [[p_two[3 * i_pos + a_pos, step + shift] for a_pos in range(3)] for shift in (-1, 0, 1)]
            moved = d_one[i_pos, step] + MECH_RATE * force(stress[0], stress[1], stress[2], k)
            row.append(moved * factor)
        last.append(row)
    deform = deformation(last[0], last[1], last[2], k)
    comps = metric(deform, [disp_ref[3 + comp, REACH] for comp in range(3)])
    for i_pos in range(3):
        disp_out[i_pos, 0] = last[1][i_pos][:own]
    for pos, comp in enumerate(comps):
        cond_out[pos, 0] = comp[:own]


def mechanics_step(info, own, planes, window):
    width = planes.parts[0].shape[-1]
    count = 2 * REACH + 1
    held = sum(part.shape[0] for part in planes.parts)
    vmem = pl.BlockSpec(memory_space=pltpu.VMEM)
    return pl.pallas_call(
        functools.partial(mechanics_kernel, planes),
        in_specs=[pl.BlockSpec(memory_space=pltpu.SMEM)] + [vmem] * (3 + len(planes.parts)),
        out_shape=[
            jax.ShapeDtypeStruct((3, 1, own, width), jnp.float32),
            jax.ShapeDtypeStruct((6, 1, own, width), jnp.float32),
        ],
        scratch_shapes=[
            pltpu.VMEM((3, count, ROWS, width), jnp.float32),
            pltpu.VMEM((9, count, ROWS, width), jnp.float32),
            pltpu.VMEM((held, ROWS, width), jnp.float32),
        ],
        compiler_params=params(),
        cost_estimate=cost(400 * count * ROWS * width, 5_000_000),
        name="mechanics",
    )(info, *window, *planes.parts)


def tie(*arrays):
    return lax.optimization_barrier(arrays)


def on_device(states, cond, tension, fiber, disp):
    slabs = lax.axis_size("slab")
    slab, col = lax.axis_index("slab"), lax.axis_index("col")
    _, planes, rows, width = states.shape
    own = rows // 8
    flip = slab % 2
    far_exists = (slab > 0) & (slab < slabs - 1)
    info = jnp.stack([slab, col, flip, far_exists]).astype(jnp.int32)

    pairs = [(i, i ^ 1) for i in range(slabs)]
    others = [(i, i if i in (0, slabs - 1) else ((i + 1) ^ 1) - 1) for i in range(slabs)]
    cross_pairs = [(2 * i + c, 2 * j + 1 - c) for i, j in pairs for c in range(2)]
    cross_others = [(2 * i + c, 2 * j + 1 - c) for i, j in others for c in range(2)]
    swap = [(0, 1), (1, 0)]

    tiled = states.reshape(4, planes, own, 8, width)
    far, near, facing, far_rows, near_rows, cond_rows = pack(info, tiled, cond)
    far_halo = lax.ppermute(far, "slab", others)
    near_halo = lax.ppermute(near, "slab", pairs)
    strip = lax.ppermute(facing, "col", swap)
    cond_strip = lax.ppermute(cond_rows, "col", swap)
    far_strip = lax.ppermute(far_rows, ("slab", "col"), cross_others)
    near_strip = lax.ppermute(near_rows, ("slab", "col"), cross_pairs)
    fields = Planes(jnp.concatenate([disp[:, 0], fiber.astype(jnp.float32)], axis=0), slabs, REACH + 1)

    coeffs = fine_coeffs(info, cond, cond_strip)
    whole = jnp.concatenate([tiled, strip[:, :, None]], axis=2)
    far_halo = jnp.concatenate([far_halo, far_strip[None]], axis=0)
    near_halo = jnp.concatenate([near_halo, near_strip[None]], axis=0)
    fields.round()

    far_part, far_inner, far_gates = half_step("first", FAR_HALF, info, (whole,), coeffs)
    near_part, near_inner, near_gates = half_step("first", NEAR_HALF, info, (whole,), coeffs)
    for turn_index in range(1, SUB):
        last = turn_index == SUB - 1
        far = halo_step(FAR_HALF, info, far_part, far_halo, coeffs)
        far_halo = lax.ppermute(far, "slab", others)
        if not last:
            (near_part, *fields.parts) = tie(near_part, *fields.parts)
            fields.round()
        far_arrays = (far, far_inner, near_inner, far_gates)
        if last:
            part = half_last(FAR_HALF, info, far_arrays, coeffs)
        else:
            far_part, far_next, far_gates = half_step("middle", FAR_HALF, info, far_arrays, coeffs)
        near = halo_step(NEAR_HALF, info, near_part, near_halo, coeffs)
        near_halo = lax.ppermute(near, "slab", pairs)
        near_arrays = (near, near_inner, far_inner, near_gates)
        if last:
            part = half_last(NEAR_HALF, info, near_arrays, coeffs, part)
        else:
            near_part, near_inner, near_gates = half_step("middle", NEAR_HALF, info, near_arrays, coeffs)
            far_inner = far_next
    strips = lax.ppermute(facing_rows(info, fields.parts), "col", swap)
    part, tension_next, active = finish_half(FAR_HALF, info, part, far_halo, coeffs, tension)
    window = passive_step(info, fields, strips)
    states_next, tension_next, active, facing = finish_half(
        NEAR_HALF, info, part, near_halo, coeffs, tension, active, tension_next
    )
    active_strip = lax.ppermute(facing, "col", swap)
    actives = Planes(jnp.concatenate([active, active_strip], axis=0), slabs, REACH)
    for _ in range(3):
        actives.round()
    disp_next, cond_next = mechanics_step(info, disp.shape[2], actives, window)
    return (states_next.reshape(states.shape), tension_next, disp_next, cond_next)


def solution(mesh):
    in_specs = (
        P(None, ("grp", "slab"), "col", None),
        P(None, ("grp", "slab"), "col", None),
        P(("grp", "slab"), "col", None),
        P(("grp", "slab"), "col", None),
        P(None, ("grp", "slab"), "col", None),
    )
    out_specs = (
        P(None, ("grp", "slab"), "col", None),
        P(("grp", "slab"), "col", None),
        P(None, ("grp", "slab"), "col", None),
        P(None, ("grp", "slab"), "col", None),
    )
    return jax.shard_map(
        on_device, mesh=mesh, in_specs=in_specs, out_specs=out_specs, check_vma=False
    )
```

```python
import functools

import jax
import jax.numpy as jnp
from jax import lax
from jax.experimental import pallas as pl
from jax.experimental.pallas import tpu as pltpu
from jax.sharding import PartitionSpec as P

SUB = 4
MECH_STEPS = 2
NFIB = 64

STEP_TIME = 0.05
LAME_FIRST = 1.0
SHEAR = 0.5
ACTIVE_GAIN = 0.5
MECH_RATE = 0.15
SIGMA_LONG = 0.16
SIGMA_TRANS = 0.04
PAIRS = ((0, 0), (1, 1), (2, 2), (0, 1), (0, 2), (1, 2))

C_ZZ, C_ZY, C_ZXR, C_ZXL, C_MID, C_YY, C_XXR, C_YXR, C_XXL, C_YXL = range(10)

SLAB, SIDE, FLIP, FAR = range(4)

HIGHEST = lax.Precision.HIGHEST
LIMIT = 40 * 1024 * 1024


def params(**kwargs):
    return pltpu.CompilerParams(vmem_limit_bytes=LIMIT, **kwargs)


def cost(flops, nbytes, trans=0):
    return pl.CostEstimate(flops=flops, bytes_accessed=nbytes, transcendentals=trans)


def row_iota():
    return lax.broadcasted_iota(jnp.int32, (8, 1024), 0)


def next_row(cur, nxt, sub):
    return pltpu.roll(jnp.where(sub == 0, nxt, cur), 7, 0)


def prev_row(cur, prv, sub):
    return pltpu.roll(jnp.where(sub == 7, prv, cur), 1, 0)


def left(val):
    return pltpu.roll(val, val.shape[-1] - 1, val.ndim - 1)


def right(val):
    return pltpu.roll(val, 1, val.ndim - 1)


def edge_masks(tile, side, own):
    before = jnp.where((tile == 0) & (side == 0), 0.0, 1.0)
    after = jnp.where((tile == own - 1) & (side == 1), 0.0, 1.0)
    return before, after


def ring_neighbours(tile, tiles):
    before = jnp.where(tile == 0, tiles - 1, tile - 1)
    after = jnp.where(tile == tiles - 1, 0, tile + 1)
    return before, after


def coeff_kernel(info_ref, cond_ref, strip_ref, out_ref):
    rows, width = cond_ref.shape[-2:]
    turn = jnp.where(info_ref[FLIP] == 1, -0.5, 0.5)
    upper_side = info_ref[SIDE] == 0
    fine = 4 * width
    mech = lax.broadcasted_iota(jnp.int32, (width, fine), 0)
    cell = lax.broadcasted_iota(jnp.int32, (width, fine), 1)
    own = rows // 2
    block = rows + 8
    sub = lax.broadcasted_iota(jnp.int32, (8, fine), 0)

    def spread(comps, shift):
        pick = jnp.where(mech == ((cell + shift) >> 2), 1.0, 0.0)
        flat = jnp.concatenate([part for comp in comps for part in (cond_ref[comp, 0], strip_ref[comp])], axis=0)
        wide = jnp.dot(flat, pick, precision=HIGHEST, preferred_element_type=jnp.float32)
        return [wide[pos * block : (pos + 1) * block] for pos in range(len(comps))]

    def both(first, second):
        return jnp.where(sub < 4, jnp.broadcast_to(first, (8, fine)), jnp.broadcast_to(second, (8, fine)))

    def store(index, wide):
        for tile in range(own):
            out_ref[index, tile] = both(wide[2 * tile : 2 * tile + 1], wide[2 * tile + 1 : 2 * tile + 2])
        head = both(wide[rows : rows + 1], wide[rows + 1 : rows + 2])
        tail = both(wide[block - 2 : block - 1], wide[block - 1 : block])
        out_ref[index, own] = jnp.where(upper_side, head, tail)

    zz, yy, xx, zy = spread((0, 1, 2, 3), 0)
    store(C_ZZ, zz)
    store(C_YY, yy)
    store(C_MID, 1.0 - 2.0 * (zz + yy + xx))
    store(C_ZY, turn * zy)
    xx, zx, yx = spread((2, 4, 5), -1)
    store(C_XXR, xx)
    store(C_ZXR, turn * zx)
    store(C_YXR, 0.5 * yx)
    xx, zx, yx = spread((2, 4, 5), 1)
    store(C_XXL, xx)
    store(C_ZXL, turn * zx)
    store(C_YXL, 0.5 * yx)


def fine_coeffs(info, cond, strip):
    rows, width = cond.shape[-2:]
    vmem = pl.BlockSpec(memory_space=pltpu.VMEM)
    return pl.pallas_call(
        coeff_kernel,
        in_specs=[pl.BlockSpec(memory_space=pltpu.SMEM), vmem, vmem],
        out_shape=jax.ShapeDtypeStruct((10, rows // 2 + 1, 8, 4 * width), jnp.float32),
        compiler_params=params(),
        cost_estimate=cost(2_000_000, 3_200_000),
        name="coeffs",
    )(info, cond, strip)


def pack_kernel(info_ref, states_ref, cond_ref, far_ref, near_ref, edge_ref, facing_ref, cond_rows, sems):
    side, flip = info_ref[SIDE], info_ref[FLIP]
    planes, own = states_ref.shape[1:3]
    far, near = flip * (planes - 1), (1 - flip) * (planes - 1)
    edge = (1 - side) * (own - 1)
    half = pl.multiple_of(8 * (1 - side), 8)
    moves = [
        (states_ref.at[0, far, edge], edge_ref.at[0]),
        (states_ref.at[0, near, edge], edge_ref.at[1]),
        (states_ref.at[0, far], far_ref),
        (states_ref.at[0, near], near_ref),
        (states_ref.at[:, :, edge], facing_ref),
        (cond_ref.at[:, 0, pl.ds(half, 8), :], cond_rows),
    ]
    copies = [pltpu.make_async_copy(src, dst, sems.at[pos]) for pos, (src, dst) in enumerate(moves)]
    for copy in copies:
        copy.start()
    for copy in copies:
        copy.wait()


def pack(info, tiled, cond):
    comps, planes, own, _, width = tiled.shape
    shapes = [(own, 8, width), (own, 8, width), (2, 8, width), (comps, planes, 8, width)]
    shapes.append((cond.shape[0], 8, cond.shape[-1]))
    return pl.pallas_call(
        pack_kernel,
        in_specs=[pl.BlockSpec(memory_space=pltpu.SMEM)] + [pl.BlockSpec(memory_space=pltpu.HBM)] * 2,
        out_specs=[pl.BlockSpec(memory_space=pltpu.VMEM)] * len(shapes),
        out_shape=[jax.ShapeDtypeStruct(shape, jnp.float32) for shape in shapes],
        scratch_shapes=[pltpu.SemaphoreType.DMA((6,))],
        compiler_params=pltpu.CompilerParams(vmem_limit_bytes=60 * 1024 * 1024),
        cost_estimate=cost(0, 2_500_000),
        name="pack",
    )(info, tiled, cond)


def fraction(val):
    return pl.reciprocal(val, approx=True)


def ionic(u, v, w, s):
    dt = STEP_TIME
    steep = 50.0 * u
    t_v = jnp.tanh(steep - 15.0)
    t_w = jnp.tanh(steep - 6.5)
    t_o = jnp.tanh(steep - 0.3)
    t_m = jnp.tanh(65.0 * u - 65.0 * 0.03)
    t_f = jnp.tanh(2.0458 * u - 2.0458 * 0.65)
    t_s = jnp.tanh(2.0994 * u - 2.0994 * 0.9087)
    hv, nv = 1.0 + t_v, 1.0 - t_v
    hw, nw = 1.0 + t_w, 1.0 - t_w
    no = 0.5 - 0.5 * t_o
    half_so = 0.5 * (30.0181 - 0.9957)
    r_vm = fraction(2.0 / dt * 605.0 + (2.0 / dt * 545.0) * t_o)
    r_wm = fraction(2.0 / dt * 37.5 - (2.0 / dt * 22.5) * t_m)
    r_so = fraction(2.0 / dt * (30.0181 - half_so) - (2.0 / dt * half_so) * t_f)
    r_s = fraction(9.3671 / dt + (6.6329 / dt) * t_w)
    r_o = fraction(2.0 / dt * 203.0 - (2.0 / dt * 197.0) * t_o)
    w_inf = 0.94 + no * (0.06 - u * (1.0 / 0.07))
    hvv = hv * v
    hww = hw * w
    fast = hvv * ((u - 0.3) * (0.5 * dt / 0.11 * 1.55 - (0.5 * dt / 0.11) * u))
    out = (u * nw) * r_o + hw * r_so
    slow = hww * (s * (0.5 * dt / 1.8875))
    v_new = v + (nv * (no - v)) * r_vm - hvv * (0.5 * dt / 1.4506)
    w_new = w + (nw * (w_inf - w)) * r_wm - hww * (0.5 * dt / 200.0)
    s_new = s + ((0.5 + 0.5 * t_s) - s) * r_s
    return fast + slow - out, v_new, w_new, s_new


FAR_HALF, NEAR_HALF = -1, 1


def half_place(info_ref, half):
    flip = info_ref[FLIP]
    return (flip, flip) if half == FAR_HALF else (1 - flip, 1 - flip)


def half_kernel(kind, half, tiles, info_ref, *refs):
    side = info_ref[SIDE]
    sub = row_iota()
    own = tiles - 1
    index, outer = half_place(info_ref, half)
    if kind == "first":
        whole_ref, coeff_ref, outer_out, inner_out, gate_out = refs
        spots = [2 * index + outer, 2 * index + 1 - outer, 2 - index]
        reads = [lambda t, z=z: whole_ref[0, z, t] for z in spots]
    else:
        *u_refs, gate_ref, coeff_ref, outer_out, inner_out, gate_out = refs
        reads = [lambda t, ref=ref: ref[t] for ref in u_refs]

    def diffused(tile):
        before, after = ring_neighbours(tile, tiles)
        mask_before, mask_after = edge_masks(tile, side, own)
        cur = [read(tile) for read in reads]
        prv = [read(before) * mask_before for read in reads]
        nxt = [read(after) * mask_after for read in reads]

        def coeff(index):
            return coeff_ref[index, tile]

        bases = []
        for plane in range(2):
            u = cur[plane]
            if plane == 0:
                around = cur[1]
                wide, wide_nxt, wide_prv = cur[1], nxt[1], prv[1]
            else:
                around = cur[0] + cur[2]
                wide, wide_nxt, wide_prv = cur[2] - cur[0], nxt[2] - nxt[0], prv[2] - prv[0]
            u_next = next_row(u, nxt[plane], sub)
            u_prev = prev_row(u, prv[plane], sub)
            tilt = coeff(C_ZY) * (next_row(wide, wide_nxt, sub) - prev_row(wide, wide_prv, sub))
            tall = u_next - u_prev
            to_left = coeff(C_XXR) * u + coeff(C_YXR) * tall
            to_right = coeff(C_XXL) * u - coeff(C_YXL) * tall
            if half == FAR_HALF:
                to_left += coeff(C_ZXR) * wide
                to_right -= coeff(C_ZXL) * wide
            else:
                to_left -= coeff(C_ZXR) * wide
                to_right += coeff(C_ZXL) * wide
            base = coeff(C_MID) * u + coeff(C_ZZ) * around + coeff(C_YY) * (u_next + u_prev)
            base = base + tilt if half == FAR_HALF else base - tilt
            bases.append(base + left(to_left) + right(to_right))
        return bases

    def react(tile, bases):
        chunk = 256
        for plane in range(2):
            for start in range(0, 1024, chunk):
                lanes = slice(start, start + chunk)
                if kind == "first":
                    u = whole_ref[0, spots[plane], tile, :, lanes]
                    gates = [whole_ref[1 + g, spots[plane], tile, :, lanes] for g in range(3)]
                else:
                    u = u_refs[plane][tile, :, lanes]
                    gates = [gate_ref[g, plane, tile, :, lanes] for g in range(3)]
                u_add, *gates = ionic(u, *gates)
                (outer_out, inner_out)[plane][tile, :, lanes] = bases[plane][:, lanes] + u_add
                for comp, value in enumerate(gates):
                    gate_out[comp, plane, tile, :, lanes] = value

    together = 2 if kind == "last" else 3

    def some(step, carry):
        numbers = [step * together + pos for pos in range(together)]
        held = [diffused(tile) for tile in numbers]
        for tile, bases in zip(numbers, held):
            react(tile, bases)
        return carry

    lax.fori_loop(0, (own if kind == "last" else tiles) // together, some, 0)


def half_step(kind, half, info, arrays, coeffs):
    _, tiles, _, width = coeffs.shape
    vmem = pl.BlockSpec(memory_space=pltpu.VMEM)
    kept = tiles - 1 if kind == "last" else tiles
    plane = jax.ShapeDtypeStruct((kept, 8, width), jnp.float32)
    cells = 2 * tiles * 8 * width
    return pl.pallas_call(
        functools.partial(half_kernel, kind, half, tiles),
        in_specs=[pl.BlockSpec(memory_space=pltpu.SMEM)] + [vmem] * (len(arrays) + 1),
        out_specs=[vmem] * 3,
        out_shape=[plane, plane, jax.ShapeDtypeStruct((3, 2, kept, 8, width), jnp.float32)],
        compiler_params=params(),
        cost_estimate=cost(100 * cells, 40 * cells, 11 * cells),
        name=kind + ("_far" if half == FAR_HALF else "_near"),
    )(info, *arrays, coeffs)


def halo_terms(halo_ref, coeff_ref, tile, tiles, side, sub, half):
    before, after = (tile - 1) % tiles, (tile + 1) % tiles
    cur, prv, nxt = halo_ref[tile], halo_ref[before], halo_ref[after]
    if tile == 0:
        prv = prv * jnp.where(side == 0, 0.0, 1.0)
    if tile == tiles - 2:
        nxt = nxt * jnp.where(side == 1, 0.0, 1.0)
    cross = coeff_ref[C_ZY, tile] * (next_row(cur, nxt, sub) - prev_row(cur, prv, sub))
    cross += left(coeff_ref[C_ZXR, tile] * cur) - right(coeff_ref[C_ZXL, tile] * cur)
    total = coeff_ref[C_ZZ, tile] * cur
    return total - cross if half == FAR_HALF else total + cross


def add_halo(half, tiles, kept, info_ref, outer_ref, halo_ref, coeff_ref, out_ref):
    side = info_ref[SIDE]
    sub = row_iota()

    def fill():
        for tile in range(kept):
            out_ref[tile] = outer_ref[tile] + halo_terms(halo_ref, coeff_ref, tile, tiles, side, sub, half)

    if half == NEAR_HALF:
        fill()
    else:
        exists = info_ref[FAR] == 1
        pl.when(exists)(fill)

        @pl.when(jnp.logical_not(exists))
        def _():
            out_ref[...] = outer_ref[...]


def halo_kernel(half, tiles, info_ref, outer_ref, halo_ref, coeff_ref, out_ref):
    add_halo(half, tiles, tiles, info_ref, outer_ref, halo_ref, coeff_ref, out_ref)


def halo_step(half, info, outer, halo, coeffs):
    tiles, _, width = outer.shape
    vmem = pl.BlockSpec(memory_space=pltpu.VMEM)
    cells = tiles * 8 * width
    return pl.pallas_call(
        functools.partial(halo_kernel, half, tiles),
        in_specs=[pl.BlockSpec(memory_space=pltpu.SMEM)] + [vmem] * 3,
        out_specs=vmem,
        out_shape=jax.ShapeDtypeStruct(outer.shape, jnp.float32),
        compiler_params=params(),
        cost_estimate=cost(15 * cells, 20 * cells),
        name="halo" + ("_far" if half == FAR_HALF else "_near"),
    )(info, outer, halo, coeffs)


def pooled(field, rows_ref):
    rows, lanes = field.shape
    fine = lax.broadcasted_iota(jnp.int32, (256, 128), 0)
    coarse = lax.broadcasted_iota(jnp.int32, (256, 128), 1)
    pick = jnp.where((fine >> 1) == coarse, 0.25, 0.0).astype(jnp.bfloat16)
    few = []
    for chunk in range(lanes // 128):
        rows_ref[chunk, :rows] = field[:, 128 * chunk : 128 * chunk + 128]
        even = rows_ref[chunk, pl.ds(0, rows // 2, stride=2), :]
        few.append(even + rows_ref[chunk, pl.ds(1, rows // 2, stride=2), :])
    pairs = [jnp.concatenate(few[pos : pos + 2], axis=1) for pos in range(0, len(few), 2)]
    rest = jnp.concatenate(pairs, axis=0)
    total = None
    for _ in range(3):
        part = rest.astype(jnp.bfloat16)
        rest = rest - part.astype(jnp.float32)
        mean = jnp.dot(part, pick, preferred_element_type=jnp.float32)
        total = mean if total is None else total + mean
    count = rows // 2
    return jnp.concatenate([total[pos * count : (pos + 1) * count] for pos in range(len(pairs))], axis=1)


def finish_kernel(half, tiles, info_ref, outer_ref, inner_ref, gate_ref, halo_ref, coeff_ref, tension_ref, *refs):
    if half == FAR_HALF:
        states_out, tension_out, active_out, u_ref, layer_ref, rows_ref, sems = refs
    else:
        active_ref, _, _, states_out, tension_out, active_out, facing_out, u_ref, layer_ref, rows_ref, sems = refs
    index, outer = half_place(info_ref, half)
    place = [2 * index + outer, 2 * index + 1 - outer]
    moves = [(gate_ref.at[g, plane], states_out.at[1 + g, place[plane]]) for g in range(3) for plane in range(2)]
    moves.append((inner_ref, states_out.at[0, place[1]]))
    copies = [pltpu.make_async_copy(src, dst, sems.at[pos]) for pos, (src, dst) in enumerate(moves)]
    for copy in copies:
        copy.start()
    own = tiles - 1
    add_halo(half, tiles, own, info_ref, outer_ref, halo_ref, coeff_ref, u_ref)
    copies.append(pltpu.make_async_copy(u_ref, states_out.at[0, place[0]], sems.at[len(moves)]))
    copies[-1].start()
    both = 0.5 * (u_ref[...] + inner_ref[...])
    mean = pooled(both.reshape(own * 8, both.shape[-1]), rows_ref)
    old = tension_ref[index]
    new = old + 0.5 * (mean - old)
    layer_ref[...] = new
    copies.append(pltpu.make_async_copy(layer_ref, tension_out.at[index], sems.at[len(moves) + 1]))
    copies[-1].start()
    mean = pooled(0.5 * new, rows_ref)
    if half == FAR_HALF:
        active_out[...] = mean
    else:
        active_out[...] = active_ref[...] + mean
        facing_out[...] = active_out[pl.ds(pl.multiple_of(8 * (1 - info_ref[SIDE]), 8), 8), :]
    for copy in copies:
        copy.wait()


def finish_half(half, info, arrays, halo, coeffs, tension, active=None, states=None, tension_next=None):
    tiles, _, width = halo.shape
    own = tiles - 1
    active_shape = (own * 2, width // 4)
    vmem, hbm = pl.BlockSpec(memory_space=pltpu.VMEM), pl.BlockSpec(memory_space=pltpu.HBM)
    in_specs = [pl.BlockSpec(memory_space=pltpu.SMEM)] + [vmem] * 6
    operands = [*arrays, halo, coeffs, tension]
    out_specs = [hbm, hbm, vmem]
    out_shape = [
        jax.ShapeDtypeStruct((4, 4, own, 8, width), jnp.float32),
        jax.ShapeDtypeStruct(tension.shape, jnp.float32),
        jax.ShapeDtypeStruct(active_shape, jnp.float32),
    ]
    aliases = {}
    if half == NEAR_HALF:
        in_specs += [vmem, hbm, hbm]
        operands += [active, states, tension_next]
        aliases = {8: 0, 9: 1}
        out_specs.append(vmem)
        out_shape.append(jax.ShapeDtypeStruct((8, width // 4), jnp.float32))
    cells = 2 * own * 8 * width
    return pl.pallas_call(
        functools.partial(finish_kernel, half, tiles),
        in_specs=in_specs,
        out_specs=out_specs,
        out_shape=out_shape,
        scratch_shapes=[
            pltpu.VMEM((own, 8, width), jnp.float32),
            pltpu.VMEM(tension.shape[1:], jnp.float32),
            pltpu.VMEM((width // 128, own * 8, 128), jnp.float32),
            pltpu.SemaphoreType.DMA((9,)),
        ],
        input_output_aliases=aliases,
        compiler_params=params(),
        cost_estimate=cost(20 * cells, 20 * cells),
        name="finish" + ("_far" if half == FAR_HALF else "_near"),
    )(info, *operands)


REACH = 4
ROWS = 24


class Weights:
    def __init__(self, side, own, width):
        row = lax.broadcasted_iota(jnp.int32, (ROWS, width), 0)
        lane = lax.broadcasted_iota(jnp.int32, (ROWS, width), 1)
        self.next_y = jnp.where((row == own - 1) & (side == 1), 0.0, 1.0)
        self.prev_y = jnp.where((row == 0) & (side == 0), 0.0, 1.0)
        self.next_x = jnp.where(lane == width - 1, 0.0, 1.0)
        self.prev_x = jnp.where(lane == 0, 0.0, 1.0)


def up_y(val):
    return pltpu.roll(val, ROWS - 1, 0)


def down_y(val):
    return pltpu.roll(val, 1, 0)


def slope_z(below, mid, above):
    return 0.5 * (above - below)


def smooth_z(below, mid, above):
    return 0.75 * mid + 0.125 * (above + below)


def gradients(below, mid, above, k):
    slope = slope_z(below, mid, above)
    smooth = smooth_z(below, mid, above)
    slope_s = 0.75 * slope + 0.125 * (up_y(slope) * k.next_y + down_y(slope) * k.prev_y)
    ahead = up_y(smooth) * k.next_y
    behind = down_y(smooth) * k.prev_y
    smooth_s = 0.75 * smooth + 0.125 * (ahead + behind)
    smooth_d = 0.5 * (ahead - behind)

    def smooth_x(val):
        return 0.75 * val + 0.125 * (left(val) * k.next_x + right(val) * k.prev_x)

    return (
        smooth_x(slope_s),
        smooth_x(smooth_d),
        0.5 * (left(smooth_s) * k.next_x - right(smooth_s) * k.prev_x),
    )


def force(below, mid, above, k):
    p_z = slope_z(below[0], mid[0], above[0])
    p_y = smooth_z(below[1], mid[1], above[1])
    p_x = smooth_z(below[2], mid[2], above[2])
    small, half = 0.125 * p_z, 0.5 * p_y
    both = 0.75 * p_z + up_y(small + half) * k.next_y + down_y(small - half) * k.prev_y
    p_x = 0.75 * p_x + 0.125 * (up_y(p_x) * k.next_y + down_y(p_x) * k.prev_y)
    small, half = 0.125 * both, 0.5 * p_x
    return 0.75 * both + left(small + half) * k.next_x + right(small - half) * k.prev_x


def deformation(below, mid, above, k):
    deform = []
    for comp in range(3):
        row = list(gradients(below[comp], mid[comp], above[comp], k))
        row[comp] = row[comp] + 1.0
        deform.append(row)
    return deform


def passive_stress(deform):
    right_c = {}
    for a_pos, b_pos in PAIRS:
        right_c[a_pos, b_pos] = sum(deform[i_pos][a_pos] * deform[i_pos][b_pos] for i_pos in range(3))
    strain = {}
    for a_pos, b_pos in PAIRS:
        strain[a_pos, b_pos] = 0.5 * (right_c[a_pos, b_pos] - (1.0 if a_pos == b_pos else 0.0))
    trace = strain[0, 0] + strain[1, 1] + strain[2, 2]
    second = {}
    for a_pos, b_pos in PAIRS:
        entry = (2.0 * SHEAR) * strain[a_pos, b_pos]
        if a_pos == b_pos:
            entry = entry + LAME_FIRST * trace
        second[a_pos, b_pos] = entry
        second[b_pos, a_pos] = entry
    return second


def times(deform, second):
    return [
        [sum(deform[i_pos][b_pos] * second[b_pos, a_pos] for b_pos in range(3)) for a_pos in range(3)]
        for i_pos in range(3)
    ]


def metric(deform, fdir):
    def cofactor(i_pos, j_pos):
        i_next, i_last = (i_pos + 1) % 3, (i_pos + 2) % 3
        j_next, j_last = (j_pos + 1) % 3, (j_pos + 2) % 3
        return deform[i_next][j_next] * deform[i_last][j_last] - deform[i_next][j_last] * deform[i_last][j_next]

    cof = [[cofactor(i_pos, j_pos) for j_pos in range(3)] for i_pos in range(3)]
    det = deform[0][0] * cof[0][0] + deform[0][1] * cof[0][1] + deform[0][2] * cof[0][2]
    scale = 1.0 / det
    inv = [[cof[i_pos][j_pos] * scale for i_pos in range(3)] for j_pos in range(3)]
    along = [sum(inv[a_pos][i_pos] * fdir[i_pos] for i_pos in range(3)) for a_pos in range(3)]
    comps = []
    for a_pos, b_pos in PAIRS:
        inner = sum(inv[a_pos][i_pos] * inv[b_pos][i_pos] for i_pos in range(3))
        comps.append(SIGMA_TRANS * inner + (SIGMA_LONG - SIGMA_TRANS) * along[a_pos] * along[b_pos])
    return comps


def inside(slab, slabs, offset):
    spot = slab + offset
    return jnp.where((spot >= 0) & (spot < slabs), 1.0, 0.0)


class Planes:
    def __init__(self, field, slabs, reach):
        self.slabs, self.reach = slabs, reach
        self.parts = [field[None]]
        self.doubling = slabs in (1, 2, 4, 8)
        self.step = 1

    def round(self):
        if self.doubling:
            if self.step < self.slabs:
                held = jnp.concatenate(self.parts, axis=0) if len(self.parts) > 1 else self.parts[0]
                perm = [(i, i ^ self.step) for i in range(self.slabs)]
                self.parts.append(lax.ppermute(held, "slab", perm))
                self.step *= 2
        elif self.step == 1:
            for shift in self.shifts()[1:]:
                perm = [((i + shift) % self.slabs, i) for i in range(self.slabs)]
                self.parts.append(lax.ppermute(self.parts[0], "slab", perm))
            self.step = 0

    def shifts(self):
        return sorted({offset % self.slabs for offset in range(-self.reach, self.reach + 1)})

    def spot(self, slab, offset):
        if self.doubling:
            return slab ^ jnp.clip(slab + offset, 0, self.slabs - 1)
        return self.shifts().index(offset % self.slabs)


def fiber_table():
    index = jnp.arange(128, dtype=jnp.float32)
    theta = -1.0 + 2.0 * index / (NFIB - 1)
    tilt = 0.3 * jnp.sin(3.0 * index)
    return jnp.stack([jnp.sin(tilt), jnp.cos(tilt) * jnp.sin(theta), jnp.cos(tilt) * jnp.cos(theta)])


def facing_kernel(info_ref, *refs):
    out_ref = refs[-1]
    first = pl.multiple_of(8 * (1 - info_ref[SIDE]), 8)
    at = 0
    for ref in refs[:-1]:
        for pos in range(ref.shape[0]):
            for comp in range(ref.shape[1]):
                out_ref[at, comp] = ref[pos, comp, pl.ds(first, 8), :]
            at += 1


def facing_rows(info, fields):
    _, comps, _, width = fields[0].shape
    count = sum(field.shape[0] for field in fields)
    vmem = pl.BlockSpec(memory_space=pltpu.VMEM)
    return pl.pallas_call(
        facing_kernel,
        in_specs=[pl.BlockSpec(memory_space=pltpu.SMEM)] + [vmem] * len(fields),
        out_shape=jax.ShapeDtypeStruct((count, comps, 8, width), jnp.float32),
        compiler_params=params(),
        cost_estimate=cost(0, 600_000),
        name="facing",
    )(info, *fields)


def passive_kernel(planes, info_ref, table_ref, strip_ref, *refs):
    own_refs, (disp_out, stress_out, pull_out, disp_all, field) = refs[:-5], refs[-5:]
    slab, slabs = info_ref[SLAB], planes.slabs
    own, width = own_refs[0].shape[-2:]
    k = Weights(info_ref[SIDE], own, width)
    reach = REACH + 1

    at = 0
    for ref in own_refs:
        for pos in range(ref.shape[0]):
            for comp in range(ref.shape[1]):
                field[at, comp, :own] = ref[pos, comp]
                field[at, comp, own:] = strip_ref[at, comp]
            at += 1

    def plane(comp, offset):
        return field[planes.spot(slab, offset), comp]

    for offset in range(-reach, reach + 1):
        factor = inside(slab, slabs, offset)
        for comp in range(3):
            disp_all[comp, offset + reach] = plane(comp, offset) * factor

    tables = [jnp.broadcast_to(table_ref[comp : comp + 1], (8, 128)) for comp in range(3)]

    def direction(index, comp):
        index = index.astype(jnp.int32)
        rows = []
        for top in range(0, ROWS, 8):
            parts = [
                jnp.take_along_axis(tables[comp], index[top : top + 8, at : at + 128], axis=1, mode="promise_in_bounds")
                for at in range(0, width, 128)
            ]
            rows.append(jnp.concatenate(parts, axis=1))
        return jnp.concatenate(rows, axis=0)

    for step in range(2 * REACH + 1):
        offset = step - REACH
        below, mid, above = ([disp_all[comp, step + shift] for comp in range(3)] for shift in range(3))
        factor = inside(slab, slabs, offset)
        deform = deformation(below, mid, above, k)
        stress = times(deform, passive_stress(deform))
        index = plane(3, offset)
        fdir = [direction(index, comp) for comp in range(3)]
        for i_pos in range(3):
            pull = (ACTIVE_GAIN * factor) * sum(deform[i_pos][b_pos] * fdir[b_pos] for b_pos in range(3))
            for a_pos in range(3):
                stress_out[3 * i_pos + a_pos, step] = stress[i_pos][a_pos] * factor
                pull_out[3 * i_pos + a_pos, step] = pull * fdir[a_pos]
            disp_out[i_pos, step] = mid[i_pos]
            disp_out[3 + i_pos, step] = fdir[i_pos]


def passive_step(info, planes, strips):
    width = strips.shape[-1]
    count = 2 * REACH + 1
    shapes = [(6, count), (9, count), (9, count)]
    vmem = pl.BlockSpec(memory_space=pltpu.VMEM)
    return pl.pallas_call(
        functools.partial(passive_kernel, planes),
        in_specs=[pl.BlockSpec(memory_space=pltpu.SMEM)] + [vmem] * (2 + len(planes.parts)),
        out_shape=[jax.ShapeDtypeStruct((a, b, ROWS, width), jnp.float32) for a, b in shapes],
        scratch_shapes=[
            pltpu.VMEM((3, count + 2, ROWS, width), jnp.float32),
            pltpu.VMEM(strips.shape[:2] + (ROWS, width), jnp.float32),
        ],
        compiler_params=params(),
        cost_estimate=cost(400 * count * ROWS * width, 5_000_000),
        name="passive",
    )(info, fiber_table(), strips, *planes.parts)


def mechanics_kernel(planes, info_ref, disp_ref, stress_ref, pull_ref, *rest):
    active_refs, (disp_out, cond_out, d_one, p_two, active) = rest[:-5], rest[-5:]
    slab, side, slabs = info_ref[SLAB], info_ref[SIDE], planes.slabs
    own, width = disp_out.shape[-2:]
    k = Weights(side, own, width)

    at = 0
    for ref in active_refs:
        active[at : at + ref.shape[0]] = ref[...]
        at += ref.shape[0]

    def active_at(step):
        return active[planes.spot(slab, step - REACH)]

    for step in range(1, 2 * REACH):
        act = [active_at(step + shift) for shift in (-1, 0, 1)]
        factor = inside(slab, slabs, step - REACH)
        for i_pos in range(3):
            stress = [
                [stress_ref[3 * i_pos + a_pos, step + shift] + act[shift + 1] * pull_ref[3 * i_pos + a_pos, step + shift] for a_pos in range(3)]
                for shift in (-1, 0, 1)
            ]
            moved = disp_ref[i_pos, step] + MECH_RATE * force(stress[0], stress[1], stress[2], k)
            d_one[i_pos, step] = moved * factor

    for step in range(2, 2 * REACH - 1):
        disp = [[d_one[comp, step + shift] for comp in range(3)] for shift in (-1, 0, 1)]
        deform = deformation(disp[0], disp[1], disp[2], k)
        second = passive_stress(deform)
        fdir = [disp_ref[3 + comp, step] for comp in range(3)]
        gain = ACTIVE_GAIN * active_at(step)
        for a_pos, b_pos in PAIRS:
            entry = second[a_pos, b_pos] + gain * fdir[a_pos] * fdir[b_pos]
            second[a_pos, b_pos] = entry
            second[b_pos, a_pos] = entry
        stress = times(deform, second)
        factor = inside(slab, slabs, step - REACH)
        for i_pos in range(3):
            for a_pos in range(3):
                p_two[3 * i_pos + a_pos, step] = stress[i_pos][a_pos] * factor

    last = []
    for step in (REACH - 1, REACH, REACH + 1):
        factor = inside(slab, slabs, step - REACH)
        row = []
        for i_pos in range(3):
            stress = [[p_two[3 * i_pos + a_pos, step + shift] for a_pos in range(3)] for shift in (-1, 0, 1)]
            moved = d_one[i_pos, step] + MECH_RATE * force(stress[0], stress[1], stress[2], k)
            row.append(moved * factor)
        last.append(row)
    deform = deformation(last[0], last[1], last[2], k)
    comps = metric(deform, [disp_ref[3 + comp, REACH] for comp in range(3)])
    for i_pos in range(3):
        disp_out[i_pos, 0] = last[1][i_pos][:own]
    for pos, comp in enumerate(comps):
        cond_out[pos, 0] = comp[:own]


def mechanics_step(info, own, planes, window):
    width = planes.parts[0].shape[-1]
    count = 2 * REACH + 1
    held = sum(part.shape[0] for part in planes.parts)
    vmem = pl.BlockSpec(memory_space=pltpu.VMEM)
    return pl.pallas_call(
        functools.partial(mechanics_kernel, planes),
        in_specs=[pl.BlockSpec(memory_space=pltpu.SMEM)] + [vmem] * (3 + len(planes.parts)),
        out_shape=[
            jax.ShapeDtypeStruct((3, 1, own, width), jnp.float32),
            jax.ShapeDtypeStruct((6, 1, own, width), jnp.float32),
        ],
        scratch_shapes=[
            pltpu.VMEM((3, count, ROWS, width), jnp.float32),
            pltpu.VMEM((9, count, ROWS, width), jnp.float32),
            pltpu.VMEM((held, ROWS, width), jnp.float32),
        ],
        compiler_params=params(),
        cost_estimate=cost(400 * count * ROWS * width, 5_000_000),
        name="mechanics",
    )(info, *window, *planes.parts)


def tie(*arrays):
    return lax.optimization_barrier(arrays)


def on_device(states, cond, tension, fiber, disp):
    slabs = lax.axis_size("slab")
    slab, col = lax.axis_index("slab"), lax.axis_index("col")
    _, planes, rows, width = states.shape
    own = rows // 8
    flip = slab % 2
    far_exists = (slab > 0) & (slab < slabs - 1)
    info = jnp.stack([slab, col, flip, far_exists]).astype(jnp.int32)

    pairs = [(i, i ^ 1) for i in range(slabs)]
    others = [(i, i if i in (0, slabs - 1) else ((i + 1) ^ 1) - 1) for i in range(slabs)]
    swap = [(0, 1), (1, 0)]

    tiled = states.reshape(4, planes, own, 8, width)
    fields = Planes(jnp.concatenate([disp[:, 0], fiber.astype(jnp.float32)], axis=0), slabs, REACH + 1)
    far, near, edges, facing, cond_rows = pack(info, tiled, cond)
    edges = lax.ppermute(edges, "col", swap)
    fields.round()
    edges, *fields.parts = tie(edges, *fields.parts)
    far_halo = lax.ppermute(jnp.concatenate([far, edges[:1]], axis=0), "slab", others)
    near_halo = lax.ppermute(jnp.concatenate([near, edges[1:]], axis=0), "slab", pairs)
    strip = lax.ppermute(facing, "col", swap)
    cond_strip = lax.ppermute(cond_rows, "col", swap)

    coeffs = fine_coeffs(info, cond, cond_strip)
    whole = jnp.concatenate([tiled, strip[:, :, None]], axis=2)

    far_part, far_inner, far_gates = half_step("first", FAR_HALF, info, (whole,), coeffs)
    near_part, near_inner, near_gates = half_step("first", NEAR_HALF, info, (whole,), coeffs)
    for turn_index in range(1, SUB):
        last = turn_index == SUB - 1
        far = halo_step(FAR_HALF, info, far_part, far_halo, coeffs)
        far_halo = lax.ppermute(far, "slab", others)
        if not last:
            (near_part, *fields.parts) = tie(near_part, *fields.parts)
            fields.round()
        far_arrays = (far, far_inner, near_inner, far_gates)
        kind = "last" if last else "middle"
        far_part, far_next, far_gates = half_step(kind, FAR_HALF, info, far_arrays, coeffs)
        near = halo_step(NEAR_HALF, info, near_part, near_halo, coeffs)
        near_halo = lax.ppermute(near, "slab", pairs)
        near_arrays = (near, near_inner, far_inner, near_gates)
        near_part, near_inner, near_gates = half_step(kind, NEAR_HALF, info, near_arrays, coeffs)
        far_inner = far_next
    strips = lax.ppermute(facing_rows(info, fields.parts), "col", swap)
    far_arrays = (far_part, far_inner, far_gates)
    near_arrays = (near_part, near_inner, near_gates)
    states_next, tension_next, active = finish_half(FAR_HALF, info, far_arrays, far_halo, coeffs, tension)
    window = passive_step(info, fields, strips)
    states_next, tension_next, active, facing = finish_half(
        NEAR_HALF, info, near_arrays, near_halo, coeffs, tension, active, states_next, tension_next
    )
    active_strip = lax.ppermute(facing, "col", swap)
    actives = Planes(jnp.concatenate([active, active_strip], axis=0), slabs, REACH)
    for _ in range(3):
        actives.round()
    disp_next, cond_next = mechanics_step(info, disp.shape[2], actives, window)
    return (states_next.reshape(states.shape), tension_next, disp_next, cond_next)


def solution(mesh):
    in_specs = (
        P(None, ("grp", "slab"), "col", None),
        P(None, ("grp", "slab"), "col", None),
        P(("grp", "slab"), "col", None),
        P(("grp", "slab"), "col", None),
        P(None, ("grp", "slab"), "col", None),
    )
    out_specs = (
        P(None, ("grp", "slab"), "col", None),
        P(("grp", "slab"), "col", None),
        P(None, ("grp", "slab"), "col", None),
        P(None, ("grp", "slab"), "col", None),
    )
    return jax.shard_map(
        on_device, mesh=mesh, in_specs=in_specs, out_specs=out_specs, check_vma=False
    )
```

```python
import functools

import jax
import jax.numpy as jnp
from jax import lax
from jax.experimental import pallas as pl
from jax.experimental.pallas import tpu as pltpu
from jax.sharding import PartitionSpec as P

SUB = 4
MECH_STEPS = 2
NFIB = 64

STEP_TIME = 0.05
LAME_FIRST = 1.0
SHEAR = 0.5
ACTIVE_GAIN = 0.5
MECH_RATE = 0.15
SIGMA_LONG = 0.16
SIGMA_TRANS = 0.04
PAIRS = ((0, 0), (1, 1), (2, 2), (0, 1), (0, 2), (1, 2))

C_ZZ, C_ZY, C_ZXR, C_ZXL, C_MID, C_YY, C_XXR, C_YXR, C_XXL, C_YXL = range(10)

SLAB, SIDE, FLIP, FAR = range(4)

HIGHEST = lax.Precision.HIGHEST
LIMIT = 40 * 1024 * 1024


def params(**kwargs):
    return pltpu.CompilerParams(vmem_limit_bytes=LIMIT, **kwargs)


def cost(flops, nbytes, trans=0):
    return pl.CostEstimate(flops=flops, bytes_accessed=nbytes, transcendentals=trans)


def row_iota():
    return lax.broadcasted_iota(jnp.int32, (8, 1024), 0)


def next_row(cur, nxt, sub):
    return pltpu.roll(jnp.where(sub == 0, nxt, cur), 7, 0)


def prev_row(cur, prv, sub):
    return pltpu.roll(jnp.where(sub == 7, prv, cur), 1, 0)


def left(val):
    return pltpu.roll(val, val.shape[-1] - 1, val.ndim - 1)


def right(val):
    return pltpu.roll(val, 1, val.ndim - 1)


def edge_masks(tile, side, own):
    before = jnp.where((tile == 0) & (side == 0), 0.0, 1.0)
    after = jnp.where((tile == own - 1) & (side == 1), 0.0, 1.0)
    return before, after


def ring_neighbours(tile, tiles):
    before = jnp.where(tile == 0, tiles - 1, tile - 1)
    after = jnp.where(tile == tiles - 1, 0, tile + 1)
    return before, after


def coeff_kernel(info_ref, cond_ref, strip_ref, out_ref):
    rows, width = cond_ref.shape[-2:]
    turn = jnp.where(info_ref[FLIP] == 1, -0.5, 0.5)
    upper_side = info_ref[SIDE] == 0
    fine = 4 * width
    mech = lax.broadcasted_iota(jnp.int32, (width, fine), 0)
    cell = lax.broadcasted_iota(jnp.int32, (width, fine), 1)
    own = rows // 2
    block = rows + 8
    sub = lax.broadcasted_iota(jnp.int32, (8, fine), 0)

    def spread(comps, shift):
        pick = jnp.where(mech == ((cell + shift) >> 2), 1.0, 0.0)
        flat = jnp.concatenate([part for comp in comps for part in (cond_ref[comp, 0], strip_ref[comp])], axis=0)
        wide = jnp.dot(flat, pick, precision=HIGHEST, preferred_element_type=jnp.float32)
        return [wide[pos * block : (pos + 1) * block] for pos in range(len(comps))]

    def both(first, second):
        return jnp.where(sub < 4, jnp.broadcast_to(first, (8, fine)), jnp.broadcast_to(second, (8, fine)))

    def store(index, wide):
        for tile in range(own):
            out_ref[index, tile] = both(wide[2 * tile : 2 * tile + 1], wide[2 * tile + 1 : 2 * tile + 2])
        head = both(wide[rows : rows + 1], wide[rows + 1 : rows + 2])
        tail = both(wide[block - 2 : block - 1], wide[block - 1 : block])
        out_ref[index, own] = jnp.where(upper_side, head, tail)

    zz, yy, xx, zy = spread((0, 1, 2, 3), 0)
    store(C_ZZ, zz)
    store(C_YY, yy)
    store(C_MID, 1.0 - 2.0 * (zz + yy + xx))
    store(C_ZY, turn * zy)
    xx, zx, yx = spread((2, 4, 5), -1)
    store(C_XXR, xx)
    store(C_ZXR, turn * zx)
    store(C_YXR, 0.5 * yx)
    xx, zx, yx = spread((2, 4, 5), 1)
    store(C_XXL, xx)
    store(C_ZXL, turn * zx)
    store(C_YXL, 0.5 * yx)


def fine_coeffs(info, cond, strip):
    rows, width = cond.shape[-2:]
    vmem = pl.BlockSpec(memory_space=pltpu.VMEM)
    return pl.pallas_call(
        coeff_kernel,
        in_specs=[pl.BlockSpec(memory_space=pltpu.SMEM), vmem, vmem],
        out_shape=jax.ShapeDtypeStruct((10, rows // 2 + 1, 8, 4 * width), jnp.float32),
        compiler_params=params(),
        cost_estimate=cost(2_000_000, 3_200_000),
        name="coeffs",
    )(info, cond, strip)


SENT, FIELD = 17, 4


def packed_strip(strip, side):
    half = strip.shape[-1] // 2
    low, high = strip[:, :half], strip[:, half:]
    sub = lax.broadcasted_iota(jnp.int32, low.shape, 0)
    first = jnp.where(side == 0, low, pltpu.roll(low, 4, 0))
    second = jnp.where(side == 0, pltpu.roll(high, 4, 0), high)
    return jnp.where(sub < 4, first, second)


def store_sent(ref, tile, tiles, value, side):
    half = value.shape[-1] // 2
    if tile < tiles - 1:
        ref[tile] = value[:, :half]
        ref[tiles - 1 + tile] = value[:, half:]
    else:
        ref[2 * tile] = packed_strip(value, side)


def load_sent(ref, tile, tiles, side):
    if tile < tiles - 1:
        return jnp.concatenate([ref[tile], ref[tiles - 1 + tile]], axis=1)
    packed = ref[2 * tile]
    turned = pltpu.roll(packed, 4, 0)
    return jnp.concatenate([jnp.where(side == 0, packed, turned), jnp.where(side == 0, turned, packed)], axis=1)


SMEM = pl.BlockSpec(memory_space=pltpu.SMEM)
VMEM = pl.BlockSpec(memory_space=pltpu.VMEM)


def shape_of(*shape):
    return jax.ShapeDtypeStruct(shape, jnp.float32)


def facing_kernel(info_ref, states_ref, cond_ref, edge_ref, facing_ref, cond_rows):
    flip, side = info_ref[FLIP], info_ref[SIDE]
    comps, planes, own = states_ref.shape[:3]
    edge = (1 - side) * (own - 1)
    edge_ref[0] = states_ref[0, flip * (planes - 1), edge]
    edge_ref[1] = states_ref[0, (1 - flip) * (planes - 1), edge]
    for comp in range(comps):
        for plane in range(planes):
            facing_ref[comp, plane] = states_ref[comp, plane, edge]
    first = pl.multiple_of(8 * (1 - side), 8)
    for comp in range(cond_ref.shape[0]):
        cond_rows[comp] = cond_ref[comp, 0, pl.ds(first, 8), :]


def sends_kernel(info_ref, edge_ref, states_ref, disp_ref, fiber_ref, far_ref, near_ref):
    flip, side = info_ref[FLIP], info_ref[SIDE]
    planes, own = states_ref.shape[1:3]
    for pos, (ref, plane) in enumerate([(far_ref, flip * (planes - 1)), (near_ref, (1 - flip) * (planes - 1))]):
        for tile in range(own):
            store_sent(ref, tile, own + 1, states_ref[0, plane, tile], side)
        store_sent(ref, own, own + 1, edge_ref[pos], side)
    for comp in range(3):
        near_ref[SENT + comp] = jnp.concatenate([disp_ref[comp, 0, :8], disp_ref[comp, 0, 8:]], axis=1)
    index = fiber_ref[0].astype(jnp.float32)
    near_ref[SENT + 3] = jnp.concatenate([index[:8], index[8:]], axis=1)


def facing_parts(info, tiled, cond):
    comps, planes, _, _, width = tiled.shape
    return pl.pallas_call(
        facing_kernel,
        in_specs=[SMEM, VMEM, VMEM],
        out_specs=[VMEM] * 3,
        out_shape=[
            shape_of(2, 8, width),
            shape_of(comps, planes, 8, width),
            shape_of(cond.shape[0], 8, cond.shape[-1]),
        ],
        compiler_params=params(),
        cost_estimate=cost(0, 1_200_000),
        name="facing_parts",
    )(info, tiled, cond)


def first_sends(info, edges, tiled, disp, fiber):
    width = tiled.shape[-1]
    return pl.pallas_call(
        sends_kernel,
        in_specs=[SMEM] + [VMEM] * 4,
        out_specs=[VMEM] * 2,
        out_shape=[shape_of(SENT, 8, width // 2), shape_of(SENT + FIELD, 8, width // 2)],
        compiler_params=params(),
        cost_estimate=cost(0, 1_200_000),
        name="sends",
    )(info, edges, tiled, disp, fiber)


def fraction(val):
    return pl.reciprocal(val, approx=True)


def ionic(u, v, w, s):
    dt = STEP_TIME
    steep = 50.0 * u
    t_v = jnp.tanh(steep - 15.0)
    t_w = jnp.tanh(steep - 6.5)
    t_o = jnp.tanh(steep - 0.3)
    t_m = jnp.tanh(65.0 * u - 65.0 * 0.03)
    t_f = jnp.tanh(2.0458 * u - 2.0458 * 0.65)
    t_s = jnp.tanh(2.0994 * u - 2.0994 * 0.9087)
    hv, nv = 1.0 + t_v, 1.0 - t_v
    hw, nw = 1.0 + t_w, 1.0 - t_w
    no = 0.5 - 0.5 * t_o
    half_so = 0.5 * (30.0181 - 0.9957)
    r_vm = fraction(2.0 / dt * 605.0 + (2.0 / dt * 545.0) * t_o)
    r_wm = fraction(2.0 / dt * 37.5 - (2.0 / dt * 22.5) * t_m)
    r_so = fraction(2.0 / dt * (30.0181 - half_so) - (2.0 / dt * half_so) * t_f)
    r_s = fraction(9.3671 / dt + (6.6329 / dt) * t_w)
    r_o = fraction(2.0 / dt * 203.0 - (2.0 / dt * 197.0) * t_o)
    w_inf = 0.94 + no * (0.06 - u * (1.0 / 0.07))
    hvv = hv * v
    hww = hw * w
    fast = hvv * ((u - 0.3) * (0.5 * dt / 0.11 * 1.55 - (0.5 * dt / 0.11) * u))
    out = (u * nw) * r_o + hw * r_so
    slow = hww * (s * (0.5 * dt / 1.8875))
    v_new = v + (nv * (no - v)) * r_vm - hvv * (0.5 * dt / 1.4506)
    w_new = w + (nw * (w_inf - w)) * r_wm - hww * (0.5 * dt / 200.0)
    s_new = s + ((0.5 + 0.5 * t_s) - s) * r_s
    return fast + slow - out, v_new, w_new, s_new


FAR_HALF, NEAR_HALF = -1, 1


def half_place(info_ref, half):
    flip = info_ref[FLIP]
    return (flip, flip) if half == FAR_HALF else (1 - flip, 1 - flip)


def half_kernel(kind, half, tiles, info_ref, *refs):
    side = info_ref[SIDE]
    sub = row_iota()
    own = tiles - 1
    index, outer = half_place(info_ref, half)
    if kind == "first":
        whole_ref, coeff_ref, outer_out, inner_out, gate_out = refs
        spots = [2 * index + outer, 2 * index + 1 - outer, 2 - index]
        reads = [lambda t, z=z: whole_ref[0, z, t] for z in spots]
    else:
        *u_refs, gate_ref, coeff_ref, outer_out, inner_out, gate_out = refs
        reads = [lambda t, ref=ref: ref[t] for ref in u_refs]

    def diffused(tile):
        before, after = ring_neighbours(tile, tiles)
        mask_before, mask_after = edge_masks(tile, side, own)
        cur = [read(tile) for read in reads]
        prv = [read(before) * mask_before for read in reads]
        nxt = [read(after) * mask_after for read in reads]

        def coeff(index):
            return coeff_ref[index, tile]

        bases = []
        for plane in range(2):
            u = cur[plane]
            if plane == 0:
                around = cur[1]
                wide, wide_nxt, wide_prv = cur[1], nxt[1], prv[1]
            else:
                around = cur[0] + cur[2]
                wide, wide_nxt, wide_prv = cur[2] - cur[0], nxt[2] - nxt[0], prv[2] - prv[0]
            u_next = next_row(u, nxt[plane], sub)
            u_prev = prev_row(u, prv[plane], sub)
            tilt = coeff(C_ZY) * (next_row(wide, wide_nxt, sub) - prev_row(wide, wide_prv, sub))
            tall = u_next - u_prev
            to_left = coeff(C_XXR) * u + coeff(C_YXR) * tall
            to_right = coeff(C_XXL) * u - coeff(C_YXL) * tall
            if half == FAR_HALF:
                to_left += coeff(C_ZXR) * wide
                to_right -= coeff(C_ZXL) * wide
            else:
                to_left -= coeff(C_ZXR) * wide
                to_right += coeff(C_ZXL) * wide
            base = coeff(C_MID) * u + coeff(C_ZZ) * around + coeff(C_YY) * (u_next + u_prev)
            base = base + tilt if half == FAR_HALF else base - tilt
            bases.append(base + left(to_left) + right(to_right))
        return bases

    def react(tile, bases):
        chunk = 256
        for plane in range(2):
            for start in range(0, 1024, chunk):
                lanes = slice(start, start + chunk)
                if kind == "first":
                    u = whole_ref[0, spots[plane], tile, :, lanes]
                    gates = [whole_ref[1 + g, spots[plane], tile, :, lanes] for g in range(3)]
                else:
                    u = u_refs[plane][tile, :, lanes]
                    gates = [gate_ref[g, plane, tile, :, lanes] for g in range(3)]
                u_add, *gates = ionic(u, *gates)
                (outer_out, inner_out)[plane][tile, :, lanes] = bases[plane][:, lanes] + u_add
                for comp, value in enumerate(gates):
                    gate_out[comp, plane, tile, :, lanes] = value

    together = 2 if kind == "last" else 3

    def some(step, carry):
        numbers = [step * together + pos for pos in range(together)]
        held = [diffused(tile) for tile in numbers]
        for tile, bases in zip(numbers, held):
            react(tile, bases)
        return carry

    lax.fori_loop(0, (own if kind == "last" else tiles) // together, some, 0)


def half_step(kind, half, info, arrays, coeffs):
    _, tiles, _, width = coeffs.shape
    vmem = pl.BlockSpec(memory_space=pltpu.VMEM)
    kept = tiles - 1 if kind == "last" else tiles
    plane = jax.ShapeDtypeStruct((kept, 8, width), jnp.float32)
    cells = 2 * tiles * 8 * width
    return pl.pallas_call(
        functools.partial(half_kernel, kind, half, tiles),
        in_specs=[pl.BlockSpec(memory_space=pltpu.SMEM)] + [vmem] * (len(arrays) + 1),
        out_specs=[vmem] * 3,
        out_shape=[plane, plane, jax.ShapeDtypeStruct((3, 2, kept, 8, width), jnp.float32)],
        compiler_params=params(),
        cost_estimate=cost(100 * cells, 40 * cells, 11 * cells),
        name=kind + ("_far" if half == FAR_HALF else "_near"),
    )(info, *arrays, coeffs)


def halo_terms(halo_ref, coeff_ref, tile, tiles, side, sub, half):
    before, after = (tile - 1) % tiles, (tile + 1) % tiles
    cur, prv, nxt = (load_sent(halo_ref, at, tiles, side) for at in (tile, before, after))
    if tile == 0:
        prv = prv * jnp.where(side == 0, 0.0, 1.0)
    if tile == tiles - 2:
        nxt = nxt * jnp.where(side == 1, 0.0, 1.0)
    cross = coeff_ref[C_ZY, tile] * (next_row(cur, nxt, sub) - prev_row(cur, prv, sub))
    cross += left(coeff_ref[C_ZXR, tile] * cur) - right(coeff_ref[C_ZXL, tile] * cur)
    total = coeff_ref[C_ZZ, tile] * cur
    return total - cross if half == FAR_HALF else total + cross


def add_halo(half, tiles, kept, info_ref, outer_ref, halo_ref, coeff_ref, out_ref, sent_ref=None):
    side = info_ref[SIDE]
    sub = row_iota()

    def fill(beyond=True):
        for tile in range(kept):
            value = outer_ref[tile]
            if beyond:
                value += halo_terms(halo_ref, coeff_ref, tile, tiles, side, sub, half)
            out_ref[tile] = value
            if sent_ref is not None:
                store_sent(sent_ref, tile, tiles, value, side)

    if half == NEAR_HALF:
        fill()
    else:
        exists = info_ref[FAR] == 1
        pl.when(exists)(fill)
        pl.when(jnp.logical_not(exists))(functools.partial(fill, False))


def halo_kernel(half, tiles, info_ref, outer_ref, halo_ref, coeff_ref, out_ref, sent_ref):
    add_halo(half, tiles, tiles, info_ref, outer_ref, halo_ref, coeff_ref, out_ref, sent_ref)


def halo_step(half, info, outer, halo, coeffs):
    tiles, _, width = outer.shape
    vmem = pl.BlockSpec(memory_space=pltpu.VMEM)
    cells = tiles * 8 * width
    return pl.pallas_call(
        functools.partial(halo_kernel, half, tiles),
        in_specs=[pl.BlockSpec(memory_space=pltpu.SMEM)] + [vmem] * 3,
        out_specs=[vmem, vmem],
        out_shape=[shape_of(*outer.shape), shape_of(SENT, 8, width // 2)],
        compiler_params=params(),
        cost_estimate=cost(15 * cells, 20 * cells),
        name="halo" + ("_far" if half == FAR_HALF else "_near"),
    )(info, outer, halo, coeffs)


def pooled(field, rows_ref):
    rows, lanes = field.shape
    fine = lax.broadcasted_iota(jnp.int32, (256, 128), 0)
    coarse = lax.broadcasted_iota(jnp.int32, (256, 128), 1)
    pick = jnp.where((fine >> 1) == coarse, 0.25, 0.0).astype(jnp.bfloat16)
    few = []
    for chunk in range(lanes // 128):
        rows_ref[chunk, :rows] = field[:, 128 * chunk : 128 * chunk + 128]
        even = rows_ref[chunk, pl.ds(0, rows // 2, stride=2), :]
        few.append(even + rows_ref[chunk, pl.ds(1, rows // 2, stride=2), :])
    pairs = [jnp.concatenate(few[pos : pos + 2], axis=1) for pos in range(0, len(few), 2)]
    rest = jnp.concatenate(pairs, axis=0)
    total = None
    for _ in range(3):
        part = rest.astype(jnp.bfloat16)
        rest = rest - part.astype(jnp.float32)
        mean = jnp.dot(part, pick, preferred_element_type=jnp.float32)
        total = mean if total is None else total + mean
    count = rows // 2
    return jnp.concatenate([total[pos * count : (pos + 1) * count] for pos in range(len(pairs))], axis=1)


def finish_kernel(half, tiles, info_ref, outer_ref, inner_ref, gate_ref, halo_ref, coeff_ref, tension_ref, *refs):
    if half == FAR_HALF:
        states_out, tension_out, active_out, u_ref, layer_ref, rows_ref, sems = refs
    else:
        active_ref, _, _, states_out, tension_out, active_out, facing_out, u_ref, layer_ref, rows_ref, sems = refs
    index, outer = half_place(info_ref, half)
    place = [2 * index + outer, 2 * index + 1 - outer]
    moves = [(gate_ref.at[g, plane], states_out.at[1 + g, place[plane]]) for g in range(3) for plane in range(2)]
    moves.append((inner_ref, states_out.at[0, place[1]]))
    copies = [pltpu.make_async_copy(src, dst, sems.at[pos]) for pos, (src, dst) in enumerate(moves)]
    for copy in copies:
        copy.start()
    own = tiles - 1
    add_halo(half, tiles, own, info_ref, outer_ref, halo_ref, coeff_ref, u_ref)
    copies.append(pltpu.make_async_copy(u_ref, states_out.at[0, place[0]], sems.at[len(moves)]))
    copies[-1].start()
    both = 0.5 * (u_ref[...] + inner_ref[...])
    mean = pooled(both.reshape(own * 8, both.shape[-1]), rows_ref)
    old = tension_ref[index]
    new = old + 0.5 * (mean - old)
    layer_ref[...] = new
    copies.append(pltpu.make_async_copy(layer_ref, tension_out.at[index], sems.at[len(moves) + 1]))
    copies[-1].start()
    mean = pooled(0.5 * new, rows_ref)
    if half == FAR_HALF:
        active_out[...] = mean
    else:
        active_out[...] = active_ref[...] + mean
        facing_out[...] = active_out[pl.ds(pl.multiple_of(8 * (1 - info_ref[SIDE]), 8), 8), :]
    for copy in copies:
        copy.wait()


def finish_half(half, info, arrays, halo, coeffs, tension, active=None, states=None, tension_next=None):
    _, tiles, _, width = coeffs.shape
    own = tiles - 1
    active_shape = (own * 2, width // 4)
    vmem, hbm = pl.BlockSpec(memory_space=pltpu.VMEM), pl.BlockSpec(memory_space=pltpu.HBM)
    in_specs = [pl.BlockSpec(memory_space=pltpu.SMEM)] + [vmem] * 6
    operands = [*arrays, halo, coeffs, tension]
    out_specs = [hbm, hbm, vmem]
    out_shape = [
        jax.ShapeDtypeStruct((4, 4, own, 8, width), jnp.float32),
        jax.ShapeDtypeStruct(tension.shape, jnp.float32),
        jax.ShapeDtypeStruct(active_shape, jnp.float32),
    ]
    aliases = {}
    if half == NEAR_HALF:
        in_specs += [vmem, hbm, hbm]
        operands += [active, states, tension_next]
        aliases = {8: 0, 9: 1}
        out_specs.append(vmem)
        out_shape.append(jax.ShapeDtypeStruct((8, width // 4), jnp.float32))
    cells = 2 * own * 8 * width
    return pl.pallas_call(
        functools.partial(finish_kernel, half, tiles),
        in_specs=in_specs,
        out_specs=out_specs,
        out_shape=out_shape,
        scratch_shapes=[
            pltpu.VMEM((own, 8, width), jnp.float32),
            pltpu.VMEM(tension.shape[1:], jnp.float32),
            pltpu.VMEM((width // 128, own * 8, 128), jnp.float32),
            pltpu.SemaphoreType.DMA((9,)),
        ],
        input_output_aliases=aliases,
        compiler_params=params(),
        cost_estimate=cost(20 * cells, 20 * cells),
        name="finish" + ("_far" if half == FAR_HALF else "_near"),
    )(info, *operands)


REACH = 4
ROWS = 24


class Weights:
    def __init__(self, side, own, width):
        row = lax.broadcasted_iota(jnp.int32, (ROWS, width), 0)
        lane = lax.broadcasted_iota(jnp.int32, (ROWS, width), 1)
        self.next_y = jnp.where((row == own - 1) & (side == 1), 0.0, 1.0)
        self.prev_y = jnp.where((row == 0) & (side == 0), 0.0, 1.0)
        self.next_x = jnp.where(lane == width - 1, 0.0, 1.0)
        self.prev_x = jnp.where(lane == 0, 0.0, 1.0)


def up_y(val):
    return pltpu.roll(val, ROWS - 1, 0)


def down_y(val):
    return pltpu.roll(val, 1, 0)


def slope_z(below, mid, above):
    return 0.5 * (above - below)


def smooth_z(below, mid, above):
    return 0.75 * mid + 0.125 * (above + below)


def gradients(below, mid, above, k):
    slope = slope_z(below, mid, above)
    smooth = smooth_z(below, mid, above)
    slope_s = 0.75 * slope + 0.125 * (up_y(slope) * k.next_y + down_y(slope) * k.prev_y)
    ahead = up_y(smooth) * k.next_y
    behind = down_y(smooth) * k.prev_y
    smooth_s = 0.75 * smooth + 0.125 * (ahead + behind)
    smooth_d = 0.5 * (ahead - behind)

    def smooth_x(val):
        return 0.75 * val + 0.125 * (left(val) * k.next_x + right(val) * k.prev_x)

    return (
        smooth_x(slope_s),
        smooth_x(smooth_d),
        0.5 * (left(smooth_s) * k.next_x - right(smooth_s) * k.prev_x),
    )


def force(below, mid, above, k):
    p_z = slope_z(below[0], mid[0], above[0])
    p_y = smooth_z(below[1], mid[1], above[1])
    p_x = smooth_z(below[2], mid[2], above[2])
    small, half = 0.125 * p_z, 0.5 * p_y
    both = 0.75 * p_z + up_y(small + half) * k.next_y + down_y(small - half) * k.prev_y
    p_x = 0.75 * p_x + 0.125 * (up_y(p_x) * k.next_y + down_y(p_x) * k.prev_y)
    small, half = 0.125 * both, 0.5 * p_x
    return 0.75 * both + left(small + half) * k.next_x + right(small - half) * k.prev_x


def deformation(below, mid, above, k):
    deform = []
    for comp in range(3):
        row = list(gradients(below[comp], mid[comp], above[comp], k))
        row[comp] = row[comp] + 1.0
        deform.append(row)
    return deform


def passive_stress(deform):
    right_c = {}
    for a_pos, b_pos in PAIRS:
        right_c[a_pos, b_pos] = sum(deform[i_pos][a_pos] * deform[i_pos][b_pos] for i_pos in range(3))
    strain = {}
    for a_pos, b_pos in PAIRS:
        strain[a_pos, b_pos] = 0.5 * (right_c[a_pos, b_pos] - (1.0 if a_pos == b_pos else 0.0))
    trace = strain[0, 0] + strain[1, 1] + strain[2, 2]
    second = {}
    for a_pos, b_pos in PAIRS:
        entry = (2.0 * SHEAR) * strain[a_pos, b_pos]
        if a_pos == b_pos:
            entry = entry + LAME_FIRST * trace
        second[a_pos, b_pos] = entry
        second[b_pos, a_pos] = entry
    return second


def times(deform, second):
    return [
        [sum(deform[i_pos][b_pos] * second[b_pos, a_pos] for b_pos in range(3)) for a_pos in range(3)]
        for i_pos in range(3)
    ]


def metric(deform, fdir):
    def cofactor(i_pos, j_pos):
        i_next, i_last = (i_pos + 1) % 3, (i_pos + 2) % 3
        j_next, j_last = (j_pos + 1) % 3, (j_pos + 2) % 3
        return deform[i_next][j_next] * deform[i_last][j_last] - deform[i_next][j_last] * deform[i_last][j_next]

    cof = [[cofactor(i_pos, j_pos) for j_pos in range(3)] for i_pos in range(3)]
    det = deform[0][0] * cof[0][0] + deform[0][1] * cof[0][1] + deform[0][2] * cof[0][2]
    scale = 1.0 / det
    inv = [[cof[i_pos][j_pos] * scale for i_pos in range(3)] for j_pos in range(3)]
    along = [sum(inv[a_pos][i_pos] * fdir[i_pos] for i_pos in range(3)) for a_pos in range(3)]
    comps = []
    for a_pos, b_pos in PAIRS:
        inner = sum(inv[a_pos][i_pos] * inv[b_pos][i_pos] for i_pos in range(3))
        comps.append(SIGMA_TRANS * inner + (SIGMA_LONG - SIGMA_TRANS) * along[a_pos] * along[b_pos])
    return comps


def inside(slab, slabs, offset):
    spot = slab + offset
    return jnp.where((spot >= 0) & (spot < slabs), 1.0, 0.0)


class Planes:
    def __init__(self, field, slabs, reach, from_pair=None):
        self.slabs, self.reach = slabs, reach
        self.parts = [field[None]]
        self.doubling = slabs in (2, 4, 8)
        self.step = 1
        if self.doubling and from_pair is not None:
            self.parts.append(from_pair[None])
            self.step = 2

    def round(self):
        if self.doubling:
            if self.step < self.slabs:
                held = jnp.concatenate(self.parts, axis=0) if len(self.parts) > 1 else self.parts[0]
                perm = [(i, i ^ self.step) for i in range(self.slabs)]
                self.parts.append(lax.ppermute(held, "slab", perm))
                self.step *= 2
        elif self.step == 1:
            for shift in self.shifts()[1:]:
                perm = [((i + shift) % self.slabs, i) for i in range(self.slabs)]
                self.parts.append(lax.ppermute(self.parts[0], "slab", perm))
            self.step = 0

    def shifts(self):
        return sorted({offset % self.slabs for offset in range(-self.reach, self.reach + 1)})

    def spot(self, slab, offset):
        if self.doubling:
            return slab ^ jnp.clip(slab + offset, 0, self.slabs - 1)
        return self.shifts().index(offset % self.slabs)


def fiber_table():
    index = jnp.arange(128, dtype=jnp.float32)
    theta = -1.0 + 2.0 * index / (NFIB - 1)
    tilt = 0.3 * jnp.sin(3.0 * index)
    return jnp.stack([jnp.sin(tilt), jnp.cos(tilt) * jnp.sin(theta), jnp.cos(tilt) * jnp.cos(theta)])


def facing_fields_kernel(info_ref, *refs):
    out_ref = refs[-1]
    upper_side = info_ref[SIDE] == 0
    at = 0
    for ref in refs[:-1]:
        for pos in range(ref.shape[0]):
            for comp in range(ref.shape[1]):
                both = ref[pos, comp]
                half = both.shape[-1] // 2
                out_ref[at, comp] = jnp.where(upper_side, both[:, half:], both[:, :half])
            at += 1


def facing_rows(info, fields):
    _, comps, _, width = fields[0].shape
    count = sum(field.shape[0] for field in fields)
    vmem = pl.BlockSpec(memory_space=pltpu.VMEM)
    return pl.pallas_call(
        facing_fields_kernel,
        in_specs=[pl.BlockSpec(memory_space=pltpu.SMEM)] + [vmem] * len(fields),
        out_shape=shape_of(count, comps, 8, width // 2),
        compiler_params=params(),
        cost_estimate=cost(0, 600_000),
        name="facing",
    )(info, *fields)


def passive_kernel(planes, info_ref, table_ref, strip_ref, *refs):
    own_refs, (disp_out, stress_out, pull_out, disp_all, field) = refs[:-5], refs[-5:]
    slab, slabs = info_ref[SLAB], planes.slabs
    width = strip_ref.shape[-1]
    own = ROWS - 8
    k = Weights(info_ref[SIDE], own, width)
    reach = REACH + 1

    at = 0
    for ref in own_refs:
        for pos in range(ref.shape[0]):
            for comp in range(ref.shape[1]):
                both = ref[pos, comp]
                field[at, comp] = jnp.concatenate([both[:, :width], both[:, width:], strip_ref[at, comp]], axis=0)
            at += 1

    def plane(comp, offset):
        return field[planes.spot(slab, offset), comp]

    for offset in range(-reach, reach + 1):
        factor = inside(slab, slabs, offset)
        for comp in range(3):
            disp_all[comp, offset + reach] = plane(comp, offset) * factor

    tables = [jnp.broadcast_to(table_ref[comp : comp + 1], (8, 128)) for comp in range(3)]

    def direction(index, comp):
        index = index.astype(jnp.int32)
        rows = []
        for top in range(0, ROWS, 8):
            parts = [
                jnp.take_along_axis(tables[comp], index[top : top + 8, at : at + 128], axis=1, mode="promise_in_bounds")
                for at in range(0, width, 128)
            ]
            rows.append(jnp.concatenate(parts, axis=1))
        return jnp.concatenate(rows, axis=0)

    for step in range(2 * REACH + 1):
        offset = step - REACH
        below, mid, above = ([disp_all[comp, step + shift] for comp in range(3)] for shift in range(3))
        factor = inside(slab, slabs, offset)
        deform = deformation(below, mid, above, k)
        stress = times(deform, passive_stress(deform))
        index = plane(3, offset)
        fdir = [direction(index, comp) for comp in range(3)]
        for i_pos in range(3):
            pull = (ACTIVE_GAIN * factor) * sum(deform[i_pos][b_pos] * fdir[b_pos] for b_pos in range(3))
            for a_pos in range(3):
                stress_out[3 * i_pos + a_pos, step] = stress[i_pos][a_pos] * factor
                pull_out[3 * i_pos + a_pos, step] = pull * fdir[a_pos]
            disp_out[i_pos, step] = mid[i_pos]
            disp_out[3 + i_pos, step] = fdir[i_pos]


def passive_step(info, planes, strips):
    width = strips.shape[-1]
    count = 2 * REACH + 1
    shapes = [(6, count), (9, count), (9, count)]
    vmem = pl.BlockSpec(memory_space=pltpu.VMEM)
    return pl.pallas_call(
        functools.partial(passive_kernel, planes),
        in_specs=[pl.BlockSpec(memory_space=pltpu.SMEM)] + [vmem] * (2 + len(planes.parts)),
        out_shape=[jax.ShapeDtypeStruct((a, b, ROWS, width), jnp.float32) for a, b in shapes],
        scratch_shapes=[
            pltpu.VMEM((3, count + 2, ROWS, width), jnp.float32),
            pltpu.VMEM(strips.shape[:2] + (ROWS, width), jnp.float32),
        ],
        compiler_params=params(),
        cost_estimate=cost(400 * count * ROWS * width, 5_000_000),
        name="passive",
    )(info, fiber_table(), strips, *planes.parts)


def mechanics_kernel(planes, info_ref, disp_ref, stress_ref, pull_ref, *rest):
    active_refs, (disp_out, cond_out, d_one, p_two, active) = rest[:-5], rest[-5:]
    slab, side, slabs = info_ref[SLAB], info_ref[SIDE], planes.slabs
    own, width = disp_out.shape[-2:]
    k = Weights(side, own, width)

    at = 0
    for ref in active_refs:
        active[at : at + ref.shape[0]] = ref[...]
        at += ref.shape[0]

    def active_at(step):
        return active[planes.spot(slab, step - REACH)]

    for step in range(1, 2 * REACH):
        act = [active_at(step + shift) for shift in (-1, 0, 1)]
        factor = inside(slab, slabs, step - REACH)
        for i_pos in range(3):
            stress = [
                [stress_ref[3 * i_pos + a_pos, step + shift] + act[shift + 1] * pull_ref[3 * i_pos + a_pos, step + shift] for a_pos in range(3)]
                for shift in (-1, 0, 1)
            ]
            moved = disp_ref[i_pos, step] + MECH_RATE * force(stress[0], stress[1], stress[2], k)
            d_one[i_pos, step] = moved * factor

    for step in range(2, 2 * REACH - 1):
        disp = [[d_one[comp, step + shift] for comp in range(3)] for shift in (-1, 0, 1)]
        deform = deformation(disp[0], disp[1], disp[2], k)
        second = passive_stress(deform)
        fdir = [disp_ref[3 + comp, step] for comp in range(3)]
        gain = ACTIVE_GAIN * active_at(step)
        for a_pos, b_pos in PAIRS:
            entry = second[a_pos, b_pos] + gain * fdir[a_pos] * fdir[b_pos]
            second[a_pos, b_pos] = entry
            second[b_pos, a_pos] = entry
        stress = times(deform, second)
        factor = inside(slab, slabs, step - REACH)
        for i_pos in range(3):
            for a_pos in range(3):
                p_two[3 * i_pos + a_pos, step] = stress[i_pos][a_pos] * factor

    last = []
    for step in (REACH - 1, REACH, REACH + 1):
        factor = inside(slab, slabs, step - REACH)
        row = []
        for i_pos in range(3):
            stress = [[p_two[3 * i_pos + a_pos, step + shift] for a_pos in range(3)] for shift in (-1, 0, 1)]
            moved = d_one[i_pos, step] + MECH_RATE * force(stress[0], stress[1], stress[2], k)
            row.append(moved * factor)
        last.append(row)
    deform = deformation(last[0], last[1], last[2], k)
    comps = metric(deform, [disp_ref[3 + comp, REACH] for comp in range(3)])
    for i_pos in range(3):
        disp_out[i_pos, 0] = last[1][i_pos][:own]
    for pos, comp in enumerate(comps):
        cond_out[pos, 0] = comp[:own]


def mechanics_step(info, own, planes, window):
    width = planes.parts[0].shape[-1]
    count = 2 * REACH + 1
    held = sum(part.shape[0] for part in planes.parts)
    vmem = pl.BlockSpec(memory_space=pltpu.VMEM)
    return pl.pallas_call(
        functools.partial(mechanics_kernel, planes),
        in_specs=[pl.BlockSpec(memory_space=pltpu.SMEM)] + [vmem] * (3 + len(planes.parts)),
        out_shape=[
            jax.ShapeDtypeStruct((3, 1, own, width), jnp.float32),
            jax.ShapeDtypeStruct((6, 1, own, width), jnp.float32),
        ],
        scratch_shapes=[
            pltpu.VMEM((3, count, ROWS, width), jnp.float32),
            pltpu.VMEM((9, count, ROWS, width), jnp.float32),
            pltpu.VMEM((held, ROWS, width), jnp.float32),
        ],
        compiler_params=params(),
        cost_estimate=cost(400 * count * ROWS * width, 5_000_000),
        name="mechanics",
    )(info, *window, *planes.parts)


def tie(*arrays):
    return lax.optimization_barrier(arrays)


def on_device(states, cond, tension, fiber, disp):
    slabs = lax.axis_size("slab")
    slab, col = lax.axis_index("slab"), lax.axis_index("col")
    _, planes, rows, width = states.shape
    own = rows // 8
    flip = slab % 2
    far_exists = (slab > 0) & (slab < slabs - 1)
    info = jnp.stack([slab, col, flip, far_exists]).astype(jnp.int32)

    pairs = [(i, i ^ 1) for i in range(slabs)]
    others = [(i, i if i in (0, slabs - 1) else ((i + 1) ^ 1) - 1) for i in range(slabs)]
    swap = [(0, 1), (1, 0)]

    tiled = states.reshape(4, planes, own, 8, width)
    edges, facing, cond_rows = facing_parts(info, tiled, cond)
    edges = lax.ppermute(edges, "col", swap)
    cond_strip = lax.ppermute(cond_rows, "col", swap)
    strip = lax.ppermute(facing, "col", swap)
    far, near = first_sends(info, edges, tiled, disp, fiber)
    far_halo = lax.ppermute(far, "slab", others)
    near_halo = lax.ppermute(near, "slab", pairs)
    fields = Planes(near[SENT:], slabs, REACH + 1, near_halo[SENT:])

    coeffs = fine_coeffs(info, cond, cond_strip)
    whole = jnp.concatenate([tiled, strip[:, :, None]], axis=2)

    far_part, far_inner, far_gates = half_step("first", FAR_HALF, info, (whole,), coeffs)
    near_part, near_inner, near_gates = half_step("first", NEAR_HALF, info, (whole,), coeffs)
    for turn_index in range(1, SUB):
        last = turn_index == SUB - 1
        far, far_send = halo_step(FAR_HALF, info, far_part, far_halo, coeffs)
        far_halo = lax.ppermute(far_send, "slab", others)
        far_arrays = (far, far_inner, near_inner, far_gates)
        kind = "last" if last else "middle"
        far_part, far_next, far_gates = half_step(kind, FAR_HALF, info, far_arrays, coeffs)
        near, near_send = halo_step(NEAR_HALF, info, near_part, near_halo, coeffs)
        near_halo = lax.ppermute(near_send, "slab", pairs)
        if not last:
            near, *fields.parts = tie(near, *fields.parts)
            fields.round()
        near_arrays = (near, near_inner, far_inner, near_gates)
        near_part, near_inner, near_gates = half_step(kind, NEAR_HALF, info, near_arrays, coeffs)
        far_inner = far_next
    strips = lax.ppermute(facing_rows(info, fields.parts), "col", swap)
    far_arrays = (far_part, far_inner, far_gates)
    near_arrays = (near_part, near_inner, near_gates)
    states_next, tension_next, active = finish_half(FAR_HALF, info, far_arrays, far_halo, coeffs, tension)
    window = passive_step(info, fields, strips)
    states_next, tension_next, active, facing = finish_half(
        NEAR_HALF, info, near_arrays, near_halo, coeffs, tension, active, states_next, tension_next
    )
    active_strip = lax.ppermute(facing, "col", swap)
    actives = Planes(jnp.concatenate([active, active_strip], axis=0), slabs, REACH)
    for _ in range(3):
        actives.round()
    disp_next, cond_next = mechanics_step(info, disp.shape[2], actives, window)
    return (states_next.reshape(states.shape), tension_next, disp_next, cond_next)


def solution(mesh):
    in_specs = (
        P(None, ("grp", "slab"), "col", None),
        P(None, ("grp", "slab"), "col", None),
        P(("grp", "slab"), "col", None),
        P(("grp", "slab"), "col", None),
        P(None, ("grp", "slab"), "col", None),
    )
    out_specs = (
        P(None, ("grp", "slab"), "col", None),
        P(("grp", "slab"), "col", None),
        P(None, ("grp", "slab"), "col", None),
        P(None, ("grp", "slab"), "col", None),
    )
    return jax.shard_map(
        on_device, mesh=mesh, in_specs=in_specs, out_specs=out_specs, check_vma=False
    )
```

```python
import functools

import jax
import jax.numpy as jnp
from jax import lax
from jax.experimental import pallas as pl
from jax.experimental.pallas import tpu as pltpu
from jax.sharding import PartitionSpec as P

SUB = 4
MECH_STEPS = 2
NFIB = 64

STEP_TIME = 0.05
LAME_FIRST = 1.0
SHEAR = 0.5
ACTIVE_GAIN = 0.5
MECH_RATE = 0.15
SIGMA_LONG = 0.16
SIGMA_TRANS = 0.04
PAIRS = ((0, 0), (1, 1), (2, 2), (0, 1), (0, 2), (1, 2))

C_ZZ, C_ZY, C_ZXR, C_ZXL, C_MID, C_YY, C_XXR, C_YXR, C_XXL, C_YXL = range(10)

SLAB, SIDE, FLIP, FAR = range(4)

HIGHEST = lax.Precision.HIGHEST
LIMIT = 40 * 1024 * 1024


def params(**kwargs):
    return pltpu.CompilerParams(vmem_limit_bytes=LIMIT, **kwargs)


def cost(flops, nbytes, trans=0):
    return pl.CostEstimate(flops=flops, bytes_accessed=nbytes, transcendentals=trans)


def row_iota():
    return lax.broadcasted_iota(jnp.int32, (8, 1024), 0)


def next_row(cur, nxt, sub):
    return pltpu.roll(jnp.where(sub == 0, nxt, cur), 7, 0)


def prev_row(cur, prv, sub):
    return pltpu.roll(jnp.where(sub == 7, prv, cur), 1, 0)


def left(val):
    return pltpu.roll(val, val.shape[-1] - 1, val.ndim - 1)


def right(val):
    return pltpu.roll(val, 1, val.ndim - 1)


def edge_masks(tile, side, own):
    before = jnp.where((tile == 0) & (side == 0), 0.0, 1.0)
    after = jnp.where((tile == own - 1) & (side == 1), 0.0, 1.0)
    return before, after


def ring_neighbours(tile, tiles):
    before = jnp.where(tile == 0, tiles - 1, tile - 1)
    after = jnp.where(tile == tiles - 1, 0, tile + 1)
    return before, after


def coeff_kernel(info_ref, cond_ref, strip_ref, out_ref):
    rows, width = cond_ref.shape[-2:]
    turn = jnp.where(info_ref[FLIP] == 1, -0.5, 0.5)
    upper_side = info_ref[SIDE] == 0
    fine = 4 * width
    mech = lax.broadcasted_iota(jnp.int32, (width, fine), 0)
    cell = lax.broadcasted_iota(jnp.int32, (width, fine), 1)
    own = rows // 2
    block = rows + 8
    sub = lax.broadcasted_iota(jnp.int32, (8, fine), 0)

    def spread(comps, shift):
        pick = jnp.where(mech == ((cell + shift) >> 2), 1.0, 0.0)
        flat = jnp.concatenate([part for comp in comps for part in (cond_ref[comp, 0], strip_ref[comp])], axis=0)
        wide = jnp.dot(flat, pick, precision=HIGHEST, preferred_element_type=jnp.float32)
        return [wide[pos * block : (pos + 1) * block] for pos in range(len(comps))]

    def both(first, second):
        return jnp.where(sub < 4, jnp.broadcast_to(first, (8, fine)), jnp.broadcast_to(second, (8, fine)))

    def store(index, wide):
        for tile in range(own):
            out_ref[index, tile] = both(wide[2 * tile : 2 * tile + 1], wide[2 * tile + 1 : 2 * tile + 2])
        head = both(wide[rows : rows + 1], wide[rows + 1 : rows + 2])
        tail = both(wide[block - 2 : block - 1], wide[block - 1 : block])
        out_ref[index, own] = jnp.where(upper_side, head, tail)

    zz, yy, xx, zy = spread((0, 1, 2, 3), 0)
    store(C_ZZ, zz)
    store(C_YY, yy)
    store(C_MID, 1.0 - 2.0 * (zz + yy + xx))
    store(C_ZY, turn * zy)
    xx, zx, yx = spread((2, 4, 5), -1)
    store(C_XXR, xx)
    store(C_ZXR, turn * zx)
    store(C_YXR, 0.5 * yx)
    xx, zx, yx = spread((2, 4, 5), 1)
    store(C_XXL, xx)
    store(C_ZXL, turn * zx)
    store(C_YXL, 0.5 * yx)


def fine_coeffs(info, cond, strip):
    rows, width = cond.shape[-2:]
    vmem = pl.BlockSpec(memory_space=pltpu.VMEM)
    return pl.pallas_call(
        coeff_kernel,
        in_specs=[pl.BlockSpec(memory_space=pltpu.SMEM), vmem, vmem],
        out_shape=jax.ShapeDtypeStruct((10, rows // 2 + 1, 8, 4 * width), jnp.float32),
        compiler_params=params(),
        cost_estimate=cost(2_000_000, 3_200_000),
        name="coeffs",
    )(info, cond, strip)


SENT, FIELD = 17, 4


def packed_strip(strip, side):
    half = strip.shape[-1] // 2
    low, high = strip[:, :half], strip[:, half:]
    sub = lax.broadcasted_iota(jnp.int32, low.shape, 0)
    first = jnp.where(side == 0, low, pltpu.roll(low, 4, 0))
    second = jnp.where(side == 0, pltpu.roll(high, 4, 0), high)
    return jnp.where(sub < 4, first, second)


def store_sent(ref, tile, tiles, value, side):
    half = value.shape[-1] // 2
    if tile < tiles - 1:
        ref[tile] = value[:, :half]
        ref[tiles - 1 + tile] = value[:, half:]
    else:
        ref[2 * tile] = packed_strip(value, side)


def load_sent(ref, tile, tiles, side):
    if tile < tiles - 1:
        return jnp.concatenate([ref[tile], ref[tiles - 1 + tile]], axis=1)
    packed = ref[2 * tile]
    turned = pltpu.roll(packed, 4, 0)
    return jnp.concatenate([jnp.where(side == 0, packed, turned), jnp.where(side == 0, turned, packed)], axis=1)


SMEM = pl.BlockSpec(memory_space=pltpu.SMEM)
VMEM = pl.BlockSpec(memory_space=pltpu.VMEM)


def shape_of(*shape):
    return jax.ShapeDtypeStruct(shape, jnp.float32)


def facing_kernel(info_ref, states_ref, cond_ref, edge_ref, facing_ref, cond_rows):
    flip, side = info_ref[FLIP], info_ref[SIDE]
    comps, planes, own = states_ref.shape[:3]
    edge = (1 - side) * (own - 1)
    edge_ref[0] = states_ref[0, flip * (planes - 1), edge]
    edge_ref[1] = states_ref[0, (1 - flip) * (planes - 1), edge]
    for comp in range(comps):
        for plane in range(planes):
            facing_ref[comp, plane] = states_ref[comp, plane, edge]
    first = pl.multiple_of(8 * (1 - side), 8)
    for comp in range(cond_ref.shape[0]):
        cond_rows[comp] = cond_ref[comp, 0, pl.ds(first, 8), :]


def field_kernel(disp_ref, fiber_ref, field_ref):
    for comp in range(3):
        field_ref[comp] = jnp.concatenate([disp_ref[comp, 0, :8], disp_ref[comp, 0, 8:]], axis=1)
    index = fiber_ref[0].astype(jnp.float32)
    field_ref[3] = jnp.concatenate([index[:8], index[8:]], axis=1)


def own_field(disp, fiber):
    return pl.pallas_call(
        field_kernel,
        in_specs=[VMEM] * 2,
        out_specs=VMEM,
        out_shape=shape_of(FIELD, 8, 2 * disp.shape[-1]),
        compiler_params=params(),
        cost_estimate=cost(0, 130_000),
        name="own_field",
    )(disp, fiber)


def sends_kernel(info_ref, edge_ref, states_ref, *refs):
    field_refs, (far_ref, near_ref) = refs[:-2], refs[-2:]
    flip, side = info_ref[FLIP], info_ref[SIDE]
    planes, own = states_ref.shape[1:3]
    for pos, (ref, plane) in enumerate([(far_ref, flip * (planes - 1)), (near_ref, (1 - flip) * (planes - 1))]):
        for tile in range(own):
            store_sent(ref, tile, own + 1, states_ref[0, plane, tile], side)
        store_sent(ref, own, own + 1, edge_ref[pos], side)
    for pos, ref in enumerate(field_refs):
        near_ref[SENT + FIELD * pos : SENT + FIELD * (pos + 1)] = ref[0]


def facing_parts(info, tiled, cond):
    comps, planes, _, _, width = tiled.shape
    return pl.pallas_call(
        facing_kernel,
        in_specs=[SMEM, VMEM, VMEM],
        out_specs=[VMEM] * 3,
        out_shape=[
            shape_of(2, 8, width),
            shape_of(comps, planes, 8, width),
            shape_of(cond.shape[0], 8, cond.shape[-1]),
        ],
        compiler_params=params(),
        cost_estimate=cost(0, 1_200_000),
        name="facing_parts",
    )(info, tiled, cond)


def first_sends(info, edges, tiled, fields):
    width = tiled.shape[-1]
    return pl.pallas_call(
        sends_kernel,
        in_specs=[SMEM] + [VMEM] * (2 + len(fields)),
        out_specs=[VMEM] * 2,
        out_shape=[shape_of(SENT, 8, width // 2), shape_of(SENT + FIELD * len(fields), 8, width // 2)],
        compiler_params=params(),
        cost_estimate=cost(0, 1_200_000),
        name="sends",
    )(info, edges, tiled, *fields)


def fraction(val):
    return pl.reciprocal(val, approx=True)


def ionic(u, v, w, s):
    dt = STEP_TIME
    steep = 50.0 * u
    t_v = jnp.tanh(steep - 15.0)
    t_w = jnp.tanh(steep - 6.5)
    t_o = jnp.tanh(steep - 0.3)
    t_m = jnp.tanh(65.0 * u - 65.0 * 0.03)
    t_f = jnp.tanh(2.0458 * u - 2.0458 * 0.65)
    t_s = jnp.tanh(2.0994 * u - 2.0994 * 0.9087)
    hv, nv = 1.0 + t_v, 1.0 - t_v
    hw, nw = 1.0 + t_w, 1.0 - t_w
    no = 0.5 - 0.5 * t_o
    half_so = 0.5 * (30.0181 - 0.9957)
    r_vm = fraction(2.0 / dt * 605.0 + (2.0 / dt * 545.0) * t_o)
    r_wm = fraction(2.0 / dt * 37.5 - (2.0 / dt * 22.5) * t_m)
    r_so = fraction(2.0 / dt * (30.0181 - half_so) - (2.0 / dt * half_so) * t_f)
    r_s = fraction(9.3671 / dt + (6.6329 / dt) * t_w)
    r_o = fraction(2.0 / dt * 203.0 - (2.0 / dt * 197.0) * t_o)
    w_inf = 0.94 + no * (0.06 - u * (1.0 / 0.07))
    hvv = hv * v
    hww = hw * w
    fast = hvv * ((u - 0.3) * (0.5 * dt / 0.11 * 1.55 - (0.5 * dt / 0.11) * u))
    out = (u * nw) * r_o + hw * r_so
    slow = hww * (s * (0.5 * dt / 1.8875))
    v_new = v + (nv * (no - v)) * r_vm - hvv * (0.5 * dt / 1.4506)
    w_new = w + (nw * (w_inf - w)) * r_wm - hww * (0.5 * dt / 200.0)
    s_new = s + ((0.5 + 0.5 * t_s) - s) * r_s
    return fast + slow - out, v_new, w_new, s_new


FAR_HALF, NEAR_HALF = -1, 1


def half_place(info_ref, half):
    flip = info_ref[FLIP]
    return (flip, flip) if half == FAR_HALF else (1 - flip, 1 - flip)


def half_kernel(kind, half, tiles, info_ref, *refs):
    side = info_ref[SIDE]
    sub = row_iota()
    own = tiles - 1
    index, outer = half_place(info_ref, half)
    if kind == "first":
        whole_ref, coeff_ref, outer_out, inner_out, gate_out = refs
        spots = [2 * index + outer, 2 * index + 1 - outer, 2 - index]
        reads = [lambda t, z=z: whole_ref[0, z, t] for z in spots]
    else:
        *u_refs, gate_ref, coeff_ref, outer_out, inner_out, gate_out = refs
        reads = [lambda t, ref=ref: ref[t] for ref in u_refs]

    def diffused(tile):
        before, after = ring_neighbours(tile, tiles)
        mask_before, mask_after = edge_masks(tile, side, own)
        cur = [read(tile) for read in reads]
        prv = [read(before) * mask_before for read in reads]
        nxt = [read(after) * mask_after for read in reads]

        def coeff(index):
            return coeff_ref[index, tile]

        bases = []
        for plane in range(2):
            u = cur[plane]
            if plane == 0:
                around = cur[1]
                wide, wide_nxt, wide_prv = cur[1], nxt[1], prv[1]
            else:
                around = cur[0] + cur[2]
                wide, wide_nxt, wide_prv = cur[2] - cur[0], nxt[2] - nxt[0], prv[2] - prv[0]
            u_next = next_row(u, nxt[plane], sub)
            u_prev = prev_row(u, prv[plane], sub)
            tilt = coeff(C_ZY) * (next_row(wide, wide_nxt, sub) - prev_row(wide, wide_prv, sub))
            tall = u_next - u_prev
            to_left = coeff(C_XXR) * u + coeff(C_YXR) * tall
            to_right = coeff(C_XXL) * u - coeff(C_YXL) * tall
            if half == FAR_HALF:
                to_left += coeff(C_ZXR) * wide
                to_right -= coeff(C_ZXL) * wide
            else:
                to_left -= coeff(C_ZXR) * wide
                to_right += coeff(C_ZXL) * wide
            base = coeff(C_MID) * u + coeff(C_ZZ) * around + coeff(C_YY) * (u_next + u_prev)
            base = base + tilt if half == FAR_HALF else base - tilt
            bases.append(base + left(to_left) + right(to_right))
        return bases

    def react(tile, bases):
        chunk = 256
        for plane in range(2):
            for start in range(0, 1024, chunk):
                lanes = slice(start, start + chunk)
                if kind == "first":
                    u = whole_ref[0, spots[plane], tile, :, lanes]
                    gates = [whole_ref[1 + g, spots[plane], tile, :, lanes] for g in range(3)]
                else:
                    u = u_refs[plane][tile, :, lanes]
                    gates = [gate_ref[g, plane, tile, :, lanes] for g in range(3)]
                u_add, *gates = ionic(u, *gates)
                (outer_out, inner_out)[plane][tile, :, lanes] = bases[plane][:, lanes] + u_add
                for comp, value in enumerate(gates):
                    gate_out[comp, plane, tile, :, lanes] = value

    together = 2 if kind == "last" else 3

    def some(step, carry):
        numbers = [step * together + pos for pos in range(together)]
        held = [diffused(tile) for tile in numbers]
        for tile, bases in zip(numbers, held):
            react(tile, bases)
        return carry

    lax.fori_loop(0, (own if kind == "last" else tiles) // together, some, 0)


def half_step(kind, half, info, arrays, coeffs):
    _, tiles, _, width = coeffs.shape
    vmem = pl.BlockSpec(memory_space=pltpu.VMEM)
    kept = tiles - 1 if kind == "last" else tiles
    plane = jax.ShapeDtypeStruct((kept, 8, width), jnp.float32)
    cells = 2 * tiles * 8 * width
    return pl.pallas_call(
        functools.partial(half_kernel, kind, half, tiles),
        in_specs=[pl.BlockSpec(memory_space=pltpu.SMEM)] + [vmem] * (len(arrays) + 1),
        out_specs=[vmem] * 3,
        out_shape=[plane, plane, jax.ShapeDtypeStruct((3, 2, kept, 8, width), jnp.float32)],
        compiler_params=params(),
        cost_estimate=cost(100 * cells, 40 * cells, 11 * cells),
        name=kind + ("_far" if half == FAR_HALF else "_near"),
    )(info, *arrays, coeffs)


def halo_terms(halo_ref, coeff_ref, tile, tiles, side, sub, half):
    before, after = (tile - 1) % tiles, (tile + 1) % tiles
    cur, prv, nxt = (load_sent(halo_ref, at, tiles, side) for at in (tile, before, after))
    if tile == 0:
        prv = prv * jnp.where(side == 0, 0.0, 1.0)
    if tile == tiles - 2:
        nxt = nxt * jnp.where(side == 1, 0.0, 1.0)
    cross = coeff_ref[C_ZY, tile] * (next_row(cur, nxt, sub) - prev_row(cur, prv, sub))
    cross += left(coeff_ref[C_ZXR, tile] * cur) - right(coeff_ref[C_ZXL, tile] * cur)
    total = coeff_ref[C_ZZ, tile] * cur
    return total - cross if half == FAR_HALF else total + cross


def add_halo(half, tiles, kept, info_ref, outer_ref, halo_ref, coeff_ref, out_ref, sent_ref=None):
    side = info_ref[SIDE]
    sub = row_iota()

    def fill(beyond=True):
        for tile in range(kept):
            value = outer_ref[tile]
            if beyond:
                value += halo_terms(halo_ref, coeff_ref, tile, tiles, side, sub, half)
            out_ref[tile] = value
            if sent_ref is not None:
                store_sent(sent_ref, tile, tiles, value, side)

    if half == NEAR_HALF:
        fill()
    else:
        exists = info_ref[FAR] == 1
        pl.when(exists)(fill)
        pl.when(jnp.logical_not(exists))(functools.partial(fill, False))


def halo_kernel(half, tiles, info_ref, outer_ref, halo_ref, coeff_ref, out_ref, sent_ref):
    add_halo(half, tiles, tiles, info_ref, outer_ref, halo_ref, coeff_ref, out_ref, sent_ref)


def halo_step(half, info, outer, halo, coeffs):
    tiles, _, width = outer.shape
    vmem = pl.BlockSpec(memory_space=pltpu.VMEM)
    cells = tiles * 8 * width
    return pl.pallas_call(
        functools.partial(halo_kernel, half, tiles),
        in_specs=[pl.BlockSpec(memory_space=pltpu.SMEM)] + [vmem] * 3,
        out_specs=[vmem, vmem],
        out_shape=[shape_of(*outer.shape), shape_of(SENT, 8, width // 2)],
        compiler_params=params(),
        cost_estimate=cost(15 * cells, 20 * cells),
        name="halo" + ("_far" if half == FAR_HALF else "_near"),
    )(info, outer, halo, coeffs)


def pooled(field, rows_ref):
    rows, lanes = field.shape
    fine = lax.broadcasted_iota(jnp.int32, (256, 128), 0)
    coarse = lax.broadcasted_iota(jnp.int32, (256, 128), 1)
    pick = jnp.where((fine >> 1) == coarse, 0.25, 0.0).astype(jnp.bfloat16)
    few = []
    for chunk in range(lanes // 128):
        rows_ref[chunk, :rows] = field[:, 128 * chunk : 128 * chunk + 128]
        even = rows_ref[chunk, pl.ds(0, rows // 2, stride=2), :]
        few.append(even + rows_ref[chunk, pl.ds(1, rows // 2, stride=2), :])
    pairs = [jnp.concatenate(few[pos : pos + 2], axis=1) for pos in range(0, len(few), 2)]
    rest = jnp.concatenate(pairs, axis=0)
    total = None
    for _ in range(3):
        part = rest.astype(jnp.bfloat16)
        rest = rest - part.astype(jnp.float32)
        mean = jnp.dot(part, pick, preferred_element_type=jnp.float32)
        total = mean if total is None else total + mean
    count = rows // 2
    return jnp.concatenate([total[pos * count : (pos + 1) * count] for pos in range(len(pairs))], axis=1)


def finish_kernel(half, tiles, info_ref, outer_ref, inner_ref, halo_ref, coeff_ref, tension_ref, *refs):
    if half == FAR_HALF:
        gate_ref, near_inner_ref, near_gate_ref, *refs = refs
        states_out, tension_out, active_out, u_ref, layer_ref, rows_ref, sems = refs
        moves = []
        for which, inners, gates in ((FAR_HALF, inner_ref, gate_ref), (NEAR_HALF, near_inner_ref, near_gate_ref)):
            index, outer = half_place(info_ref, which)
            place = [2 * index + outer, 2 * index + 1 - outer]
            moves += [(gates.at[g, plane], states_out.at[1 + g, place[plane]]) for g in range(3) for plane in range(2)]
            moves.append((inners, states_out.at[0, place[1]]))
    else:
        active_ref, _, _, states_out, tension_out, active_out, facing_out, u_ref, layer_ref, rows_ref, sems = refs
        moves = []
    copies = []

    def start(src, dst):
        copies.append(pltpu.make_async_copy(src, dst, sems.at[len(copies)]))
        copies[-1].start()

    for src, dst in moves:
        start(src, dst)
    index, outer = half_place(info_ref, half)
    own = tiles - 1
    add_halo(half, tiles, own, info_ref, outer_ref, halo_ref, coeff_ref, u_ref)
    start(u_ref, states_out.at[0, 2 * index + outer])
    both = 0.5 * (u_ref[...] + inner_ref[...])
    mean = pooled(both.reshape(own * 8, both.shape[-1]), rows_ref)
    old = tension_ref[index]
    new = old + 0.5 * (mean - old)
    layer_ref[...] = new
    start(layer_ref, tension_out.at[index])
    mean = pooled(0.5 * new, rows_ref)
    if half == FAR_HALF:
        active_out[...] = mean
    else:
        active_out[...] = active_ref[...] + mean
        facing_out[...] = active_out[pl.ds(pl.multiple_of(8 * (1 - info_ref[SIDE]), 8), 8), :]
    for copy in copies:
        copy.wait()


def finish_half(half, info, outer, inner, halo, coeffs, tension, others):
    _, tiles, _, width = coeffs.shape
    own = tiles - 1
    active_shape = (own * 2, width // 4)
    hbm = pl.BlockSpec(memory_space=pltpu.HBM)
    out_specs = [hbm, hbm, VMEM]
    out_shape = [shape_of(4, 4, own, 8, width), shape_of(*tension.shape), shape_of(*active_shape)]
    aliases = {}
    if half == FAR_HALF:
        in_specs = [SMEM] + [VMEM] * 8
    else:
        in_specs = [SMEM] + [VMEM] * 6 + [hbm, hbm]
        aliases = {7: 0, 8: 1}
        out_specs.append(VMEM)
        out_shape.append(shape_of(8, width // 4))
    cells = 2 * own * 8 * width
    return pl.pallas_call(
        functools.partial(finish_kernel, half, tiles),
        in_specs=in_specs,
        out_specs=out_specs,
        out_shape=out_shape,
        scratch_shapes=[
            pltpu.VMEM((own, 8, width), jnp.float32),
            pltpu.VMEM(tension.shape[1:], jnp.float32),
            pltpu.VMEM((width // 128, own * 8, 128), jnp.float32),
            pltpu.SemaphoreType.DMA((16 if half == FAR_HALF else 2,)),
        ],
        input_output_aliases=aliases,
        compiler_params=params(),
        cost_estimate=cost(20 * cells, 20 * cells),
        name="finish" + ("_far" if half == FAR_HALF else "_near"),
    )(info, outer, inner, halo, coeffs, tension, *others)


REACH = 4
ROWS = 24


class Weights:
    def __init__(self, side, own, width):
        row = lax.broadcasted_iota(jnp.int32, (ROWS, width), 0)
        lane = lax.broadcasted_iota(jnp.int32, (ROWS, width), 1)
        self.next_y = jnp.where((row == own - 1) & (side == 1), 0.0, 1.0)
        self.prev_y = jnp.where((row == 0) & (side == 0), 0.0, 1.0)
        self.next_x = jnp.where(lane == width - 1, 0.0, 1.0)
        self.prev_x = jnp.where(lane == 0, 0.0, 1.0)


def up_y(val):
    return pltpu.roll(val, ROWS - 1, 0)


def down_y(val):
    return pltpu.roll(val, 1, 0)


def slope_z(below, mid, above):
    return 0.5 * (above - below)


def smooth_z(below, mid, above):
    return 0.75 * mid + 0.125 * (above + below)


def gradients(below, mid, above, k):
    slope = slope_z(below, mid, above)
    smooth = smooth_z(below, mid, above)
    slope_s = 0.75 * slope + 0.125 * (up_y(slope) * k.next_y + down_y(slope) * k.prev_y)
    ahead = up_y(smooth) * k.next_y
    behind = down_y(smooth) * k.prev_y
    smooth_s = 0.75 * smooth + 0.125 * (ahead + behind)
    smooth_d = 0.5 * (ahead - behind)

    def smooth_x(val):
        return 0.75 * val + 0.125 * (left(val) * k.next_x + right(val) * k.prev_x)

    return (
        smooth_x(slope_s),
        smooth_x(smooth_d),
        0.5 * (left(smooth_s) * k.next_x - right(smooth_s) * k.prev_x),
    )


def force(below, mid, above, k):
    p_z = slope_z(below[0], mid[0], above[0])
    p_y = smooth_z(below[1], mid[1], above[1])
    p_x = smooth_z(below[2], mid[2], above[2])
    small, half = 0.125 * p_z, 0.5 * p_y
    both = 0.75 * p_z + up_y(small + half) * k.next_y + down_y(small - half) * k.prev_y
    p_x = 0.75 * p_x + 0.125 * (up_y(p_x) * k.next_y + down_y(p_x) * k.prev_y)
    small, half = 0.125 * both, 0.5 * p_x
    return 0.75 * both + left(small + half) * k.next_x + right(small - half) * k.prev_x


def deformation(below, mid, above, k):
    deform = []
    for comp in range(3):
        row = list(gradients(below[comp], mid[comp], above[comp], k))
        row[comp] = row[comp] + 1.0
        deform.append(row)
    return deform


def passive_stress(deform):
    right_c = {}
    for a_pos, b_pos in PAIRS:
        right_c[a_pos, b_pos] = sum(deform[i_pos][a_pos] * deform[i_pos][b_pos] for i_pos in range(3))
    strain = {}
    for a_pos, b_pos in PAIRS:
        strain[a_pos, b_pos] = 0.5 * (right_c[a_pos, b_pos] - (1.0 if a_pos == b_pos else 0.0))
    trace = strain[0, 0] + strain[1, 1] + strain[2, 2]
    second = {}
    for a_pos, b_pos in PAIRS:
        entry = (2.0 * SHEAR) * strain[a_pos, b_pos]
        if a_pos == b_pos:
            entry = entry + LAME_FIRST * trace
        second[a_pos, b_pos] = entry
        second[b_pos, a_pos] = entry
    return second


def times(deform, second):
    return [
        [sum(deform[i_pos][b_pos] * second[b_pos, a_pos] for b_pos in range(3)) for a_pos in range(3)]
        for i_pos in range(3)
    ]


def metric(deform, fdir):
    def cofactor(i_pos, j_pos):
        i_next, i_last = (i_pos + 1) % 3, (i_pos + 2) % 3
        j_next, j_last = (j_pos + 1) % 3, (j_pos + 2) % 3
        return deform[i_next][j_next] * deform[i_last][j_last] - deform[i_next][j_last] * deform[i_last][j_next]

    cof = [[cofactor(i_pos, j_pos) for j_pos in range(3)] for i_pos in range(3)]
    det = deform[0][0] * cof[0][0] + deform[0][1] * cof[0][1] + deform[0][2] * cof[0][2]
    scale = 1.0 / det
    inv = [[cof[i_pos][j_pos] * scale for i_pos in range(3)] for j_pos in range(3)]
    along = [sum(inv[a_pos][i_pos] * fdir[i_pos] for i_pos in range(3)) for a_pos in range(3)]
    comps = []
    for a_pos, b_pos in PAIRS:
        inner = sum(inv[a_pos][i_pos] * inv[b_pos][i_pos] for i_pos in range(3))
        comps.append(SIGMA_TRANS * inner + (SIGMA_LONG - SIGMA_TRANS) * along[a_pos] * along[b_pos])
    return comps


def inside(slab, slabs, offset):
    spot = slab + offset
    return jnp.where((spot >= 0) & (spot < slabs), 1.0, 0.0)


class Planes:
    def __init__(self, field, slabs, reach, order):
        self.slabs, self.reach, self.order = slabs, reach, order
        self.parts = [field[None]]
        self.doubling = slabs == 8
        self.rounds = 0

    def round(self):
        if self.doubling:
            held = jnp.concatenate(self.parts, axis=0) if len(self.parts) > 1 else self.parts[0]
            perm = [(i, i ^ self.order[self.rounds]) for i in range(self.slabs)]
            self.take(lax.ppermute(held, "slab", perm))
        elif self.rounds == 0:
            for shift in self.shifts()[1:]:
                perm = [((i + shift) % self.slabs, i) for i in range(self.slabs)]
                self.take(lax.ppermute(self.parts[0], "slab", perm))

    def take(self, part):
        self.parts.append(part)
        self.rounds += 1

    def shifts(self):
        return sorted({offset % self.slabs for offset in range(-self.reach, self.reach + 1)})

    def spot(self, slab, offset):
        if self.doubling:
            apart = slab ^ jnp.clip(slab + offset, 0, self.slabs - 1)
            bits = [(apart & step) // step for step in self.order]
            return bits[0] + 2 * bits[1] + 4 * bits[2]
        return self.shifts().index(offset % self.slabs)


def fiber_table():
    index = jnp.arange(128, dtype=jnp.float32)
    theta = -1.0 + 2.0 * index / (NFIB - 1)
    tilt = 0.3 * jnp.sin(3.0 * index)
    return jnp.stack([jnp.sin(tilt), jnp.cos(tilt) * jnp.sin(theta), jnp.cos(tilt) * jnp.cos(theta)])


def facing_fields_kernel(info_ref, *refs):
    out_ref = refs[-1]
    upper_side = info_ref[SIDE] == 0
    at = 0
    for ref in refs[:-1]:
        for pos in range(ref.shape[0]):
            for comp in range(ref.shape[1]):
                both = ref[pos, comp]
                half = both.shape[-1] // 2
                out_ref[at, comp] = jnp.where(upper_side, both[:, half:], both[:, :half])
            at += 1


def facing_rows(info, fields):
    _, comps, _, width = fields[0].shape
    count = sum(field.shape[0] for field in fields)
    vmem = pl.BlockSpec(memory_space=pltpu.VMEM)
    return pl.pallas_call(
        facing_fields_kernel,
        in_specs=[pl.BlockSpec(memory_space=pltpu.SMEM)] + [vmem] * len(fields),
        out_shape=shape_of(count, comps, 8, width // 2),
        compiler_params=params(),
        cost_estimate=cost(0, 600_000),
        name="facing",
    )(info, *fields)


def passive_kernel(planes, info_ref, table_ref, strip_ref, *refs):
    own_refs, (disp_out, stress_out, pull_out, disp_all, field) = refs[:-5], refs[-5:]
    slab, slabs = info_ref[SLAB], planes.slabs
    width = strip_ref.shape[-1]
    own = ROWS - 8
    k = Weights(info_ref[SIDE], own, width)
    reach = REACH + 1

    at = 0
    for ref in own_refs:
        for pos in range(ref.shape[0]):
            for comp in range(ref.shape[1]):
                both = ref[pos, comp]
                field[at, comp] = jnp.concatenate([both[:, :width], both[:, width:], strip_ref[at, comp]], axis=0)
            at += 1

    def plane(comp, offset):
        return field[planes.spot(slab, offset), comp]

    for offset in range(-reach, reach + 1):
        factor = inside(slab, slabs, offset)
        for comp in range(3):
            disp_all[comp, offset + reach] = plane(comp, offset) * factor

    tables = [jnp.broadcast_to(table_ref[comp : comp + 1], (8, 128)) for comp in range(3)]

    def direction(index, comp):
        index = index.astype(jnp.int32)
        rows = []
        for top in range(0, ROWS, 8):
            parts = [
                jnp.take_along_axis(tables[comp], index[top : top + 8, at : at + 128], axis=1, mode="promise_in_bounds")
                for at in range(0, width, 128)
            ]
            rows.append(jnp.concatenate(parts, axis=1))
        return jnp.concatenate(rows, axis=0)

    for step in range(2 * REACH + 1):
        offset = step - REACH
        below, mid, above = ([disp_all[comp, step + shift] for comp in range(3)] for shift in range(3))
        factor = inside(slab, slabs, offset)
        deform = deformation(below, mid, above, k)
        stress = times(deform, passive_stress(deform))
        index = plane(3, offset)
        fdir = [direction(index, comp) for comp in range(3)]
        for i_pos in range(3):
            pull = (ACTIVE_GAIN * factor) * sum(deform[i_pos][b_pos] * fdir[b_pos] for b_pos in range(3))
            for a_pos in range(3):
                stress_out[3 * i_pos + a_pos, step] = stress[i_pos][a_pos] * factor
                pull_out[3 * i_pos + a_pos, step] = pull * fdir[a_pos]
            disp_out[i_pos, step] = mid[i_pos]
            disp_out[3 + i_pos, step] = fdir[i_pos]


def passive_step(info, planes, strips):
    width = strips.shape[-1]
    count = 2 * REACH + 1
    shapes = [(6, count), (9, count), (9, count)]
    vmem = pl.BlockSpec(memory_space=pltpu.VMEM)
    return pl.pallas_call(
        functools.partial(passive_kernel, planes),
        in_specs=[pl.BlockSpec(memory_space=pltpu.SMEM)] + [vmem] * (2 + len(planes.parts)),
        out_shape=[jax.ShapeDtypeStruct((a, b, ROWS, width), jnp.float32) for a, b in shapes],
        scratch_shapes=[
            pltpu.VMEM((3, count + 2, ROWS, width), jnp.float32),
            pltpu.VMEM(strips.shape[:2] + (ROWS, width), jnp.float32),
        ],
        compiler_params=params(),
        cost_estimate=cost(400 * count * ROWS * width, 5_000_000),
        name="passive",
    )(info, fiber_table(), strips, *planes.parts)


def mechanics_kernel(planes, info_ref, disp_ref, stress_ref, pull_ref, *rest):
    active_refs, (disp_out, cond_out, d_one, p_two, active) = rest[:-5], rest[-5:]
    slab, side, slabs = info_ref[SLAB], info_ref[SIDE], planes.slabs
    own, width = disp_out.shape[-2:]
    k = Weights(side, own, width)

    at = 0
    for ref in active_refs:
        active[at : at + ref.shape[0]] = ref[...]
        at += ref.shape[0]

    def active_at(step):
        return active[planes.spot(slab, step - REACH)]

    for step in range(1, 2 * REACH):
        act = [active_at(step + shift) for shift in (-1, 0, 1)]
        factor = inside(slab, slabs, step - REACH)
        for i_pos in range(3):
            stress = [
                [stress_ref[3 * i_pos + a_pos, step + shift] + act[shift + 1] * pull_ref[3 * i_pos + a_pos, step + shift] for a_pos in range(3)]
                for shift in (-1, 0, 1)
            ]
            moved = disp_ref[i_pos, step] + MECH_RATE * force(stress[0], stress[1], stress[2], k)
            d_one[i_pos, step] = moved * factor

    for step in range(2, 2 * REACH - 1):
        disp = [[d_one[comp, step + shift] for comp in range(3)] for shift in (-1, 0, 1)]
        deform = deformation(disp[0], disp[1], disp[2], k)
        second = passive_stress(deform)
        fdir = [disp_ref[3 + comp, step] for comp in range(3)]
        gain = ACTIVE_GAIN * active_at(step)
        for a_pos, b_pos in PAIRS:
            entry = second[a_pos, b_pos] + gain * fdir[a_pos] * fdir[b_pos]
            second[a_pos, b_pos] = entry
            second[b_pos, a_pos] = entry
        stress = times(deform, second)
        factor = inside(slab, slabs, step - REACH)
        for i_pos in range(3):
            for a_pos in range(3):
                p_two[3 * i_pos + a_pos, step] = stress[i_pos][a_pos] * factor

    last = []
    for step in (REACH - 1, REACH, REACH + 1):
        factor = inside(slab, slabs, step - REACH)
        row = []
        for i_pos in range(3):
            stress = [[p_two[3 * i_pos + a_pos, step + shift] for a_pos in range(3)] for shift in (-1, 0, 1)]
            moved = d_one[i_pos, step] + MECH_RATE * force(stress[0], stress[1], stress[2], k)
            row.append(moved * factor)
        last.append(row)
    deform = deformation(last[0], last[1], last[2], k)
    comps = metric(deform, [disp_ref[3 + comp, REACH] for comp in range(3)])
    for i_pos in range(3):
        disp_out[i_pos, 0] = last[1][i_pos][:own]
    for pos, comp in enumerate(comps):
        cond_out[pos, 0] = comp[:own]


def mechanics_step(info, own, planes, window):
    width = planes.parts[0].shape[-1]
    count = 2 * REACH + 1
    held = sum(part.shape[0] for part in planes.parts)
    vmem = pl.BlockSpec(memory_space=pltpu.VMEM)
    return pl.pallas_call(
        functools.partial(mechanics_kernel, planes),
        in_specs=[pl.BlockSpec(memory_space=pltpu.SMEM)] + [vmem] * (3 + len(planes.parts)),
        out_shape=[
            jax.ShapeDtypeStruct((3, 1, own, width), jnp.float32),
            jax.ShapeDtypeStruct((6, 1, own, width), jnp.float32),
        ],
        scratch_shapes=[
            pltpu.VMEM((3, count, ROWS, width), jnp.float32),
            pltpu.VMEM((9, count, ROWS, width), jnp.float32),
            pltpu.VMEM((held, ROWS, width), jnp.float32),
        ],
        compiler_params=params(),
        cost_estimate=cost(400 * count * ROWS * width, 5_000_000),
        name="mechanics",
    )(info, *window, *planes.parts)


def tie(*arrays):
    return lax.optimization_barrier(arrays)


def on_device(states, cond, tension, fiber, disp):
    slabs = lax.axis_size("slab")
    slab, col = lax.axis_index("slab"), lax.axis_index("col")
    _, planes, rows, width = states.shape
    own = rows // 8
    flip = slab % 2
    far_exists = (slab > 0) & (slab < slabs - 1)
    info = jnp.stack([slab, col, flip, far_exists]).astype(jnp.int32)

    pairs = [(i, i ^ 1) for i in range(slabs)]
    others = [(i, i if i in (0, slabs - 1) else ((i + 1) ^ 1) - 1) for i in range(slabs)]
    swap = [(0, 1), (1, 0)]

    tiled = states.reshape(4, planes, own, 8, width)
    fields = Planes(own_field(disp, fiber), slabs, REACH + 1, (1, 4, 2))
    edges, facing, cond_rows = facing_parts(info, tiled, cond)
    edges = lax.ppermute(edges, "col", swap)
    cond_strip = lax.ppermute(cond_rows, "col", swap)
    strip = lax.ppermute(facing, "col", swap)
    carried = fields.parts if fields.doubling else []
    far, near = first_sends(info, edges, tiled, carried)
    far_halo = lax.ppermute(far, "slab", others)
    near_halo = lax.ppermute(near, "slab", pairs)

    coeffs = fine_coeffs(info, cond, cond_strip)
    whole = jnp.concatenate([tiled, strip[:, :, None]], axis=2)

    far_part, far_inner, far_gates = half_step("first", FAR_HALF, info, (whole,), coeffs)
    near_part, near_inner, near_gates = half_step("first", NEAR_HALF, info, (whole,), coeffs)
    if fields.doubling:
        near_part, near_halo = tie(near_part, near_halo)
        fields.take(near_halo[SENT:][None])
    for turn_index in range(1, SUB):
        last = turn_index == SUB - 1
        far, far_send = halo_step(FAR_HALF, info, far_part, far_halo, coeffs)
        far_halo = lax.ppermute(far_send, "slab", others)
        far_arrays = (far, far_inner, near_inner, far_gates)
        kind = "last" if last else "middle"
        far_part, far_next, far_gates = half_step(kind, FAR_HALF, info, far_arrays, coeffs)
        if turn_index >= 2:
            near_part, *fields.parts = tie(near_part, *fields.parts)
        near, near_send = halo_step(NEAR_HALF, info, near_part, near_halo, coeffs)
        near_halo = lax.ppermute(near_send, "slab", pairs)
        if not last:
            fields.round()
        near_arrays = (near, near_inner, far_inner, near_gates)
        near_part, near_inner, near_gates = half_step(kind, NEAR_HALF, info, near_arrays, coeffs)
        far_inner = far_next
    strips = lax.ppermute(facing_rows(info, fields.parts), "col", swap)
    states_next, tension_next, active = finish_half(
        FAR_HALF, info, far_part, far_inner, far_halo, coeffs, tension, (far_gates, near_inner, near_gates)
    )
    window = passive_step(info, fields, strips)
    states_next, tension_next, active, facing = finish_half(
        NEAR_HALF, info, near_part, near_inner, near_halo, coeffs, tension, (active, states_next, tension_next)
    )
    active_strip = lax.ppermute(facing, "col", swap)
    actives = Planes(jnp.concatenate([active, active_strip], axis=0), slabs, REACH, (4, 1, 2))
    for _ in range(3):
        actives.round()
    disp_next, cond_next = mechanics_step(info, disp.shape[2], actives, window)
    return (states_next.reshape(states.shape), tension_next, disp_next, cond_next)


def solution(mesh):
    in_specs = (
        P(None, ("grp", "slab"), "col", None),
        P(None, ("grp", "slab"), "col", None),
        P(("grp", "slab"), "col", None),
        P(("grp", "slab"), "col", None),
        P(None, ("grp", "slab"), "col", None),
    )
    out_specs = (
        P(None, ("grp", "slab"), "col", None),
        P(("grp", "slab"), "col", None),
        P(None, ("grp", "slab"), "col", None),
        P(None, ("grp", "slab"), "col", None),
    )
    return jax.shard_map(
        on_device, mesh=mesh, in_specs=in_specs, out_specs=out_specs, check_vma=False
    )
```

```python
import functools

import jax
import jax.numpy as jnp
from jax import lax
from jax.experimental import pallas as pl
from jax.experimental.pallas import tpu as pltpu
from jax.sharding import PartitionSpec as P

SUB = 4
MECH_STEPS = 2
NFIB = 64

STEP_TIME = 0.05
LAME_FIRST = 1.0
SHEAR = 0.5
ACTIVE_GAIN = 0.5
MECH_RATE = 0.15
SIGMA_LONG = 0.16
SIGMA_TRANS = 0.04
PAIRS = ((0, 0), (1, 1), (2, 2), (0, 1), (0, 2), (1, 2))

C_ZZ, C_ZY, C_ZXR, C_ZXL, C_MID, C_YY, C_XXR, C_YXR, C_XXL, C_YXL = range(10)

SLAB, SIDE, FLIP, FAR = range(4)

LIMIT = 40 * 1024 * 1024


def params(**kwargs):
    return pltpu.CompilerParams(vmem_limit_bytes=LIMIT, **kwargs)


def cost(flops, nbytes, trans=0):
    return pl.CostEstimate(flops=flops, bytes_accessed=nbytes, transcendentals=trans)


def row_iota():
    return lax.broadcasted_iota(jnp.int32, (8, 1024), 0)


def next_row(cur, nxt, sub):
    return pltpu.roll(jnp.where(sub == 0, nxt, cur), 7, 0)


def prev_row(cur, prv, sub):
    return pltpu.roll(jnp.where(sub == 7, prv, cur), 1, 0)


def left(val):
    return pltpu.roll(val, val.shape[-1] - 1, val.ndim - 1)


def right(val):
    return pltpu.roll(val, 1, val.ndim - 1)


def edge_masks(tile, side, own):
    before = jnp.where((tile == 0) & (side == 0), 0.0, 1.0)
    after = jnp.where((tile == own - 1) & (side == 1), 0.0, 1.0)
    return before, after


def ring_neighbours(tile, tiles):
    before = jnp.where(tile == 0, tiles - 1, tile - 1)
    after = jnp.where(tile == tiles - 1, 0, tile + 1)
    return before, after


def split_dot(rest, pick):
    total = None
    for _ in range(3):
        part = rest.astype(jnp.bfloat16)
        rest = rest - part.astype(jnp.float32)
        product = jnp.dot(part, pick, preferred_element_type=jnp.float32)
        total = product if total is None else total + product
    return total


def coeff_kernel(info_ref, cond_ref, strip_ref, out_ref):
    rows, width = cond_ref.shape[-2:]
    turn = jnp.where(info_ref[FLIP] == 1, -0.5, 0.5)
    upper_side = info_ref[SIDE] == 0
    fine = 4 * width
    apart = lax.broadcasted_iota(jnp.int32, (width, fine), 1) - 4 * lax.broadcasted_iota(jnp.int32, (width, fine), 0)
    own = rows // 2
    sub = lax.broadcasted_iota(jnp.int32, (8, width), 0)

    def tall(val):
        tiles = []
        for row in range(0, val.shape[0], 2):
            first, second = (jnp.broadcast_to(val[at : at + 1], (8, width)) for at in (row, row + 1))
            tiles.append(jnp.where(sub < 4, first, second))
        return tiles

    comps = []
    for comp in range(6):
        strip = tall(strip_ref[comp])
        comps.append(tall(cond_ref[comp, 0]) + [jnp.where(upper_side, strip[0], strip[-1])])

    def spread(names, shift):
        pick = jnp.where((apart >= -shift) & (apart < 4 - shift), 1.0, 0.0).astype(jnp.bfloat16)
        return split_dot(jnp.concatenate([tile for name in names for tile in comps[name]], axis=0), pick)

    def store(index, wide, place, factor):
        for tile in range(own + 1):
            at = 8 * (place * (own + 1) + tile)
            out_ref[index, tile] = wide[at : at + 8] if factor is None else factor * wide[at : at + 8]

    wide = spread((0, 1, 3, 2), 0)
    store(C_ZZ, wide, 0, None)
    store(C_YY, wide, 1, None)
    store(C_ZY, wide, 2, turn)
    for tile in range(own + 1):
        zz, yy, xx = (wide[8 * (place * (own + 1) + tile) :][:8] for place in (0, 1, 3))
        out_ref[C_MID, tile] = 1.0 - 2.0 * (zz + yy + xx)
    for shift, (name_xx, name_zx, name_yx) in ((-1, (C_XXR, C_ZXR, C_YXR)), (1, (C_XXL, C_ZXL, C_YXL))):
        wide = spread((2, 4, 5), shift)
        store(name_xx, wide, 0, None)
        store(name_zx, wide, 1, turn)
        store(name_yx, wide, 2, 0.5)


def fine_coeffs(info, cond, strip):
    rows, width = cond.shape[-2:]
    vmem = pl.BlockSpec(memory_space=pltpu.VMEM)
    return pl.pallas_call(
        coeff_kernel,
        in_specs=[pl.BlockSpec(memory_space=pltpu.SMEM), vmem, vmem],
        out_shape=jax.ShapeDtypeStruct((10, rows // 2 + 1, 8, 4 * width), jnp.float32),
        compiler_params=params(),
        cost_estimate=cost(2_000_000, 3_200_000),
        name="coeffs",
    )(info, cond, strip)


SENT, FIELD = 17, 4


def packed_strip(strip, side):
    half = strip.shape[-1] // 2
    low, high = strip[:, :half], strip[:, half:]
    sub = lax.broadcasted_iota(jnp.int32, low.shape, 0)
    first = jnp.where(side == 0, low, pltpu.roll(low, 4, 0))
    second = jnp.where(side == 0, pltpu.roll(high, 4, 0), high)
    return jnp.where(sub < 4, first, second)


def store_sent(ref, tile, tiles, value, side):
    half = value.shape[-1] // 2
    if tile < tiles - 1:
        ref[tile] = value[:, :half]
        ref[tiles - 1 + tile] = value[:, half:]
    else:
        ref[2 * tile] = packed_strip(value, side)


def load_sent(ref, tile, tiles, side):
    if tile < tiles - 1:
        return jnp.concatenate([ref[tile], ref[tiles - 1 + tile]], axis=1)
    packed = ref[2 * tile]
    turned = pltpu.roll(packed, 4, 0)
    return jnp.concatenate([jnp.where(side == 0, packed, turned), jnp.where(side == 0, turned, packed)], axis=1)


SMEM = pl.BlockSpec(memory_space=pltpu.SMEM)
VMEM = pl.BlockSpec(memory_space=pltpu.VMEM)


def shape_of(*shape):
    return jax.ShapeDtypeStruct(shape, jnp.float32)


def facing_kernel(info_ref, states_ref, cond_ref, edge_ref, facing_ref, cond_rows):
    flip, side = info_ref[FLIP], info_ref[SIDE]
    comps, planes, own = states_ref.shape[:3]
    edge = (1 - side) * (own - 1)
    edge_ref[0] = states_ref[0, flip * (planes - 1), edge]
    edge_ref[1] = states_ref[0, (1 - flip) * (planes - 1), edge]
    for comp in range(comps):
        for plane in range(planes):
            facing_ref[comp, plane] = states_ref[comp, plane, edge]
    first = pl.multiple_of(8 * (1 - side), 8)
    for comp in range(cond_ref.shape[0]):
        cond_rows[comp] = cond_ref[comp, 0, pl.ds(first, 8), :]


def field_kernel(disp_ref, fiber_ref, field_ref):
    for comp in range(3):
        field_ref[comp] = jnp.concatenate([disp_ref[comp, 0, :8], disp_ref[comp, 0, 8:]], axis=1)
    index = fiber_ref[0].astype(jnp.float32)
    field_ref[3] = jnp.concatenate([index[:8], index[8:]], axis=1)


def own_field(disp, fiber):
    return pl.pallas_call(
        field_kernel,
        in_specs=[VMEM] * 2,
        out_specs=VMEM,
        out_shape=shape_of(FIELD, 8, 2 * disp.shape[-1]),
        compiler_params=params(),
        cost_estimate=cost(0, 130_000),
        name="own_field",
    )(disp, fiber)


def sends_kernel(info_ref, edge_ref, states_ref, far_ref, near_ref):
    flip, side = info_ref[FLIP], info_ref[SIDE]
    planes, own = states_ref.shape[1:3]
    for pos, (ref, plane) in enumerate([(far_ref, flip * (planes - 1)), (near_ref, (1 - flip) * (planes - 1))]):
        for tile in range(own):
            store_sent(ref, tile, own + 1, states_ref[0, plane, tile], side)
        store_sent(ref, own, own + 1, edge_ref[pos], side)


def facing_parts(info, tiled, cond):
    comps, planes, _, _, width = tiled.shape
    return pl.pallas_call(
        facing_kernel,
        in_specs=[SMEM, VMEM, VMEM],
        out_specs=[VMEM] * 3,
        out_shape=[
            shape_of(2, 8, width),
            shape_of(comps, planes, 8, width),
            shape_of(cond.shape[0], 8, cond.shape[-1]),
        ],
        compiler_params=params(),
        cost_estimate=cost(0, 1_200_000),
        name="facing_parts",
    )(info, tiled, cond)


def first_sends(info, edges, tiled):
    width = tiled.shape[-1]
    return pl.pallas_call(
        sends_kernel,
        in_specs=[SMEM] + [VMEM] * 2,
        out_specs=[VMEM] * 2,
        out_shape=[shape_of(SENT, 8, width // 2)] * 2,
        compiler_params=params(),
        cost_estimate=cost(0, 1_200_000),
        name="sends",
    )(info, edges, tiled)


def fraction(val):
    return pl.reciprocal(val, approx=True)


def ionic(u, v, w, s):
    dt = STEP_TIME
    steep = 50.0 * u
    t_v = jnp.tanh(steep - 15.0)
    t_w = jnp.tanh(steep - 6.5)
    t_o = jnp.tanh(steep - 0.3)
    t_m = jnp.tanh(65.0 * u - 65.0 * 0.03)
    t_f = jnp.tanh(2.0458 * u - 2.0458 * 0.65)
    t_s = jnp.tanh(2.0994 * u - 2.0994 * 0.9087)
    hv, nv = 1.0 + t_v, 1.0 - t_v
    hw, nw = 1.0 + t_w, 1.0 - t_w
    no = 0.5 - 0.5 * t_o
    half_so = 0.5 * (30.0181 - 0.9957)
    r_vm = fraction(2.0 / dt * 605.0 + (2.0 / dt * 545.0) * t_o)
    r_wm = fraction(2.0 / dt * 37.5 - (2.0 / dt * 22.5) * t_m)
    r_so = fraction(2.0 / dt * (30.0181 - half_so) - (2.0 / dt * half_so) * t_f)
    r_s = fraction(9.3671 / dt + (6.6329 / dt) * t_w)
    r_o = fraction(2.0 / dt * 203.0 - (2.0 / dt * 197.0) * t_o)
    w_inf = 0.94 + no * (0.06 - u * (1.0 / 0.07))
    hvv = hv * v
    hww = hw * w
    fast = hvv * ((u - 0.3) * (0.5 * dt / 0.11 * 1.55 - (0.5 * dt / 0.11) * u))
    out = (u * nw) * r_o + hw * r_so
    slow = hww * (s * (0.5 * dt / 1.8875))
    v_new = v + (nv * (no - v)) * r_vm - hvv * (0.5 * dt / 1.4506)
    w_new = w + (nw * (w_inf - w)) * r_wm - hww * (0.5 * dt / 200.0)
    s_new = s + ((0.5 + 0.5 * t_s) - s) * r_s
    return fast + slow - out, v_new, w_new, s_new


FAR_HALF, NEAR_HALF = -1, 1


def half_place(info_ref, half):
    flip = info_ref[FLIP]
    return (flip, flip) if half == FAR_HALF else (1 - flip, 1 - flip)


def half_kernel(kind, half, tiles, info_ref, *refs):
    side = info_ref[SIDE]
    sub = row_iota()
    own = tiles - 1
    index, outer = half_place(info_ref, half)
    if kind == "first":
        whole_ref, coeff_ref, outer_out, inner_out, gate_out = refs
        spots = [2 * index + outer, 2 * index + 1 - outer, 2 - index]
        reads = [lambda t, z=z: whole_ref[0, z, t] for z in spots]
    else:
        *u_refs, gate_ref, coeff_ref, outer_out, inner_out, gate_out = refs
        reads = [lambda t, ref=ref: ref[t] for ref in u_refs]

    def diffused(tile):
        before, after = ring_neighbours(tile, tiles)
        mask_before, mask_after = edge_masks(tile, side, own)
        cur = [read(tile) for read in reads]
        prv = [read(before) * mask_before for read in reads]
        nxt = [read(after) * mask_after for read in reads]

        def coeff(index):
            return coeff_ref[index, tile]

        bases = []
        for plane in range(2):
            u = cur[plane]
            if plane == 0:
                around = cur[1]
                wide, wide_nxt, wide_prv = cur[1], nxt[1], prv[1]
            else:
                around = cur[0] + cur[2]
                wide, wide_nxt, wide_prv = cur[2] - cur[0], nxt[2] - nxt[0], prv[2] - prv[0]
            u_next = next_row(u, nxt[plane], sub)
            u_prev = prev_row(u, prv[plane], sub)
            tilt = coeff(C_ZY) * (next_row(wide, wide_nxt, sub) - prev_row(wide, wide_prv, sub))
            tall = u_next - u_prev
            to_left = coeff(C_XXR) * u + coeff(C_YXR) * tall
            to_right = coeff(C_XXL) * u - coeff(C_YXL) * tall
            if half == FAR_HALF:
                to_left += coeff(C_ZXR) * wide
                to_right -= coeff(C_ZXL) * wide
            else:
                to_left -= coeff(C_ZXR) * wide
                to_right += coeff(C_ZXL) * wide
            base = coeff(C_MID) * u + coeff(C_ZZ) * around + coeff(C_YY) * (u_next + u_prev)
            base = base + tilt if half == FAR_HALF else base - tilt
            bases.append(base + left(to_left) + right(to_right))
        return bases

    def react(tile, bases):
        chunk = 256
        for plane in range(2):
            for start in range(0, 1024, chunk):
                lanes = slice(start, start + chunk)
                if kind == "first":
                    u = whole_ref[0, spots[plane], tile, :, lanes]
                    gates = [whole_ref[1 + g, spots[plane], tile, :, lanes] for g in range(3)]
                else:
                    u = u_refs[plane][tile, :, lanes]
                    gates = [gate_ref[g, plane, tile, :, lanes] for g in range(3)]
                u_add, *gates = ionic(u, *gates)
                (outer_out, inner_out)[plane][tile, :, lanes] = bases[plane][:, lanes] + u_add
                for comp, value in enumerate(gates):
                    gate_out[comp, plane, tile, :, lanes] = value

    together = 2 if kind == "last" else 3

    def some(step, carry):
        numbers = [step * together + pos for pos in range(together)]
        held = [diffused(tile) for tile in numbers]
        for tile, bases in zip(numbers, held):
            react(tile, bases)
        return carry

    lax.fori_loop(0, (own if kind == "last" else tiles) // together, some, 0)


def half_step(kind, half, info, arrays, coeffs):
    _, tiles, _, width = coeffs.shape
    vmem = pl.BlockSpec(memory_space=pltpu.VMEM)
    kept = tiles - 1 if kind == "last" else tiles
    plane = jax.ShapeDtypeStruct((kept, 8, width), jnp.float32)
    cells = 2 * tiles * 8 * width
    return pl.pallas_call(
        functools.partial(half_kernel, kind, half, tiles),
        in_specs=[pl.BlockSpec(memory_space=pltpu.SMEM)] + [vmem] * (len(arrays) + 1),
        out_specs=[vmem] * 3,
        out_shape=[plane, plane, jax.ShapeDtypeStruct((3, 2, kept, 8, width), jnp.float32)],
        compiler_params=params(),
        cost_estimate=cost(100 * cells, 40 * cells, 11 * cells),
        name=kind + ("_far" if half == FAR_HALF else "_near"),
    )(info, *arrays, coeffs)


def halo_terms(halo_ref, coeff_ref, tile, tiles, side, sub, half):
    before, after = (tile - 1) % tiles, (tile + 1) % tiles
    cur, prv, nxt = (load_sent(halo_ref, at, tiles, side) for at in (tile, before, after))
    if tile == 0:
        prv = prv * jnp.where(side == 0, 0.0, 1.0)
    if tile == tiles - 2:
        nxt = nxt * jnp.where(side == 1, 0.0, 1.0)
    cross = coeff_ref[C_ZY, tile] * (next_row(cur, nxt, sub) - prev_row(cur, prv, sub))
    cross += left(coeff_ref[C_ZXR, tile] * cur) - right(coeff_ref[C_ZXL, tile] * cur)
    total = coeff_ref[C_ZZ, tile] * cur
    return total - cross if half == FAR_HALF else total + cross


def add_halo(half, tiles, kept, info_ref, outer_ref, halo_ref, coeff_ref, out_ref, sent_ref=None):
    side = info_ref[SIDE]
    sub = row_iota()

    def fill(beyond=True):
        for tile in range(kept):
            value = outer_ref[tile]
            if beyond:
                value += halo_terms(halo_ref, coeff_ref, tile, tiles, side, sub, half)
            out_ref[tile] = value
            if sent_ref is not None:
                store_sent(sent_ref, tile, tiles, value, side)

    if half == NEAR_HALF:
        fill()
    else:
        exists = info_ref[FAR] == 1
        pl.when(exists)(fill)
        pl.when(jnp.logical_not(exists))(functools.partial(fill, False))


def halo_kernel(half, tiles, info_ref, outer_ref, halo_ref, coeff_ref, out_ref, sent_ref):
    add_halo(half, tiles, tiles, info_ref, outer_ref, halo_ref, coeff_ref, out_ref, sent_ref)


def halo_step(half, info, outer, halo, coeffs):
    tiles, _, width = outer.shape
    cells = tiles * 8 * width
    return pl.pallas_call(
        functools.partial(halo_kernel, half, tiles),
        in_specs=[SMEM] + [VMEM] * 3,
        out_specs=[VMEM] * 2,
        out_shape=[shape_of(*outer.shape), shape_of(SENT, 8, width // 2)],
        compiler_params=params(),
        cost_estimate=cost(15 * cells, 20 * cells),
        name="halo" + ("_far" if half == FAR_HALF else "_near"),
    )(info, outer, halo, coeffs)


def pooled(field, rows_ref):
    rows, lanes = field.shape
    fine = lax.broadcasted_iota(jnp.int32, (256, 128), 0)
    coarse = lax.broadcasted_iota(jnp.int32, (256, 128), 1)
    pick = jnp.where((fine >> 1) == coarse, 0.25, 0.0).astype(jnp.bfloat16)
    few = []
    for chunk in range(lanes // 128):
        rows_ref[chunk, :rows] = field[:, 128 * chunk : 128 * chunk + 128]
        even = rows_ref[chunk, pl.ds(0, rows // 2, stride=2), :]
        few.append(even + rows_ref[chunk, pl.ds(1, rows // 2, stride=2), :])
    pairs = [jnp.concatenate(few[pos : pos + 2], axis=1) for pos in range(0, len(few), 2)]
    total = split_dot(jnp.concatenate(pairs, axis=0), pick)
    count = rows // 2
    return jnp.concatenate([total[pos * count : (pos + 1) * count] for pos in range(len(pairs))], axis=1)


def finish_kernel(half, tiles, info_ref, outer_ref, inner_ref, halo_ref, coeff_ref, tension_ref, *refs):
    if half == FAR_HALF:
        gate_ref, near_inner_ref, near_gate_ref, *refs = refs
        states_out, tension_out, active_out, u_ref, layer_ref, rows_ref, sems = refs
        moves = []
        for which, inners, gates in ((FAR_HALF, inner_ref, gate_ref), (NEAR_HALF, near_inner_ref, near_gate_ref)):
            index, outer = half_place(info_ref, which)
            place = [2 * index + outer, 2 * index + 1 - outer]
            moves += [(gates.at[g, plane], states_out.at[1 + g, place[plane]]) for g in range(3) for plane in range(2)]
            moves.append((inners, states_out.at[0, place[1]]))
    else:
        active_ref, _, _, states_out, tension_out, active_out, facing_out, u_ref, layer_ref, rows_ref, sems = refs
        moves = []
    copies = []

    def start(src, dst):
        copies.append(pltpu.make_async_copy(src, dst, sems.at[len(copies)]))
        copies[-1].start()

    for src, dst in moves:
        start(src, dst)
    index, outer = half_place(info_ref, half)
    own = tiles - 1
    add_halo(half, tiles, own, info_ref, outer_ref, halo_ref, coeff_ref, u_ref)
    start(u_ref, states_out.at[0, 2 * index + outer])
    both = 0.5 * (u_ref[...] + inner_ref[...])
    mean = pooled(both.reshape(own * 8, both.shape[-1]), rows_ref)
    old = tension_ref[index]
    new = old + 0.5 * (mean - old)
    layer_ref[...] = new
    start(layer_ref, tension_out.at[index])
    mean = pooled(0.5 * new, rows_ref)
    if half == FAR_HALF:
        active_out[...] = mean
    else:
        active_out[...] = active_ref[...] + mean
        facing_out[...] = active_out[pl.ds(pl.multiple_of(8 * (1 - info_ref[SIDE]), 8), 8), :]
    for copy in copies:
        copy.wait()


def finish_half(half, info, outer, inner, halo, coeffs, tension, others):
    _, tiles, _, width = coeffs.shape
    own = tiles - 1
    active_shape = (own * 2, width // 4)
    hbm = pl.BlockSpec(memory_space=pltpu.HBM)
    out_specs = [hbm, hbm, VMEM]
    out_shape = [shape_of(4, 4, own, 8, width), shape_of(*tension.shape), shape_of(*active_shape)]
    aliases = {}
    if half == FAR_HALF:
        in_specs = [SMEM] + [VMEM] * 8
    else:
        in_specs = [SMEM] + [VMEM] * 6 + [hbm, hbm]
        aliases = {7: 0, 8: 1}
        out_specs.append(VMEM)
        out_shape.append(shape_of(8, width // 4))
    cells = 2 * own * 8 * width
    return pl.pallas_call(
        functools.partial(finish_kernel, half, tiles),
        in_specs=in_specs,
        out_specs=out_specs,
        out_shape=out_shape,
        scratch_shapes=[
            pltpu.VMEM((own, 8, width), jnp.float32),
            pltpu.VMEM(tension.shape[1:], jnp.float32),
            pltpu.VMEM((width // 128, own * 8, 128), jnp.float32),
            pltpu.SemaphoreType.DMA((16 if half == FAR_HALF else 2,)),
        ],
        input_output_aliases=aliases,
        compiler_params=params(),
        cost_estimate=cost(20 * cells, 20 * cells),
        name="finish" + ("_far" if half == FAR_HALF else "_near"),
    )(info, outer, inner, halo, coeffs, tension, *others)


REACH = 4
ROWS = 24


class Weights:
    def __init__(self, side, own, width):
        row = lax.broadcasted_iota(jnp.int32, (ROWS, width), 0)
        lane = lax.broadcasted_iota(jnp.int32, (ROWS, width), 1)
        self.next_y = jnp.where((row == own - 1) & (side == 1), 0.0, 1.0)
        self.prev_y = jnp.where((row == 0) & (side == 0), 0.0, 1.0)
        self.next_x = jnp.where(lane == width - 1, 0.0, 1.0)
        self.prev_x = jnp.where(lane == 0, 0.0, 1.0)


def up_y(val):
    return pltpu.roll(val, ROWS - 1, 0)


def down_y(val):
    return pltpu.roll(val, 1, 0)


def slope_z(below, mid, above):
    return 0.5 * (above - below)


def smooth_z(below, mid, above):
    return 0.75 * mid + 0.125 * (above + below)


def gradients(below, mid, above, k):
    slope = slope_z(below, mid, above)
    smooth = smooth_z(below, mid, above)
    slope_s = 0.75 * slope + 0.125 * (up_y(slope) * k.next_y + down_y(slope) * k.prev_y)
    ahead = up_y(smooth) * k.next_y
    behind = down_y(smooth) * k.prev_y
    smooth_s = 0.75 * smooth + 0.125 * (ahead + behind)
    smooth_d = 0.5 * (ahead - behind)

    def smooth_x(val):
        return 0.75 * val + 0.125 * (left(val) * k.next_x + right(val) * k.prev_x)

    return (
        smooth_x(slope_s),
        smooth_x(smooth_d),
        0.5 * (left(smooth_s) * k.next_x - right(smooth_s) * k.prev_x),
    )


def force(below, mid, above, k):
    p_z = slope_z(below[0], mid[0], above[0])
    p_y = smooth_z(below[1], mid[1], above[1])
    p_x = smooth_z(below[2], mid[2], above[2])
    small, half = 0.125 * p_z, 0.5 * p_y
    both = 0.75 * p_z + up_y(small + half) * k.next_y + down_y(small - half) * k.prev_y
    p_x = 0.75 * p_x + 0.125 * (up_y(p_x) * k.next_y + down_y(p_x) * k.prev_y)
    small, half = 0.125 * both, 0.5 * p_x
    return 0.75 * both + left(small + half) * k.next_x + right(small - half) * k.prev_x


def deformation(below, mid, above, k):
    deform = []
    for comp in range(3):
        row = list(gradients(below[comp], mid[comp], above[comp], k))
        row[comp] = row[comp] + 1.0
        deform.append(row)
    return deform


def passive_stress(deform):
    right_c = {}
    for a_pos, b_pos in PAIRS:
        right_c[a_pos, b_pos] = sum(deform[i_pos][a_pos] * deform[i_pos][b_pos] for i_pos in range(3))
    strain = {}
    for a_pos, b_pos in PAIRS:
        strain[a_pos, b_pos] = 0.5 * (right_c[a_pos, b_pos] - (1.0 if a_pos == b_pos else 0.0))
    trace = strain[0, 0] + strain[1, 1] + strain[2, 2]
    second = {}
    for a_pos, b_pos in PAIRS:
        entry = (2.0 * SHEAR) * strain[a_pos, b_pos]
        if a_pos == b_pos:
            entry = entry + LAME_FIRST * trace
        second[a_pos, b_pos] = entry
        second[b_pos, a_pos] = entry
    return second


def times(deform, second):
    return [
        [sum(deform[i_pos][b_pos] * second[b_pos, a_pos] for b_pos in range(3)) for a_pos in range(3)]
        for i_pos in range(3)
    ]


def metric(deform, fdir):
    def cofactor(i_pos, j_pos):
        i_next, i_last = (i_pos + 1) % 3, (i_pos + 2) % 3
        j_next, j_last = (j_pos + 1) % 3, (j_pos + 2) % 3
        return deform[i_next][j_next] * deform[i_last][j_last] - deform[i_next][j_last] * deform[i_last][j_next]

    cof = [[cofactor(i_pos, j_pos) for j_pos in range(3)] for i_pos in range(3)]
    det = deform[0][0] * cof[0][0] + deform[0][1] * cof[0][1] + deform[0][2] * cof[0][2]
    scale = 1.0 / det
    inv = [[cof[i_pos][j_pos] * scale for i_pos in range(3)] for j_pos in range(3)]
    along = [sum(inv[a_pos][i_pos] * fdir[i_pos] for i_pos in range(3)) for a_pos in range(3)]
    comps = []
    for a_pos, b_pos in PAIRS:
        inner = sum(inv[a_pos][i_pos] * inv[b_pos][i_pos] for i_pos in range(3))
        comps.append(SIGMA_TRANS * inner + (SIGMA_LONG - SIGMA_TRANS) * along[a_pos] * along[b_pos])
    return comps


def inside(slab, slabs, offset):
    spot = slab + offset
    return jnp.where((spot >= 0) & (spot < slabs), 1.0, 0.0)


class Planes:
    def __init__(self, field, slabs, reach, order):
        self.slabs, self.reach, self.order = slabs, reach, order
        self.parts = [field[None]]
        self.doubling = slabs == 8
        self.rounds = 0

    def round(self):
        if self.doubling:
            held = jnp.concatenate(self.parts, axis=0) if len(self.parts) > 1 else self.parts[0]
            perm = [(i, i ^ self.order[self.rounds]) for i in range(self.slabs)]
            self.take(lax.ppermute(held, "slab", perm))
        elif self.rounds == 0:
            for shift in self.shifts()[1:]:
                perm = [((i + shift) % self.slabs, i) for i in range(self.slabs)]
                self.take(lax.ppermute(self.parts[0], "slab", perm))

    def take(self, part):
        self.parts.append(part)
        self.rounds += 1

    def shifts(self):
        return sorted({offset % self.slabs for offset in range(-self.reach, self.reach + 1)})

    def spot(self, slab, offset):
        if self.doubling:
            apart = slab ^ jnp.clip(slab + offset, 0, self.slabs - 1)
            bits = [(apart & step) // step for step in self.order]
            return bits[0] + 2 * bits[1] + 4 * bits[2]
        return self.shifts().index(offset % self.slabs)


def fiber_table():
    index = jnp.arange(128, dtype=jnp.float32)
    theta = -1.0 + 2.0 * index / (NFIB - 1)
    tilt = 0.3 * jnp.sin(3.0 * index)
    return jnp.stack([jnp.sin(tilt), jnp.cos(tilt) * jnp.sin(theta), jnp.cos(tilt) * jnp.cos(theta)])


def facing_fields_kernel(info_ref, *refs):
    out_ref = refs[-1]
    upper_side = info_ref[SIDE] == 0
    at = 0
    for ref in refs[:-1]:
        for pos in range(ref.shape[0]):
            for comp in range(ref.shape[1]):
                both = ref[pos, comp]
                half = both.shape[-1] // 2
                out_ref[at, comp] = jnp.where(upper_side, both[:, half:], both[:, :half])
            at += 1


def facing_rows(info, fields):
    _, comps, _, width = fields[0].shape
    count = sum(field.shape[0] for field in fields)
    vmem = pl.BlockSpec(memory_space=pltpu.VMEM)
    return pl.pallas_call(
        facing_fields_kernel,
        in_specs=[pl.BlockSpec(memory_space=pltpu.SMEM)] + [vmem] * len(fields),
        out_shape=shape_of(count, comps, 8, width // 2),
        compiler_params=params(),
        cost_estimate=cost(0, 600_000),
        name="facing",
    )(info, *fields)


def passive_kernel(planes, info_ref, table_ref, strip_ref, *refs):
    own_refs, (disp_out, stress_out, pull_out, disp_all, field) = refs[:-5], refs[-5:]
    slab, slabs = info_ref[SLAB], planes.slabs
    width = strip_ref.shape[-1]
    own = ROWS - 8
    k = Weights(info_ref[SIDE], own, width)
    reach = REACH + 1

    at = 0
    for ref in own_refs:
        for pos in range(ref.shape[0]):
            for comp in range(ref.shape[1]):
                both = ref[pos, comp]
                field[at, comp] = jnp.concatenate([both[:, :width], both[:, width:], strip_ref[at, comp]], axis=0)
            at += 1

    def plane(comp, offset):
        return field[planes.spot(slab, offset), comp]

    for offset in range(-reach, reach + 1):
        factor = inside(slab, slabs, offset)
        for comp in range(3):
            disp_all[comp, offset + reach] = plane(comp, offset) * factor

    tables = [jnp.broadcast_to(table_ref[comp : comp + 1], (8, 128)) for comp in range(3)]

    def direction(index, comp):
        index = index.astype(jnp.int32)
        rows = []
        for top in range(0, ROWS, 8):
            parts = [
                jnp.take_along_axis(tables[comp], index[top : top + 8, at : at + 128], axis=1, mode="promise_in_bounds")
                for at in range(0, width, 128)
            ]
            rows.append(jnp.concatenate(parts, axis=1))
        return jnp.concatenate(rows, axis=0)

    for step in range(2 * REACH + 1):
        offset = step - REACH
        below, mid, above = ([disp_all[comp, step + shift] for comp in range(3)] for shift in range(3))
        factor = inside(slab, slabs, offset)
        deform = deformation(below, mid, above, k)
        stress = times(deform, passive_stress(deform))
        index = plane(3, offset)
        fdir = [direction(index, comp) for comp in range(3)]
        for i_pos in range(3):
            pull = (ACTIVE_GAIN * factor) * sum(deform[i_pos][b_pos] * fdir[b_pos] for b_pos in range(3))
            for a_pos in range(3):
                stress_out[3 * i_pos + a_pos, step] = stress[i_pos][a_pos] * factor
                pull_out[3 * i_pos + a_pos, step] = pull * fdir[a_pos]
            disp_out[i_pos, step] = mid[i_pos]
            disp_out[3 + i_pos, step] = fdir[i_pos]


def passive_step(info, planes, strips):
    width = strips.shape[-1]
    count = 2 * REACH + 1
    shapes = [(6, count), (9, count), (9, count)]
    vmem = pl.BlockSpec(memory_space=pltpu.VMEM)
    return pl.pallas_call(
        functools.partial(passive_kernel, planes),
        in_specs=[pl.BlockSpec(memory_space=pltpu.SMEM)] + [vmem] * (2 + len(planes.parts)),
        out_shape=[jax.ShapeDtypeStruct((a, b, ROWS, width), jnp.float32) for a, b in shapes],
        scratch_shapes=[
            pltpu.VMEM((3, count + 2, ROWS, width), jnp.float32),
            pltpu.VMEM(strips.shape[:2] + (ROWS, width), jnp.float32),
        ],
        compiler_params=params(),
        cost_estimate=cost(400 * count * ROWS * width, 5_000_000),
        name="passive",
    )(info, fiber_table(), strips, *planes.parts)


def mechanics_kernel(planes, info_ref, disp_ref, stress_ref, pull_ref, *rest):
    active_refs, (disp_out, cond_out, d_one, p_two, active) = rest[:-5], rest[-5:]
    slab, side, slabs = info_ref[SLAB], info_ref[SIDE], planes.slabs
    own, width = disp_out.shape[-2:]
    k = Weights(side, own, width)

    at = 0
    for ref in active_refs:
        active[at : at + ref.shape[0]] = ref[...]
        at += ref.shape[0]

    def active_at(step):
        return active[planes.spot(slab, step - REACH)]

    for step in range(1, 2 * REACH):
        act = [active_at(step + shift) for shift in (-1, 0, 1)]
        factor = inside(slab, slabs, step - REACH)
        for i_pos in range(3):
            stress = [
                [stress_ref[3 * i_pos + a_pos, step + shift] + act[shift + 1] * pull_ref[3 * i_pos + a_pos, step + shift] for a_pos in range(3)]
                for shift in (-1, 0, 1)
            ]
            moved = disp_ref[i_pos, step] + MECH_RATE * force(stress[0], stress[1], stress[2], k)
            d_one[i_pos, step] = moved * factor

    for step in range(2, 2 * REACH - 1):
        disp = [[d_one[comp, step + shift] for comp in range(3)] for shift in (-1, 0, 1)]
        deform = deformation(disp[0], disp[1], disp[2], k)
        second = passive_stress(deform)
        fdir = [disp_ref[3 + comp, step] for comp in range(3)]
        gain = ACTIVE_GAIN * active_at(step)
        for a_pos, b_pos in PAIRS:
            entry = second[a_pos, b_pos] + gain * fdir[a_pos] * fdir[b_pos]
            second[a_pos, b_pos] = entry
            second[b_pos, a_pos] = entry
        stress = times(deform, second)
        factor = inside(slab, slabs, step - REACH)
        for i_pos in range(3):
            for a_pos in range(3):
                p_two[3 * i_pos + a_pos, step] = stress[i_pos][a_pos] * factor

    last = []
    for step in (REACH - 1, REACH, REACH + 1):
        factor = inside(slab, slabs, step - REACH)
        row = []
        for i_pos in range(3):
            stress = [[p_two[3 * i_pos + a_pos, step + shift] for a_pos in range(3)] for shift in (-1, 0, 1)]
            moved = d_one[i_pos, step] + MECH_RATE * force(stress[0], stress[1], stress[2], k)
            row.append(moved * factor)
        last.append(row)
    deform = deformation(last[0], last[1], last[2], k)
    comps = metric(deform, [disp_ref[3 + comp, REACH] for comp in range(3)])
    for i_pos in range(3):
        disp_out[i_pos, 0] = last[1][i_pos][:own]
    for pos, comp in enumerate(comps):
        cond_out[pos, 0] = comp[:own]


def mechanics_step(info, own, planes, window):
    width = planes.parts[0].shape[-1]
    count = 2 * REACH + 1
    held = sum(part.shape[0] for part in planes.parts)
    vmem = pl.BlockSpec(memory_space=pltpu.VMEM)
    return pl.pallas_call(
        functools.partial(mechanics_kernel, planes),
        in_specs=[pl.BlockSpec(memory_space=pltpu.SMEM)] + [vmem] * (3 + len(planes.parts)),
        out_shape=[
            jax.ShapeDtypeStruct((3, 1, own, width), jnp.float32),
            jax.ShapeDtypeStruct((6, 1, own, width), jnp.float32),
        ],
        scratch_shapes=[
            pltpu.VMEM((3, count, ROWS, width), jnp.float32),
            pltpu.VMEM((9, count, ROWS, width), jnp.float32),
            pltpu.VMEM((held, ROWS, width), jnp.float32),
        ],
        compiler_params=params(),
        cost_estimate=cost(400 * count * ROWS * width, 5_000_000),
        name="mechanics",
    )(info, *window, *planes.parts)


def tie(*arrays):
    return lax.optimization_barrier(arrays)


def on_device(states, cond, tension, fiber, disp):
    slabs = lax.axis_size("slab")
    slab, col = lax.axis_index("slab"), lax.axis_index("col")
    _, planes, rows, width = states.shape
    own = rows // 8
    flip = slab % 2
    far_exists = (slab > 0) & (slab < slabs - 1)
    info = jnp.stack([slab, col, flip, far_exists]).astype(jnp.int32)

    pairs = [(i, i ^ 1) for i in range(slabs)]
    others = [(i, i if i in (0, slabs - 1) else ((i + 1) ^ 1) - 1) for i in range(slabs)]
    swap = [(0, 1), (1, 0)]

    tiled = states.reshape(4, planes, own, 8, width)
    fields = Planes(own_field(disp, fiber), slabs, REACH + 1, (1, 4, 2))
    edges, facing, cond_rows = facing_parts(info, tiled, cond)
    edges = lax.ppermute(edges, "col", swap)
    cond_strip = lax.ppermute(cond_rows, "col", swap)
    strip = lax.ppermute(facing, "col", swap)
    far, near = first_sends(info, edges, tiled)
    far_halo = lax.ppermute(far, "slab", others)
    near_halo = lax.ppermute(near, "slab", pairs)
    coeffs = fine_coeffs(info, cond, cond_strip)
    whole = jnp.concatenate([tiled, strip[:, :, None]], axis=2)

    far_part, far_inner, far_gates = half_step("first", FAR_HALF, info, (whole,), coeffs)
    near_kind, near_arrays = "first", (whole,)
    for turn_index in range(1, SUB):
        last = turn_index == SUB - 1
        kind = "last" if last else "middle"
        far, far_send = halo_step(FAR_HALF, info, far_part, far_halo, coeffs)
        far_send, *near_arrays = tie(far_send, *near_arrays)
        near_part, near_inner, near_gates = half_step(near_kind, NEAR_HALF, info, near_arrays, coeffs)
        far_halo = lax.ppermute(far_send, "slab", others)
        far_part, far_next, far_gates = half_step(kind, FAR_HALF, info, (far, far_inner, near_inner, far_gates), coeffs)
        if last:
            near_part, far_part, *fields.parts = tie(near_part, far_part, *fields.parts)
        near, near_send = halo_step(NEAR_HALF, info, near_part, near_halo, coeffs)
        near_halo = lax.ppermute(near_send, "slab", pairs)
        fields.round()
        near_kind, near_arrays = kind, (near, near_inner, far_inner, near_gates)
        far_inner = far_next
    near_part, near_inner, near_gates = half_step(near_kind, NEAR_HALF, info, near_arrays, coeffs)
    strips = lax.ppermute(facing_rows(info, fields.parts), "col", swap)
    states_next, tension_next, active = finish_half(
        FAR_HALF, info, far_part, far_inner, far_halo, coeffs, tension, (far_gates, near_inner, near_gates)
    )
    window = passive_step(info, fields, strips)
    states_next, tension_next, active, facing = finish_half(
        NEAR_HALF, info, near_part, near_inner, near_halo, coeffs, tension, (active, states_next, tension_next)
    )
    active_strip = lax.ppermute(facing, "col", swap)
    actives = Planes(jnp.concatenate([active, active_strip], axis=0), slabs, REACH, (4, 1, 2))
    for _ in range(3):
        actives.round()
    disp_next, cond_next = mechanics_step(info, disp.shape[2], actives, window)
    return (states_next.reshape(states.shape), tension_next, disp_next, cond_next)


def solution(mesh):
    in_specs = (
        P(None, ("grp", "slab"), "col", None),
        P(None, ("grp", "slab"), "col", None),
        P(("grp", "slab"), "col", None),
        P(("grp", "slab"), "col", None),
        P(None, ("grp", "slab"), "col", None),
    )
    out_specs = (
        P(None, ("grp", "slab"), "col", None),
        P(("grp", "slab"), "col", None),
        P(None, ("grp", "slab"), "col", None),
        P(None, ("grp", "slab"), "col", None),
    )
    return jax.shard_map(
        on_device, mesh=mesh, in_specs=in_specs, out_specs=out_specs, check_vma=False
    )
```

```python
import functools

import jax
import jax.numpy as jnp
from jax import lax
from jax.experimental import pallas as pl
from jax.experimental.pallas import tpu as pltpu
from jax.sharding import PartitionSpec as P

SUB = 4
MECH_STEPS = 2
NFIB = 64

STEP_TIME = 0.05
LAME_FIRST = 1.0
SHEAR = 0.5
ACTIVE_GAIN = 0.5
MECH_RATE = 0.15
SIGMA_LONG = 0.16
SIGMA_TRANS = 0.04
PAIRS = ((0, 0), (1, 1), (2, 2), (0, 1), (0, 2), (1, 2))

C_ZZ, C_ZY, C_ZXR, C_ZXL, C_MID, C_YY, C_XXR, C_YXR, C_XXL, C_YXL = range(10)

SLAB, SIDE, FLIP, FAR = range(4)

LIMIT = 40 * 1024 * 1024


def params(**kwargs):
    return pltpu.CompilerParams(vmem_limit_bytes=LIMIT, **kwargs)


def cost(flops, nbytes, trans=0):
    return pl.CostEstimate(flops=flops, bytes_accessed=nbytes, transcendentals=trans)


def row_iota():
    return lax.broadcasted_iota(jnp.int32, (8, 1024), 0)


def next_row(cur, nxt, sub):
    return pltpu.roll(jnp.where(sub == 0, nxt, cur), 7, 0)


def prev_row(cur, prv, sub):
    return pltpu.roll(jnp.where(sub == 7, prv, cur), 1, 0)


def left(val):
    return pltpu.roll(val, val.shape[-1] - 1, val.ndim - 1)


def right(val):
    return pltpu.roll(val, 1, val.ndim - 1)


def edge_masks(tile, side, own):
    before = jnp.where((tile == 0) & (side == 0), 0.0, 1.0)
    after = jnp.where((tile == own - 1) & (side == 1), 0.0, 1.0)
    return before, after


def ring_neighbours(tile, tiles):
    before = jnp.where(tile == 0, tiles - 1, tile - 1)
    after = jnp.where(tile == tiles - 1, 0, tile + 1)
    return before, after


def split_dot(rest, pick):
    total = None
    for _ in range(3):
        part = rest.astype(jnp.bfloat16)
        rest = rest - part.astype(jnp.float32)
        product = jnp.dot(part, pick, preferred_element_type=jnp.float32)
        total = product if total is None else total + product
    return total


def coeff_kernel(info_ref, cond_ref, strip_ref, out_ref):
    rows, width = cond_ref.shape[-2:]
    turn = jnp.where(info_ref[FLIP] == 1, -0.5, 0.5)
    upper_side = info_ref[SIDE] == 0
    fine = 4 * width
    apart = lax.broadcasted_iota(jnp.int32, (width, fine), 1) - 4 * lax.broadcasted_iota(jnp.int32, (width, fine), 0)
    own = rows // 2
    sub = lax.broadcasted_iota(jnp.int32, (8, width), 0)

    def tall(val):
        tiles = []
        for row in range(0, val.shape[0], 2):
            first, second = (jnp.broadcast_to(val[at : at + 1], (8, width)) for at in (row, row + 1))
            tiles.append(jnp.where(sub < 4, first, second))
        return tiles

    comps = []
    for comp in range(6):
        strip = tall(strip_ref[comp])
        comps.append(tall(cond_ref[comp, 0]) + [jnp.where(upper_side, strip[0], strip[-1])])

    def spread(names, shift):
        pick = jnp.where((apart >= -shift) & (apart < 4 - shift), 1.0, 0.0).astype(jnp.bfloat16)
        return split_dot(jnp.concatenate([tile for name in names for tile in comps[name]], axis=0), pick)

    def store(index, wide, place, factor):
        for tile in range(own + 1):
            at = 8 * (place * (own + 1) + tile)
            out_ref[index, tile] = wide[at : at + 8] if factor is None else factor * wide[at : at + 8]

    wide = spread((0, 1, 3, 2), 0)
    store(C_ZZ, wide, 0, None)
    store(C_YY, wide, 1, None)
    store(C_ZY, wide, 2, turn)
    for tile in range(own + 1):
        zz, yy, xx = (wide[8 * (place * (own + 1) + tile) :][:8] for place in (0, 1, 3))
        out_ref[C_MID, tile] = 1.0 - 2.0 * (zz + yy + xx)
    for shift, (name_xx, name_zx, name_yx) in ((-1, (C_XXR, C_ZXR, C_YXR)), (1, (C_XXL, C_ZXL, C_YXL))):
        wide = spread((2, 4, 5), shift)
        store(name_xx, wide, 0, None)
        store(name_zx, wide, 1, turn)
        store(name_yx, wide, 2, 0.5)


def fine_coeffs(info, cond, strip):
    rows, width = cond.shape[-2:]
    vmem = pl.BlockSpec(memory_space=pltpu.VMEM)
    return pl.pallas_call(
        coeff_kernel,
        in_specs=[pl.BlockSpec(memory_space=pltpu.SMEM), vmem, vmem],
        out_shape=jax.ShapeDtypeStruct((10, rows // 2 + 1, 8, 4 * width), jnp.float32),
        compiler_params=params(),
        cost_estimate=cost(2_000_000, 3_200_000),
        name="coeffs",
    )(info, cond, strip)


SENT, FIELD = 17, 4


def packed_strip(strip, side):
    half = strip.shape[-1] // 2
    low, high = strip[:, :half], strip[:, half:]
    sub = lax.broadcasted_iota(jnp.int32, low.shape, 0)
    first = jnp.where(side == 0, low, pltpu.roll(low, 4, 0))
    second = jnp.where(side == 0, pltpu.roll(high, 4, 0), high)
    return jnp.where(sub < 4, first, second)


def store_sent(ref, tile, tiles, value, side):
    half = value.shape[-1] // 2
    if tile < tiles - 1:
        ref[tile] = value[:, :half]
        ref[tiles - 1 + tile] = value[:, half:]
    else:
        ref[2 * tile] = packed_strip(value, side)


def load_sent(ref, tile, tiles, side):
    if tile < tiles - 1:
        return jnp.concatenate([ref[tile], ref[tiles - 1 + tile]], axis=1)
    packed = ref[2 * tile]
    turned = pltpu.roll(packed, 4, 0)
    return jnp.concatenate([jnp.where(side == 0, packed, turned), jnp.where(side == 0, turned, packed)], axis=1)


SMEM = pl.BlockSpec(memory_space=pltpu.SMEM)
VMEM = pl.BlockSpec(memory_space=pltpu.VMEM)


def shape_of(*shape):
    return jax.ShapeDtypeStruct(shape, jnp.float32)


def edges_kernel(info_ref, u_ref, edge_ref):
    flip, side = info_ref[FLIP], info_ref[SIDE]
    planes, own = u_ref.shape[:2]
    edge = (1 - side) * (own - 1)
    edge_ref[0] = u_ref[flip * (planes - 1), edge]
    edge_ref[1] = u_ref[(1 - flip) * (planes - 1), edge]


def facing_kernel(info_ref, states_ref, cond_ref, facing_ref, cond_rows):
    side = info_ref[SIDE]
    comps, planes, own = states_ref.shape[:3]
    edge = (1 - side) * (own - 1)
    for comp in range(comps):
        for plane in range(planes):
            facing_ref[comp, plane] = states_ref[comp, plane, edge]
    first = pl.multiple_of(8 * (1 - side), 8)
    for comp in range(cond_ref.shape[0]):
        cond_rows[comp] = cond_ref[comp, 0, pl.ds(first, 8), :]


def edge_rows(info, u):
    return pl.pallas_call(
        edges_kernel,
        in_specs=[SMEM, VMEM],
        out_specs=VMEM,
        out_shape=shape_of(2, 8, u.shape[-1]),
        compiler_params=params(),
        cost_estimate=cost(0, 130_000),
        name="edges",
    )(info, u)


def field_kernel(disp_ref, fiber_ref, field_ref):
    for comp in range(3):
        field_ref[comp] = jnp.concatenate([disp_ref[comp, 0, :8], disp_ref[comp, 0, 8:]], axis=1)
    index = fiber_ref[0].astype(jnp.float32)
    field_ref[3] = jnp.concatenate([index[:8], index[8:]], axis=1)


def own_field(disp, fiber):
    return pl.pallas_call(
        field_kernel,
        in_specs=[VMEM] * 2,
        out_specs=VMEM,
        out_shape=shape_of(FIELD, 8, 2 * disp.shape[-1]),
        compiler_params=params(),
        cost_estimate=cost(0, 130_000),
        name="own_field",
    )(disp, fiber)


def sends_kernel(info_ref, edge_ref, u_ref, far_ref, near_ref):
    flip, side = info_ref[FLIP], info_ref[SIDE]
    planes, own = u_ref.shape[:2]
    for pos, (ref, plane) in enumerate([(far_ref, flip * (planes - 1)), (near_ref, (1 - flip) * (planes - 1))]):
        for tile in range(own):
            store_sent(ref, tile, own + 1, u_ref[plane, tile], side)
        store_sent(ref, own, own + 1, edge_ref[pos], side)


def facing_parts(info, tiled, cond):
    comps, planes, _, _, width = tiled.shape
    return pl.pallas_call(
        facing_kernel,
        in_specs=[SMEM, VMEM, VMEM],
        out_specs=[VMEM] * 2,
        out_shape=[
            shape_of(comps, planes, 8, width),
            shape_of(cond.shape[0], 8, cond.shape[-1]),
        ],
        compiler_params=params(),
        cost_estimate=cost(0, 1_200_000),
        name="facing_parts",
    )(info, tiled, cond)


def first_sends(info, edges, u):
    width = u.shape[-1]
    return pl.pallas_call(
        sends_kernel,
        in_specs=[SMEM] + [VMEM] * 2,
        out_specs=[VMEM] * 2,
        out_shape=[shape_of(SENT, 8, width // 2)] * 2,
        compiler_params=params(),
        cost_estimate=cost(0, 1_200_000),
        name="sends",
    )(info, edges, u)


def fraction(val):
    return pl.reciprocal(val, approx=True)


def ionic(u, v, w, s):
    dt = STEP_TIME
    steep = 50.0 * u
    t_v = jnp.tanh(steep - 15.0)
    t_w = jnp.tanh(steep - 6.5)
    t_o = jnp.tanh(steep - 0.3)
    t_m = jnp.tanh(65.0 * u - 65.0 * 0.03)
    t_f = jnp.tanh(2.0458 * u - 2.0458 * 0.65)
    t_s = jnp.tanh(2.0994 * u - 2.0994 * 0.9087)
    hv, nv = 1.0 + t_v, 1.0 - t_v
    hw, nw = 1.0 + t_w, 1.0 - t_w
    no = 0.5 - 0.5 * t_o
    half_so = 0.5 * (30.0181 - 0.9957)
    r_vm = fraction(2.0 / dt * 605.0 + (2.0 / dt * 545.0) * t_o)
    r_wm = fraction(2.0 / dt * 37.5 - (2.0 / dt * 22.5) * t_m)
    r_so = fraction(2.0 / dt * (30.0181 - half_so) - (2.0 / dt * half_so) * t_f)
    r_s = fraction(9.3671 / dt + (6.6329 / dt) * t_w)
    r_o = fraction(2.0 / dt * 203.0 - (2.0 / dt * 197.0) * t_o)
    w_inf = 0.94 + no * (0.06 - u * (1.0 / 0.07))
    hvv = hv * v
    hww = hw * w
    fast = hvv * ((u - 0.3) * (0.5 * dt / 0.11 * 1.55 - (0.5 * dt / 0.11) * u))
    out = (u * nw) * r_o + hw * r_so
    slow = hww * (s * (0.5 * dt / 1.8875))
    v_new = v + (nv * (no - v)) * r_vm - hvv * (0.5 * dt / 1.4506)
    w_new = w + (nw * (w_inf - w)) * r_wm - hww * (0.5 * dt / 200.0)
    s_new = s + ((0.5 + 0.5 * t_s) - s) * r_s
    return fast + slow - out, v_new, w_new, s_new


FAR_HALF, NEAR_HALF = -1, 1


def half_place(info_ref, half):
    flip = info_ref[FLIP]
    return (flip, flip) if half == FAR_HALF else (1 - flip, 1 - flip)


def half_kernel(kind, half, tiles, info_ref, *refs):
    side = info_ref[SIDE]
    sub = row_iota()
    own = tiles - 1
    index, outer = half_place(info_ref, half)
    if kind == "first":
        whole_ref, coeff_ref, outer_out, inner_out, gate_out = refs
        spots = [2 * index + outer, 2 * index + 1 - outer, 2 - index]
        reads = [lambda t, z=z: whole_ref[0, z, t] for z in spots]
    else:
        *u_refs, gate_ref, coeff_ref, outer_out, inner_out, gate_out = refs
        reads = [lambda t, ref=ref: ref[t] for ref in u_refs]

    def diffused(tile):
        before, after = ring_neighbours(tile, tiles)
        mask_before, mask_after = edge_masks(tile, side, own)
        cur = [read(tile) for read in reads]
        prv = [read(before) * mask_before for read in reads]
        nxt = [read(after) * mask_after for read in reads]

        def coeff(index):
            return coeff_ref[index, tile]

        bases = []
        for plane in range(2):
            u = cur[plane]
            if plane == 0:
                around = cur[1]
                wide, wide_nxt, wide_prv = cur[1], nxt[1], prv[1]
            else:
                around = cur[0] + cur[2]
                wide, wide_nxt, wide_prv = cur[2] - cur[0], nxt[2] - nxt[0], prv[2] - prv[0]
            u_next = next_row(u, nxt[plane], sub)
            u_prev = prev_row(u, prv[plane], sub)
            tilt = coeff(C_ZY) * (next_row(wide, wide_nxt, sub) - prev_row(wide, wide_prv, sub))
            tall = u_next - u_prev
            to_left = coeff(C_XXR) * u + coeff(C_YXR) * tall
            to_right = coeff(C_XXL) * u - coeff(C_YXL) * tall
            if half == FAR_HALF:
                to_left += coeff(C_ZXR) * wide
                to_right -= coeff(C_ZXL) * wide
            else:
                to_left -= coeff(C_ZXR) * wide
                to_right += coeff(C_ZXL) * wide
            base = coeff(C_MID) * u + coeff(C_ZZ) * around + coeff(C_YY) * (u_next + u_prev)
            base = base + tilt if half == FAR_HALF else base - tilt
            bases.append(base + left(to_left) + right(to_right))
        return bases

    def react(tile, bases):
        chunk = 256
        for plane in range(2):
            for start in range(0, 1024, chunk):
                lanes = slice(start, start + chunk)
                if kind == "first":
                    u = whole_ref[0, spots[plane], tile, :, lanes]
                    gates = [whole_ref[1 + g, spots[plane], tile, :, lanes] for g in range(3)]
                else:
                    u = u_refs[plane][tile, :, lanes]
                    gates = [gate_ref[g, plane, tile, :, lanes] for g in range(3)]
                u_add, *gates = ionic(u, *gates)
                (outer_out, inner_out)[plane][tile, :, lanes] = bases[plane][:, lanes] + u_add
                for comp, value in enumerate(gates):
                    gate_out[comp, plane, tile, :, lanes] = value

    together = 2 if kind == "last" else 3

    def some(step, carry):
        numbers = [step * together + pos for pos in range(together)]
        held = [diffused(tile) for tile in numbers]
        for tile, bases in zip(numbers, held):
            react(tile, bases)
        return carry

    lax.fori_loop(0, (own if kind == "last" else tiles) // together, some, 0)


def half_step(kind, half, info, arrays, coeffs):
    _, tiles, _, width = coeffs.shape
    vmem = pl.BlockSpec(memory_space=pltpu.VMEM)
    kept = tiles - 1 if kind == "last" else tiles
    plane = jax.ShapeDtypeStruct((kept, 8, width), jnp.float32)
    cells = 2 * tiles * 8 * width
    return pl.pallas_call(
        functools.partial(half_kernel, kind, half, tiles),
        in_specs=[pl.BlockSpec(memory_space=pltpu.SMEM)] + [vmem] * (len(arrays) + 1),
        out_specs=[vmem] * 3,
        out_shape=[plane, plane, jax.ShapeDtypeStruct((3, 2, kept, 8, width), jnp.float32)],
        compiler_params=params(),
        cost_estimate=cost(100 * cells, 40 * cells, 11 * cells),
        name=kind + ("_far" if half == FAR_HALF else "_near"),
    )(info, *arrays, coeffs)


def halo_terms(halo_ref, coeff_ref, tile, tiles, side, sub, half):
    before, after = (tile - 1) % tiles, (tile + 1) % tiles
    cur, prv, nxt = (load_sent(halo_ref, at, tiles, side) for at in (tile, before, after))
    if tile == 0:
        prv = prv * jnp.where(side == 0, 0.0, 1.0)
    if tile == tiles - 2:
        nxt = nxt * jnp.where(side == 1, 0.0, 1.0)
    cross = coeff_ref[C_ZY, tile] * (next_row(cur, nxt, sub) - prev_row(cur, prv, sub))
    cross += left(coeff_ref[C_ZXR, tile] * cur) - right(coeff_ref[C_ZXL, tile] * cur)
    total = coeff_ref[C_ZZ, tile] * cur
    return total - cross if half == FAR_HALF else total + cross


def add_halo(half, tiles, kept, info_ref, outer_ref, halo_ref, coeff_ref, out_ref, sent_ref=None):
    side = info_ref[SIDE]
    sub = row_iota()

    def fill(beyond=True):
        for tile in range(kept):
            value = outer_ref[tile]
            if beyond:
                value += halo_terms(halo_ref, coeff_ref, tile, tiles, side, sub, half)
            out_ref[tile] = value
            if sent_ref is not None:
                store_sent(sent_ref, tile, tiles, value, side)

    if half == NEAR_HALF:
        fill()
    else:
        exists = info_ref[FAR] == 1
        pl.when(exists)(fill)
        pl.when(jnp.logical_not(exists))(functools.partial(fill, False))


def halo_kernel(half, tiles, info_ref, outer_ref, halo_ref, coeff_ref, out_ref, sent_ref):
    add_halo(half, tiles, tiles, info_ref, outer_ref, halo_ref, coeff_ref, out_ref, sent_ref)


def halo_step(half, info, outer, halo, coeffs):
    tiles, _, width = outer.shape
    cells = tiles * 8 * width
    return pl.pallas_call(
        functools.partial(halo_kernel, half, tiles),
        in_specs=[SMEM] + [VMEM] * 3,
        out_specs=[VMEM] * 2,
        out_shape=[shape_of(*outer.shape), shape_of(SENT, 8, width // 2)],
        compiler_params=params(),
        cost_estimate=cost(15 * cells, 20 * cells),
        name="halo" + ("_far" if half == FAR_HALF else "_near"),
    )(info, outer, halo, coeffs)


def pooled(field, rows_ref):
    rows, lanes = field.shape
    fine = lax.broadcasted_iota(jnp.int32, (256, 128), 0)
    coarse = lax.broadcasted_iota(jnp.int32, (256, 128), 1)
    pick = jnp.where((fine >> 1) == coarse, 0.25, 0.0).astype(jnp.bfloat16)
    few = []
    for chunk in range(lanes // 128):
        rows_ref[chunk, :rows] = field[:, 128 * chunk : 128 * chunk + 128]
        even = rows_ref[chunk, pl.ds(0, rows // 2, stride=2), :]
        few.append(even + rows_ref[chunk, pl.ds(1, rows // 2, stride=2), :])
    pairs = [jnp.concatenate(few[pos : pos + 2], axis=1) for pos in range(0, len(few), 2)]
    total = split_dot(jnp.concatenate(pairs, axis=0), pick)
    count = rows // 2
    return jnp.concatenate([total[pos * count : (pos + 1) * count] for pos in range(len(pairs))], axis=1)


def finish_kernel(half, tiles, info_ref, outer_ref, inner_ref, halo_ref, coeff_ref, tension_ref, *refs):
    if half == FAR_HALF:
        gate_ref, near_inner_ref, near_gate_ref, *refs = refs
        states_out, tension_out, active_out, u_ref, layer_ref, rows_ref, sems = refs
        moves = []
        for which, inners, gates in ((FAR_HALF, inner_ref, gate_ref), (NEAR_HALF, near_inner_ref, near_gate_ref)):
            index, outer = half_place(info_ref, which)
            place = [2 * index + outer, 2 * index + 1 - outer]
            moves += [(gates.at[g, plane], states_out.at[1 + g, place[plane]]) for g in range(3) for plane in range(2)]
            moves.append((inners, states_out.at[0, place[1]]))
    else:
        active_ref, _, _, states_out, tension_out, active_out, facing_out, u_ref, layer_ref, rows_ref, sems = refs
        moves = []
    copies = []

    def start(src, dst):
        copies.append(pltpu.make_async_copy(src, dst, sems.at[len(copies)]))
        copies[-1].start()

    for src, dst in moves:
        start(src, dst)
    index, outer = half_place(info_ref, half)
    own = tiles - 1
    add_halo(half, tiles, own, info_ref, outer_ref, halo_ref, coeff_ref, u_ref)
    start(u_ref, states_out.at[0, 2 * index + outer])
    both = 0.5 * (u_ref[...] + inner_ref[...])
    mean = pooled(both.reshape(own * 8, both.shape[-1]), rows_ref)
    old = tension_ref[index]
    new = old + 0.5 * (mean - old)
    layer_ref[...] = new
    start(layer_ref, tension_out.at[index])
    mean = pooled(0.5 * new, rows_ref)
    if half == FAR_HALF:
        active_out[...] = mean
    else:
        active_out[...] = active_ref[...] + mean
        facing_out[...] = active_out[pl.ds(pl.multiple_of(8 * (1 - info_ref[SIDE]), 8), 8), :]
    for copy in copies:
        copy.wait()


def finish_half(half, info, outer, inner, halo, coeffs, tension, others):
    _, tiles, _, width = coeffs.shape
    own = tiles - 1
    active_shape = (own * 2, width // 4)
    hbm = pl.BlockSpec(memory_space=pltpu.HBM)
    out_specs = [hbm, hbm, VMEM]
    out_shape = [shape_of(4, 4, own, 8, width), shape_of(*tension.shape), shape_of(*active_shape)]
    aliases = {}
    if half == FAR_HALF:
        in_specs = [SMEM] + [VMEM] * 8
    else:
        in_specs = [SMEM] + [VMEM] * 6 + [hbm, hbm]
        aliases = {7: 0, 8: 1}
        out_specs.append(VMEM)
        out_shape.append(shape_of(8, width // 4))
    cells = 2 * own * 8 * width
    return pl.pallas_call(
        functools.partial(finish_kernel, half, tiles),
        in_specs=in_specs,
        out_specs=out_specs,
        out_shape=out_shape,
        scratch_shapes=[
            pltpu.VMEM((own, 8, width), jnp.float32),
            pltpu.VMEM(tension.shape[1:], jnp.float32),
            pltpu.VMEM((width // 128, own * 8, 128), jnp.float32),
            pltpu.SemaphoreType.DMA((16 if half == FAR_HALF else 2,)),
        ],
        input_output_aliases=aliases,
        compiler_params=params(),
        cost_estimate=cost(20 * cells, 20 * cells),
        name="finish" + ("_far" if half == FAR_HALF else "_near"),
    )(info, outer, inner, halo, coeffs, tension, *others)


REACH = 4
ROWS = 24


class Weights:
    def __init__(self, side, own, width):
        row = lax.broadcasted_iota(jnp.int32, (ROWS, width), 0)
        lane = lax.broadcasted_iota(jnp.int32, (ROWS, width), 1)
        self.next_y = jnp.where((row == own - 1) & (side == 1), 0.0, 1.0)
        self.prev_y = jnp.where((row == 0) & (side == 0), 0.0, 1.0)
        self.next_x = jnp.where(lane == width - 1, 0.0, 1.0)
        self.prev_x = jnp.where(lane == 0, 0.0, 1.0)


def up_y(val):
    return pltpu.roll(val, ROWS - 1, 0)


def down_y(val):
    return pltpu.roll(val, 1, 0)


def slope_z(below, mid, above):
    return 0.5 * (above - below)


def smooth_z(below, mid, above):
    return 0.75 * mid + 0.125 * (above + below)


def gradients(below, mid, above, k):
    slope = slope_z(below, mid, above)
    smooth = smooth_z(below, mid, above)
    slope_s = 0.75 * slope + 0.125 * (up_y(slope) * k.next_y + down_y(slope) * k.prev_y)
    ahead = up_y(smooth) * k.next_y
    behind = down_y(smooth) * k.prev_y
    smooth_s = 0.75 * smooth + 0.125 * (ahead + behind)
    smooth_d = 0.5 * (ahead - behind)

    def smooth_x(val):
        return 0.75 * val + 0.125 * (left(val) * k.next_x + right(val) * k.prev_x)

    return (
        smooth_x(slope_s),
        smooth_x(smooth_d),
        0.5 * (left(smooth_s) * k.next_x - right(smooth_s) * k.prev_x),
    )


def force(below, mid, above, k):
    p_z = slope_z(below[0], mid[0], above[0])
    p_y = smooth_z(below[1], mid[1], above[1])
    p_x = smooth_z(below[2], mid[2], above[2])
    small, half = 0.125 * p_z, 0.5 * p_y
    both = 0.75 * p_z + up_y(small + half) * k.next_y + down_y(small - half) * k.prev_y
    p_x = 0.75 * p_x + 0.125 * (up_y(p_x) * k.next_y + down_y(p_x) * k.prev_y)
    small, half = 0.125 * both, 0.5 * p_x
    return 0.75 * both + left(small + half) * k.next_x + right(small - half) * k.prev_x


def deformation(below, mid, above, k):
    deform = []
    for comp in range(3):
        row = list(gradients(below[comp], mid[comp], above[comp], k))
        row[comp] = row[comp] + 1.0
        deform.append(row)
    return deform


def passive_stress(deform):
    right_c = {}
    for a_pos, b_pos in PAIRS:
        right_c[a_pos, b_pos] = sum(deform[i_pos][a_pos] * deform[i_pos][b_pos] for i_pos in range(3))
    strain = {}
    for a_pos, b_pos in PAIRS:
        strain[a_pos, b_pos] = 0.5 * (right_c[a_pos, b_pos] - (1.0 if a_pos == b_pos else 0.0))
    trace = strain[0, 0] + strain[1, 1] + strain[2, 2]
    second = {}
    for a_pos, b_pos in PAIRS:
        entry = (2.0 * SHEAR) * strain[a_pos, b_pos]
        if a_pos == b_pos:
            entry = entry + LAME_FIRST * trace
        second[a_pos, b_pos] = entry
        second[b_pos, a_pos] = entry
    return second


def times(deform, second):
    return [
        [sum(deform[i_pos][b_pos] * second[b_pos, a_pos] for b_pos in range(3)) for a_pos in range(3)]
        for i_pos in range(3)
    ]


def metric(deform, fdir):
    def cofactor(i_pos, j_pos):
        i_next, i_last = (i_pos + 1) % 3, (i_pos + 2) % 3
        j_next, j_last = (j_pos + 1) % 3, (j_pos + 2) % 3
        return deform[i_next][j_next] * deform[i_last][j_last] - deform[i_next][j_last] * deform[i_last][j_next]

    cof = [[cofactor(i_pos, j_pos) for j_pos in range(3)] for i_pos in range(3)]
    det = deform[0][0] * cof[0][0] + deform[0][1] * cof[0][1] + deform[0][2] * cof[0][2]
    scale = 1.0 / det
    inv = [[cof[i_pos][j_pos] * scale for i_pos in range(3)] for j_pos in range(3)]
    along = [sum(inv[a_pos][i_pos] * fdir[i_pos] for i_pos in range(3)) for a_pos in range(3)]
    comps = []
    for a_pos, b_pos in PAIRS:
        inner = sum(inv[a_pos][i_pos] * inv[b_pos][i_pos] for i_pos in range(3))
        comps.append(SIGMA_TRANS * inner + (SIGMA_LONG - SIGMA_TRANS) * along[a_pos] * along[b_pos])
    return comps


def inside(slab, slabs, offset):
    spot = slab + offset
    return jnp.where((spot >= 0) & (spot < slabs), 1.0, 0.0)


class Planes:
    def __init__(self, field, slabs, reach, order):
        self.slabs, self.reach, self.order = slabs, reach, order
        self.parts = [field[None]]
        self.doubling = slabs == 8
        self.rounds = 0

    def round(self):
        if self.doubling:
            held = jnp.concatenate(self.parts, axis=0) if len(self.parts) > 1 else self.parts[0]
            perm = [(i, i ^ self.order[self.rounds]) for i in range(self.slabs)]
            self.take(lax.ppermute(held, "slab", perm))
        elif self.rounds == 0:
            for shift in self.shifts()[1:]:
                perm = [((i + shift) % self.slabs, i) for i in range(self.slabs)]
                self.take(lax.ppermute(self.parts[0], "slab", perm))

    def take(self, part):
        self.parts.append(part)
        self.rounds += 1

    def shifts(self):
        return sorted({offset % self.slabs for offset in range(-self.reach, self.reach + 1)})

    def spot(self, slab, offset):
        if self.doubling:
            apart = slab ^ jnp.clip(slab + offset, 0, self.slabs - 1)
            bits = [(apart & step) // step for step in self.order]
            return bits[0] + 2 * bits[1] + 4 * bits[2]
        return self.shifts().index(offset % self.slabs)


def fiber_table():
    index = jnp.arange(128, dtype=jnp.float32)
    theta = -1.0 + 2.0 * index / (NFIB - 1)
    tilt = 0.3 * jnp.sin(3.0 * index)
    return jnp.stack([jnp.sin(tilt), jnp.cos(tilt) * jnp.sin(theta), jnp.cos(tilt) * jnp.cos(theta)])


def facing_fields_kernel(info_ref, *refs):
    out_ref = refs[-1]
    upper_side = info_ref[SIDE] == 0
    at = 0
    for ref in refs[:-1]:
        for pos in range(ref.shape[0]):
            for comp in range(ref.shape[1]):
                both = ref[pos, comp]
                half = both.shape[-1] // 2
                out_ref[at, comp] = jnp.where(upper_side, both[:, half:], both[:, :half])
            at += 1


def facing_rows(info, fields):
    _, comps, _, width = fields[0].shape
    count = sum(field.shape[0] for field in fields)
    vmem = pl.BlockSpec(memory_space=pltpu.VMEM)
    return pl.pallas_call(
        facing_fields_kernel,
        in_specs=[pl.BlockSpec(memory_space=pltpu.SMEM)] + [vmem] * len(fields),
        out_shape=shape_of(count, comps, 8, width // 2),
        compiler_params=params(),
        cost_estimate=cost(0, 600_000),
        name="facing",
    )(info, *fields)


def passive_kernel(planes, info_ref, table_ref, strip_ref, *refs):
    own_refs, (disp_out, stress_out, pull_out, disp_all, field) = refs[:-5], refs[-5:]
    slab, slabs = info_ref[SLAB], planes.slabs
    width = strip_ref.shape[-1]
    own = ROWS - 8
    k = Weights(info_ref[SIDE], own, width)
    reach = REACH + 1

    at = 0
    for ref in own_refs:
        for pos in range(ref.shape[0]):
            for comp in range(ref.shape[1]):
                both = ref[pos, comp]
                field[at, comp] = jnp.concatenate([both[:, :width], both[:, width:], strip_ref[at, comp]], axis=0)
            at += 1

    def plane(comp, offset):
        return field[planes.spot(slab, offset), comp]

    for offset in range(-reach, reach + 1):
        factor = inside(slab, slabs, offset)
        for comp in range(3):
            disp_all[comp, offset + reach] = plane(comp, offset) * factor

    tables = [jnp.broadcast_to(table_ref[comp : comp + 1], (8, 128)) for comp in range(3)]

    def direction(index, comp):
        index = index.astype(jnp.int32)
        rows = []
        for top in range(0, ROWS, 8):
            parts = [
                jnp.take_along_axis(tables[comp], index[top : top + 8, at : at + 128], axis=1, mode="promise_in_bounds")
                for at in range(0, width, 128)
            ]
            rows.append(jnp.concatenate(parts, axis=1))
        return jnp.concatenate(rows, axis=0)

    for step in range(2 * REACH + 1):
        offset = step - REACH
        below, mid, above = ([disp_all[comp, step + shift] for comp in range(3)] for shift in range(3))
        factor = inside(slab, slabs, offset)
        deform = deformation(below, mid, above, k)
        stress = times(deform, passive_stress(deform))
        index = plane(3, offset)
        fdir = [direction(index, comp) for comp in range(3)]
        for i_pos in range(3):
            pull = (ACTIVE_GAIN * factor) * sum(deform[i_pos][b_pos] * fdir[b_pos] for b_pos in range(3))
            for a_pos in range(3):
                stress_out[3 * i_pos + a_pos, step] = stress[i_pos][a_pos] * factor
                pull_out[3 * i_pos + a_pos, step] = pull * fdir[a_pos]
            disp_out[i_pos, step] = mid[i_pos]
            disp_out[3 + i_pos, step] = fdir[i_pos]


def passive_step(info, planes, strips):
    width = strips.shape[-1]
    count = 2 * REACH + 1
    shapes = [(6, count), (9, count), (9, count)]
    vmem = pl.BlockSpec(memory_space=pltpu.VMEM)
    return pl.pallas_call(
        functools.partial(passive_kernel, planes),
        in_specs=[pl.BlockSpec(memory_space=pltpu.SMEM)] + [vmem] * (2 + len(planes.parts)),
        out_shape=[jax.ShapeDtypeStruct((a, b, ROWS, width), jnp.float32) for a, b in shapes],
        scratch_shapes=[
            pltpu.VMEM((3, count + 2, ROWS, width), jnp.float32),
            pltpu.VMEM(strips.shape[:2] + (ROWS, width), jnp.float32),
        ],
        compiler_params=params(),
        cost_estimate=cost(400 * count * ROWS * width, 5_000_000),
        name="passive",
    )(info, fiber_table(), strips, *planes.parts)


def mechanics_kernel(planes, info_ref, disp_ref, stress_ref, pull_ref, *rest):
    active_refs, (disp_out, cond_out, d_one, p_two, active) = rest[:-5], rest[-5:]
    slab, side, slabs = info_ref[SLAB], info_ref[SIDE], planes.slabs
    own, width = disp_out.shape[-2:]
    k = Weights(side, own, width)

    at = 0
    for ref in active_refs:
        active[at : at + ref.shape[0]] = ref[...]
        at += ref.shape[0]

    def active_at(step):
        return active[planes.spot(slab, step - REACH)]

    for step in range(1, 2 * REACH):
        act = [active_at(step + shift) for shift in (-1, 0, 1)]
        factor = inside(slab, slabs, step - REACH)
        for i_pos in range(3):
            stress = [
                [stress_ref[3 * i_pos + a_pos, step + shift] + act[shift + 1] * pull_ref[3 * i_pos + a_pos, step + shift] for a_pos in range(3)]
                for shift in (-1, 0, 1)
            ]
            moved = disp_ref[i_pos, step] + MECH_RATE * force(stress[0], stress[1], stress[2], k)
            d_one[i_pos, step] = moved * factor

    for step in range(2, 2 * REACH - 1):
        disp = [[d_one[comp, step + shift] for comp in range(3)] for shift in (-1, 0, 1)]
        deform = deformation(disp[0], disp[1], disp[2], k)
        second = passive_stress(deform)
        fdir = [disp_ref[3 + comp, step] for comp in range(3)]
        gain = ACTIVE_GAIN * active_at(step)
        for a_pos, b_pos in PAIRS:
            entry = second[a_pos, b_pos] + gain * fdir[a_pos] * fdir[b_pos]
            second[a_pos, b_pos] = entry
            second[b_pos, a_pos] = entry
        stress = times(deform, second)
        factor = inside(slab, slabs, step - REACH)
        for i_pos in range(3):
            for a_pos in range(3):
                p_two[3 * i_pos + a_pos, step] = stress[i_pos][a_pos] * factor

    last = []
    for step in (REACH - 1, REACH, REACH + 1):
        factor = inside(slab, slabs, step - REACH)
        row = []
        for i_pos in range(3):
            stress = [[p_two[3 * i_pos + a_pos, step + shift] for a_pos in range(3)] for shift in (-1, 0, 1)]
            moved = d_one[i_pos, step] + MECH_RATE * force(stress[0], stress[1], stress[2], k)
            row.append(moved * factor)
        last.append(row)
    deform = deformation(last[0], last[1], last[2], k)
    comps = metric(deform, [disp_ref[3 + comp, REACH] for comp in range(3)])
    for i_pos in range(3):
        disp_out[i_pos, 0] = last[1][i_pos][:own]
    for pos, comp in enumerate(comps):
        cond_out[pos, 0] = comp[:own]


def mechanics_step(info, own, planes, window):
    width = planes.parts[0].shape[-1]
    count = 2 * REACH + 1
    held = sum(part.shape[0] for part in planes.parts)
    vmem = pl.BlockSpec(memory_space=pltpu.VMEM)
    return pl.pallas_call(
        functools.partial(mechanics_kernel, planes),
        in_specs=[pl.BlockSpec(memory_space=pltpu.SMEM)] + [vmem] * (3 + len(planes.parts)),
        out_shape=[
            jax.ShapeDtypeStruct((3, 1, own, width), jnp.float32),
            jax.ShapeDtypeStruct((6, 1, own, width), jnp.float32),
        ],
        scratch_shapes=[
            pltpu.VMEM((3, count, ROWS, width), jnp.float32),
            pltpu.VMEM((9, count, ROWS, width), jnp.float32),
            pltpu.VMEM((held, ROWS, width), jnp.float32),
        ],
        compiler_params=params(),
        cost_estimate=cost(400 * count * ROWS * width, 5_000_000),
        name="mechanics",
    )(info, *window, *planes.parts)


def tie(*arrays):
    return lax.optimization_barrier(arrays)


def on_device(states, cond, tension, fiber, disp):
    slabs = lax.axis_size("slab")
    slab, col = lax.axis_index("slab"), lax.axis_index("col")
    _, planes, rows, width = states.shape
    own = rows // 8
    flip = slab % 2
    far_exists = (slab > 0) & (slab < slabs - 1)
    info = jnp.stack([slab, col, flip, far_exists]).astype(jnp.int32)

    pairs = [(i, i ^ 1) for i in range(slabs)]
    others = [(i, i if i in (0, slabs - 1) else ((i + 1) ^ 1) - 1) for i in range(slabs)]
    swap = [(0, 1), (1, 0)]

    tiled = states.reshape(4, planes, own, 8, width)
    fields = Planes(own_field(disp, fiber), slabs, REACH + 1, (1, 4, 2))
    edges = lax.ppermute(edge_rows(info, tiled[0]), "col", swap)
    far, near = first_sends(info, edges, tiled[0])
    late_info, far, near = tie(info, far, near)
    far_halo = lax.ppermute(far, "slab", others)
    near_halo = lax.ppermute(near, "slab", pairs)
    facing, cond_rows = facing_parts(late_info, tiled, cond)
    cond_strip = lax.ppermute(cond_rows, "col", swap)
    strip = lax.ppermute(facing, "col", swap)
    coeffs = fine_coeffs(info, cond, cond_strip)
    whole = jnp.concatenate([tiled, strip[:, :, None]], axis=2)

    far_part, far_inner, far_gates = half_step("first", FAR_HALF, info, (whole,), coeffs)
    near_kind, near_arrays = "first", (whole,)
    for turn_index in range(1, SUB):
        last = turn_index == SUB - 1
        kind = "last" if last else "middle"
        far, far_send = halo_step(FAR_HALF, info, far_part, far_halo, coeffs)
        far_send, *near_arrays = tie(far_send, *near_arrays)
        near_part, near_inner, near_gates = half_step(near_kind, NEAR_HALF, info, near_arrays, coeffs)
        far_halo = lax.ppermute(far_send, "slab", others)
        far_part, far_next, far_gates = half_step(kind, FAR_HALF, info, (far, far_inner, near_inner, far_gates), coeffs)
        if last:
            near_part, far_part, *fields.parts = tie(near_part, far_part, *fields.parts)
        near, near_send = halo_step(NEAR_HALF, info, near_part, near_halo, coeffs)
        near_halo = lax.ppermute(near_send, "slab", pairs)
        fields.round()
        near_kind, near_arrays = kind, (near, near_inner, far_inner, near_gates)
        far_inner = far_next
    near_part, near_inner, near_gates = half_step(near_kind, NEAR_HALF, info, near_arrays, coeffs)
    strips = lax.ppermute(facing_rows(info, fields.parts), "col", swap)
    states_next, tension_next, active = finish_half(
        FAR_HALF, info, far_part, far_inner, far_halo, coeffs, tension, (far_gates, near_inner, near_gates)
    )
    window = passive_step(info, fields, strips)
    states_next, tension_next, active, facing = finish_half(
        NEAR_HALF, info, near_part, near_inner, near_halo, coeffs, tension, (active, states_next, tension_next)
    )
    active_strip = lax.ppermute(facing, "col", swap)
    actives = Planes(jnp.concatenate([active, active_strip], axis=0), slabs, REACH, (4, 1, 2))
    for _ in range(3):
        actives.round()
    disp_next, cond_next = mechanics_step(info, disp.shape[2], actives, window)
    return (states_next.reshape(states.shape), tension_next, disp_next, cond_next)


def solution(mesh):
    in_specs = (
        P(None, ("grp", "slab"), "col", None),
        P(None, ("grp", "slab"), "col", None),
        P(("grp", "slab"), "col", None),
        P(("grp", "slab"), "col", None),
        P(None, ("grp", "slab"), "col", None),
    )
    out_specs = (
        P(None, ("grp", "slab"), "col", None),
        P(("grp", "slab"), "col", None),
        P(None, ("grp", "slab"), "col", None),
        P(None, ("grp", "slab"), "col", None),
    )
    return jax.shard_map(
        on_device, mesh=mesh, in_specs=in_specs, out_specs=out_specs, check_vma=False
    )
```

```python
import functools

import jax
import jax.numpy as jnp
from jax import lax
from jax.experimental import pallas as pl
from jax.experimental.pallas import tpu as pltpu
from jax.sharding import PartitionSpec as P

SUB = 4
MECH_STEPS = 2
NFIB = 64

STEP_TIME = 0.05
LAME_FIRST = 1.0
SHEAR = 0.5
ACTIVE_GAIN = 0.5
MECH_RATE = 0.15
SIGMA_LONG = 0.16
SIGMA_TRANS = 0.04
PAIRS = ((0, 0), (1, 1), (2, 2), (0, 1), (0, 2), (1, 2))

C_ZZ, C_ZY, C_ZXR, C_ZXL, C_MID, C_YY, C_XXR, C_YXR, C_XXL, C_YXL = range(10)

SLAB, SIDE, FLIP, FAR = range(4)

LIMIT = 40 * 1024 * 1024


def params(**kwargs):
    return pltpu.CompilerParams(vmem_limit_bytes=LIMIT, **kwargs)


def cost(flops, nbytes, trans=0):
    return pl.CostEstimate(flops=flops, bytes_accessed=nbytes, transcendentals=trans)


def row_iota():
    return lax.broadcasted_iota(jnp.int32, (8, 1024), 0)


def next_row(cur, nxt, sub):
    return pltpu.roll(jnp.where(sub == 0, nxt, cur), 7, 0)


def prev_row(cur, prv, sub):
    return pltpu.roll(jnp.where(sub == 7, prv, cur), 1, 0)


def left(val):
    return pltpu.roll(val, val.shape[-1] - 1, val.ndim - 1)


def right(val):
    return pltpu.roll(val, 1, val.ndim - 1)


def edge_masks(tile, side, own):
    before = jnp.where((tile == 0) & (side == 0), 0.0, 1.0)
    after = jnp.where((tile == own - 1) & (side == 1), 0.0, 1.0)
    return before, after


def ring_neighbours(tile, tiles):
    before = jnp.where(tile == 0, tiles - 1, tile - 1)
    after = jnp.where(tile == tiles - 1, 0, tile + 1)
    return before, after


def split_dot(rest, pick):
    total = None
    for _ in range(3):
        part = rest.astype(jnp.bfloat16)
        rest = rest - part.astype(jnp.float32)
        product = jnp.dot(part, pick, preferred_element_type=jnp.float32)
        total = product if total is None else total + product
    return total


def coeff_kernel(info_ref, cond_ref, strip_ref, out_ref):
    rows, width = cond_ref.shape[-2:]
    turn = jnp.where(info_ref[FLIP] == 1, -0.5, 0.5)
    upper_side = info_ref[SIDE] == 0
    fine = 4 * width
    apart = lax.broadcasted_iota(jnp.int32, (width, fine), 1) - 4 * lax.broadcasted_iota(jnp.int32, (width, fine), 0)
    own = rows // 2
    sub = lax.broadcasted_iota(jnp.int32, (8, width), 0)

    def tall(val):
        tiles = []
        for row in range(0, val.shape[0], 2):
            first, second = (jnp.broadcast_to(val[at : at + 1], (8, width)) for at in (row, row + 1))
            tiles.append(jnp.where(sub < 4, first, second))
        return tiles

    comps = []
    for comp in range(6):
        strip = tall(strip_ref[comp])
        comps.append(tall(cond_ref[comp, 0]) + [jnp.where(upper_side, strip[0], strip[-1])])

    def spread(names, shift):
        pick = jnp.where((apart >= -shift) & (apart < 4 - shift), 1.0, 0.0).astype(jnp.bfloat16)
        return split_dot(jnp.concatenate([tile for name in names for tile in comps[name]], axis=0), pick)

    def store(index, wide, place, factor):
        for tile in range(own + 1):
            at = 8 * (place * (own + 1) + tile)
            out_ref[index, tile] = wide[at : at + 8] if factor is None else factor * wide[at : at + 8]

    wide = spread((0, 1, 3, 2), 0)
    store(C_ZZ, wide, 0, None)
    store(C_YY, wide, 1, None)
    store(C_ZY, wide, 2, turn)
    for tile in range(own + 1):
        zz, yy, xx = (wide[8 * (place * (own + 1) + tile) :][:8] for place in (0, 1, 3))
        out_ref[C_MID, tile] = 1.0 - 2.0 * (zz + yy + xx)
    for shift, (name_xx, name_zx, name_yx) in ((-1, (C_XXR, C_ZXR, C_YXR)), (1, (C_XXL, C_ZXL, C_YXL))):
        wide = spread((2, 4, 5), shift)
        store(name_xx, wide, 0, None)
        store(name_zx, wide, 1, turn)
        store(name_yx, wide, 2, 0.5)


def fine_coeffs(info, cond, strip):
    rows, width = cond.shape[-2:]
    vmem = pl.BlockSpec(memory_space=pltpu.VMEM)
    return pl.pallas_call(
        coeff_kernel,
        in_specs=[pl.BlockSpec(memory_space=pltpu.SMEM), vmem, vmem],
        out_shape=jax.ShapeDtypeStruct((10, rows // 2 + 1, 8, 4 * width), jnp.float32),
        compiler_params=params(),
        cost_estimate=cost(2_000_000, 3_200_000),
        name="coeffs",
    )(info, cond, strip)


SENT, FIELD = 17, 4


def packed_strip(strip, side):
    half = strip.shape[-1] // 2
    low, high = strip[:, :half], strip[:, half:]
    sub = lax.broadcasted_iota(jnp.int32, low.shape, 0)
    first = jnp.where(side == 0, low, pltpu.roll(low, 4, 0))
    second = jnp.where(side == 0, pltpu.roll(high, 4, 0), high)
    return jnp.where(sub < 4, first, second)


def store_sent(ref, tile, tiles, value, side):
    half = value.shape[-1] // 2
    if tile < tiles - 1:
        ref[tile] = value[:, :half]
        ref[tiles - 1 + tile] = value[:, half:]
    else:
        ref[2 * tile] = packed_strip(value, side)


def load_sent(ref, tile, tiles, side):
    if tile < tiles - 1:
        return jnp.concatenate([ref[tile], ref[tiles - 1 + tile]], axis=1)
    packed = ref[2 * tile]
    turned = pltpu.roll(packed, 4, 0)
    return jnp.concatenate([jnp.where(side == 0, packed, turned), jnp.where(side == 0, turned, packed)], axis=1)


SMEM = pl.BlockSpec(memory_space=pltpu.SMEM)
VMEM = pl.BlockSpec(memory_space=pltpu.VMEM)


def shape_of(*shape):
    return jax.ShapeDtypeStruct(shape, jnp.float32)


def cond_rows_kernel(info_ref, cond_ref, cond_rows):
    first = pl.multiple_of(8 * (1 - info_ref[SIDE]), 8)
    for comp in range(cond_ref.shape[0]):
        cond_rows[comp] = cond_ref[comp, 0, pl.ds(first, 8), :]


def facing_kernel(info_ref, states_ref, edge_ref, facing_ref):
    flip, side = info_ref[FLIP], info_ref[SIDE]
    comps, planes, own = states_ref.shape[:3]
    edge = (1 - side) * (own - 1)
    edge_ref[0] = states_ref[0, flip * (planes - 1), edge]
    edge_ref[1] = states_ref[0, (1 - flip) * (planes - 1), edge]
    for comp in range(comps):
        for plane in range(planes):
            facing_ref[comp, plane] = states_ref[comp, plane, edge]


def field_kernel(disp_ref, fiber_ref, field_ref):
    for comp in range(3):
        field_ref[comp] = jnp.concatenate([disp_ref[comp, 0, :8], disp_ref[comp, 0, 8:]], axis=1)
    index = fiber_ref[0].astype(jnp.float32)
    field_ref[3] = jnp.concatenate([index[:8], index[8:]], axis=1)


def own_field(disp, fiber):
    return pl.pallas_call(
        field_kernel,
        in_specs=[VMEM] * 2,
        out_specs=VMEM,
        out_shape=shape_of(FIELD, 8, 2 * disp.shape[-1]),
        compiler_params=params(),
        cost_estimate=cost(0, 130_000),
        name="own_field",
    )(disp, fiber)


def sends_kernel(info_ref, edge_ref, states_ref, far_ref, near_ref):
    flip, side = info_ref[FLIP], info_ref[SIDE]
    planes, own = states_ref.shape[1:3]
    for pos, (ref, plane) in enumerate([(far_ref, flip * (planes - 1)), (near_ref, (1 - flip) * (planes - 1))]):
        for tile in range(own):
            store_sent(ref, tile, own + 1, states_ref[0, plane, tile], side)
        store_sent(ref, own, own + 1, edge_ref[pos], side)


def facing_parts(info, tiled):
    comps, planes, _, _, width = tiled.shape
    return pl.pallas_call(
        facing_kernel,
        in_specs=[SMEM, VMEM],
        out_specs=[VMEM] * 2,
        out_shape=[shape_of(2, 8, width), shape_of(comps, planes, 8, width)],
        compiler_params=params(),
        cost_estimate=cost(0, 1_200_000),
        name="facing_parts",
    )(info, tiled)


def facing_cond(info, cond):
    return pl.pallas_call(
        cond_rows_kernel,
        in_specs=[SMEM, VMEM],
        out_specs=VMEM,
        out_shape=shape_of(cond.shape[0], 8, cond.shape[-1]),
        compiler_params=params(),
        cost_estimate=cost(0, 100_000),
        name="facing_cond",
    )(info, cond)


def first_sends(info, edges, tiled):
    width = tiled.shape[-1]
    return pl.pallas_call(
        sends_kernel,
        in_specs=[SMEM] + [VMEM] * 2,
        out_specs=[VMEM] * 2,
        out_shape=[shape_of(SENT, 8, width // 2)] * 2,
        compiler_params=params(),
        cost_estimate=cost(0, 1_200_000),
        name="sends",
    )(info, edges, tiled)


def fraction(val):
    return pl.reciprocal(val, approx=True)


def ionic(u, v, w, s):
    dt = STEP_TIME
    steep = 50.0 * u
    t_v = jnp.tanh(steep - 15.0)
    t_w = jnp.tanh(steep - 6.5)
    t_o = jnp.tanh(steep - 0.3)
    t_m = jnp.tanh(65.0 * u - 65.0 * 0.03)
    t_f = jnp.tanh(2.0458 * u - 2.0458 * 0.65)
    t_s = jnp.tanh(2.0994 * u - 2.0994 * 0.9087)
    hv, nv = 1.0 + t_v, 1.0 - t_v
    hw, nw = 1.0 + t_w, 1.0 - t_w
    no = 0.5 - 0.5 * t_o
    half_so = 0.5 * (30.0181 - 0.9957)
    r_vm = fraction(2.0 / dt * 605.0 + (2.0 / dt * 545.0) * t_o)
    r_wm = fraction(2.0 / dt * 37.5 - (2.0 / dt * 22.5) * t_m)
    r_so = fraction(2.0 / dt * (30.0181 - half_so) - (2.0 / dt * half_so) * t_f)
    r_s = fraction(9.3671 / dt + (6.6329 / dt) * t_w)
    r_o = fraction(2.0 / dt * 203.0 - (2.0 / dt * 197.0) * t_o)
    w_inf = 0.94 + no * (0.06 - u * (1.0 / 0.07))
    hvv = hv * v
    hww = hw * w
    fast = hvv * ((u - 0.3) * (0.5 * dt / 0.11 * 1.55 - (0.5 * dt / 0.11) * u))
    out = (u * nw) * r_o + hw * r_so
    slow = hww * (s * (0.5 * dt / 1.8875))
    v_new = v + (nv * (no - v)) * r_vm - hvv * (0.5 * dt / 1.4506)
    w_new = w + (nw * (w_inf - w)) * r_wm - hww * (0.5 * dt / 200.0)
    s_new = s + ((0.5 + 0.5 * t_s) - s) * r_s
    return fast + slow - out, v_new, w_new, s_new


FAR_HALF, NEAR_HALF = -1, 1


def half_place(info_ref, half):
    flip = info_ref[FLIP]
    return (flip, flip) if half == FAR_HALF else (1 - flip, 1 - flip)


def half_kernel(kind, half, tiles, info_ref, *refs):
    side = info_ref[SIDE]
    sub = row_iota()
    own = tiles - 1
    index, outer = half_place(info_ref, half)
    if kind == "first":
        whole_ref, coeff_ref, outer_out, inner_out, gate_out = refs
        spots = [2 * index + outer, 2 * index + 1 - outer, 2 - index]
        reads = [lambda t, z=z: whole_ref[0, z, t] for z in spots]
    else:
        *u_refs, gate_ref, coeff_ref, outer_out, inner_out, gate_out = refs
        reads = [lambda t, ref=ref: ref[t] for ref in u_refs]

    def diffused(tile):
        before, after = ring_neighbours(tile, tiles)
        mask_before, mask_after = edge_masks(tile, side, own)
        cur = [read(tile) for read in reads]
        prv = [read(before) * mask_before for read in reads]
        nxt = [read(after) * mask_after for read in reads]

        def coeff(index):
            return coeff_ref[index, tile]

        bases = []
        for plane in range(2):
            u = cur[plane]
            if plane == 0:
                around = cur[1]
                wide, wide_nxt, wide_prv = cur[1], nxt[1], prv[1]
            else:
                around = cur[0] + cur[2]
                wide, wide_nxt, wide_prv = cur[2] - cur[0], nxt[2] - nxt[0], prv[2] - prv[0]
            u_next = next_row(u, nxt[plane], sub)
            u_prev = prev_row(u, prv[plane], sub)
            tilt = coeff(C_ZY) * (next_row(wide, wide_nxt, sub) - prev_row(wide, wide_prv, sub))
            tall = u_next - u_prev
            to_left = coeff(C_XXR) * u + coeff(C_YXR) * tall
            to_right = coeff(C_XXL) * u - coeff(C_YXL) * tall
            if half == FAR_HALF:
                to_left += coeff(C_ZXR) * wide
                to_right -= coeff(C_ZXL) * wide
            else:
                to_left -= coeff(C_ZXR) * wide
                to_right += coeff(C_ZXL) * wide
            base = coeff(C_MID) * u + coeff(C_ZZ) * around + coeff(C_YY) * (u_next + u_prev)
            base = base + tilt if half == FAR_HALF else base - tilt
            bases.append(base + left(to_left) + right(to_right))
        return bases

    def react(tile, bases):
        chunk = 256
        for plane in range(2):
            for start in range(0, 1024, chunk):
                lanes = slice(start, start + chunk)
                if kind == "first":
                    u = whole_ref[0, spots[plane], tile, :, lanes]
                    gates = [whole_ref[1 + g, spots[plane], tile, :, lanes] for g in range(3)]
                else:
                    u = u_refs[plane][tile, :, lanes]
                    gates = [gate_ref[g, plane, tile, :, lanes] for g in range(3)]
                u_add, *gates = ionic(u, *gates)
                (outer_out, inner_out)[plane][tile, :, lanes] = bases[plane][:, lanes] + u_add
                for comp, value in enumerate(gates):
                    gate_out[comp, plane, tile, :, lanes] = value

    together = 2 if kind == "last" else 3

    def some(step, carry):
        numbers = [step * together + pos for pos in range(together)]
        held = [diffused(tile) for tile in numbers]
        for tile, bases in zip(numbers, held):
            react(tile, bases)
        return carry

    lax.fori_loop(0, (own if kind == "last" else tiles) // together, some, 0)


def half_step(kind, half, info, arrays, coeffs):
    _, tiles, _, width = coeffs.shape
    vmem = pl.BlockSpec(memory_space=pltpu.VMEM)
    kept = tiles - 1 if kind == "last" else tiles
    plane = jax.ShapeDtypeStruct((kept, 8, width), jnp.float32)
    cells = 2 * tiles * 8 * width
    return pl.pallas_call(
        functools.partial(half_kernel, kind, half, tiles),
        in_specs=[pl.BlockSpec(memory_space=pltpu.SMEM)] + [vmem] * (len(arrays) + 1),
        out_specs=[vmem] * 3,
        out_shape=[plane, plane, jax.ShapeDtypeStruct((3, 2, kept, 8, width), jnp.float32)],
        compiler_params=params(),
        cost_estimate=cost(100 * cells, 40 * cells, 11 * cells),
        name=kind + ("_far" if half == FAR_HALF else "_near"),
    )(info, *arrays, coeffs)


def halo_terms(halo_ref, coeff_ref, tile, tiles, side, sub, half):
    before, after = (tile - 1) % tiles, (tile + 1) % tiles
    cur, prv, nxt = (load_sent(halo_ref, at, tiles, side) for at in (tile, before, after))
    if tile == 0:
        prv = prv * jnp.where(side == 0, 0.0, 1.0)
    if tile == tiles - 2:
        nxt = nxt * jnp.where(side == 1, 0.0, 1.0)
    cross = coeff_ref[C_ZY, tile] * (next_row(cur, nxt, sub) - prev_row(cur, prv, sub))
    cross += left(coeff_ref[C_ZXR, tile] * cur) - right(coeff_ref[C_ZXL, tile] * cur)
    total = coeff_ref[C_ZZ, tile] * cur
    return total - cross if half == FAR_HALF else total + cross


def add_halo(half, tiles, kept, info_ref, outer_ref, halo_ref, coeff_ref, out_ref, sent_ref=None):
    side = info_ref[SIDE]
    sub = row_iota()

    def fill(beyond=True):
        for tile in range(kept):
            value = outer_ref[tile]
            if beyond:
                value += halo_terms(halo_ref, coeff_ref, tile, tiles, side, sub, half)
            out_ref[tile] = value
            if sent_ref is not None:
                store_sent(sent_ref, tile, tiles, value, side)

    if half == NEAR_HALF:
        fill()
    else:
        exists = info_ref[FAR] == 1
        pl.when(exists)(fill)
        pl.when(jnp.logical_not(exists))(functools.partial(fill, False))


def halo_kernel(half, tiles, info_ref, outer_ref, halo_ref, coeff_ref, out_ref, sent_ref):
    add_halo(half, tiles, tiles, info_ref, outer_ref, halo_ref, coeff_ref, out_ref, sent_ref)


def halo_step(half, info, outer, halo, coeffs):
    tiles, _, width = outer.shape
    cells = tiles * 8 * width
    return pl.pallas_call(
        functools.partial(halo_kernel, half, tiles),
        in_specs=[SMEM] + [VMEM] * 3,
        out_specs=[VMEM] * 2,
        out_shape=[shape_of(*outer.shape), shape_of(SENT, 8, width // 2)],
        compiler_params=params(),
        cost_estimate=cost(15 * cells, 20 * cells),
        name="halo" + ("_far" if half == FAR_HALF else "_near"),
    )(info, outer, halo, coeffs)


def pooled(field, rows_ref):
    rows, lanes = field.shape
    fine = lax.broadcasted_iota(jnp.int32, (256, 128), 0)
    coarse = lax.broadcasted_iota(jnp.int32, (256, 128), 1)
    pick = jnp.where((fine >> 1) == coarse, 0.25, 0.0).astype(jnp.bfloat16)
    few = []
    for chunk in range(lanes // 128):
        rows_ref[chunk, :rows] = field[:, 128 * chunk : 128 * chunk + 128]
        even = rows_ref[chunk, pl.ds(0, rows // 2, stride=2), :]
        few.append(even + rows_ref[chunk, pl.ds(1, rows // 2, stride=2), :])
    pairs = [jnp.concatenate(few[pos : pos + 2], axis=1) for pos in range(0, len(few), 2)]
    total = split_dot(jnp.concatenate(pairs, axis=0), pick)
    count = rows // 2
    return jnp.concatenate([total[pos * count : (pos + 1) * count] for pos in range(len(pairs))], axis=1)


def finish_kernel(half, tiles, info_ref, outer_ref, inner_ref, halo_ref, coeff_ref, tension_ref, *refs):
    if half == FAR_HALF:
        gate_ref, near_inner_ref, near_gate_ref, *refs = refs
        states_out, tension_out, active_out, u_ref, layer_ref, rows_ref, sems = refs
        moves = []
        for which, inners, gates in ((FAR_HALF, inner_ref, gate_ref), (NEAR_HALF, near_inner_ref, near_gate_ref)):
            index, outer = half_place(info_ref, which)
            place = [2 * index + outer, 2 * index + 1 - outer]
            moves += [(gates.at[g, plane], states_out.at[1 + g, place[plane]]) for g in range(3) for plane in range(2)]
            moves.append((inners, states_out.at[0, place[1]]))
    else:
        active_ref, _, _, states_out, tension_out, active_out, facing_out, u_ref, layer_ref, rows_ref, sems = refs
        moves = []
    copies = []

    def start(src, dst):
        copies.append(pltpu.make_async_copy(src, dst, sems.at[len(copies)]))
        copies[-1].start()

    for src, dst in moves:
        start(src, dst)
    index, outer = half_place(info_ref, half)
    own = tiles - 1
    add_halo(half, tiles, own, info_ref, outer_ref, halo_ref, coeff_ref, u_ref)
    start(u_ref, states_out.at[0, 2 * index + outer])
    both = 0.5 * (u_ref[...] + inner_ref[...])
    mean = pooled(both.reshape(own * 8, both.shape[-1]), rows_ref)
    old = tension_ref[index]
    new = old + 0.5 * (mean - old)
    layer_ref[...] = new
    start(layer_ref, tension_out.at[index])
    mean = pooled(0.5 * new, rows_ref)
    if half == FAR_HALF:
        active_out[...] = mean
    else:
        active_out[...] = active_ref[...] + mean
        facing_out[...] = active_out[pl.ds(pl.multiple_of(8 * (1 - info_ref[SIDE]), 8), 8), :]
    for copy in copies:
        copy.wait()


def finish_half(half, info, outer, inner, halo, coeffs, tension, others):
    _, tiles, _, width = coeffs.shape
    own = tiles - 1
    active_shape = (own * 2, width // 4)
    hbm = pl.BlockSpec(memory_space=pltpu.HBM)
    out_specs = [hbm, hbm, VMEM]
    out_shape = [shape_of(4, 4, own, 8, width), shape_of(*tension.shape), shape_of(*active_shape)]
    aliases = {}
    if half == FAR_HALF:
        in_specs = [SMEM] + [VMEM] * 8
    else:
        in_specs = [SMEM] + [VMEM] * 6 + [hbm, hbm]
        aliases = {7: 0, 8: 1}
        out_specs.append(VMEM)
        out_shape.append(shape_of(8, width // 4))
    cells = 2 * own * 8 * width
    return pl.pallas_call(
        functools.partial(finish_kernel, half, tiles),
        in_specs=in_specs,
        out_specs=out_specs,
        out_shape=out_shape,
        scratch_shapes=[
            pltpu.VMEM((own, 8, width), jnp.float32),
            pltpu.VMEM(tension.shape[1:], jnp.float32),
            pltpu.VMEM((width // 128, own * 8, 128), jnp.float32),
            pltpu.SemaphoreType.DMA((16 if half == FAR_HALF else 2,)),
        ],
        input_output_aliases=aliases,
        compiler_params=params(),
        cost_estimate=cost(20 * cells, 20 * cells),
        name="finish" + ("_far" if half == FAR_HALF else "_near"),
    )(info, outer, inner, halo, coeffs, tension, *others)


REACH = 4
ROWS = 24


class Weights:
    def __init__(self, side, own, width):
        row = lax.broadcasted_iota(jnp.int32, (ROWS, width), 0)
        lane = lax.broadcasted_iota(jnp.int32, (ROWS, width), 1)
        self.next_y = jnp.where((row == own - 1) & (side == 1), 0.0, 1.0)
        self.prev_y = jnp.where((row == 0) & (side == 0), 0.0, 1.0)
        self.next_x = jnp.where(lane == width - 1, 0.0, 1.0)
        self.prev_x = jnp.where(lane == 0, 0.0, 1.0)


def up_y(val):
    return pltpu.roll(val, ROWS - 1, 0)


def down_y(val):
    return pltpu.roll(val, 1, 0)


def slope_z(below, mid, above):
    return 0.5 * (above - below)


def smooth_z(below, mid, above):
    return 0.75 * mid + 0.125 * (above + below)


def gradients(below, mid, above, k):
    slope = slope_z(below, mid, above)
    smooth = smooth_z(below, mid, above)
    slope_s = 0.75 * slope + 0.125 * (up_y(slope) * k.next_y + down_y(slope) * k.prev_y)
    ahead = up_y(smooth) * k.next_y
    behind = down_y(smooth) * k.prev_y
    smooth_s = 0.75 * smooth + 0.125 * (ahead + behind)
    smooth_d = 0.5 * (ahead - behind)

    def smooth_x(val):
        return 0.75 * val + 0.125 * (left(val) * k.next_x + right(val) * k.prev_x)

    return (
        smooth_x(slope_s),
        smooth_x(smooth_d),
        0.5 * (left(smooth_s) * k.next_x - right(smooth_s) * k.prev_x),
    )


def force(below, mid, above, k):
    p_z = slope_z(below[0], mid[0], above[0])
    p_y = smooth_z(below[1], mid[1], above[1])
    p_x = smooth_z(below[2], mid[2], above[2])
    small, half = 0.125 * p_z, 0.5 * p_y
    both = 0.75 * p_z + up_y(small + half) * k.next_y + down_y(small - half) * k.prev_y
    p_x = 0.75 * p_x + 0.125 * (up_y(p_x) * k.next_y + down_y(p_x) * k.prev_y)
    small, half = 0.125 * both, 0.5 * p_x
    return 0.75 * both + left(small + half) * k.next_x + right(small - half) * k.prev_x


def deformation(below, mid, above, k):
    deform = []
    for comp in range(3):
        row = list(gradients(below[comp], mid[comp], above[comp], k))
        row[comp] = row[comp] + 1.0
        deform.append(row)
    return deform


def passive_stress(deform):
    right_c = {}
    for a_pos, b_pos in PAIRS:
        right_c[a_pos, b_pos] = sum(deform[i_pos][a_pos] * deform[i_pos][b_pos] for i_pos in range(3))
    strain = {}
    for a_pos, b_pos in PAIRS:
        strain[a_pos, b_pos] = 0.5 * (right_c[a_pos, b_pos] - (1.0 if a_pos == b_pos else 0.0))
    trace = strain[0, 0] + strain[1, 1] + strain[2, 2]
    second = {}
    for a_pos, b_pos in PAIRS:
        entry = (2.0 * SHEAR) * strain[a_pos, b_pos]
        if a_pos == b_pos:
            entry = entry + LAME_FIRST * trace
        second[a_pos, b_pos] = entry
        second[b_pos, a_pos] = entry
    return second


def times(deform, second):
    return [
        [sum(deform[i_pos][b_pos] * second[b_pos, a_pos] for b_pos in range(3)) for a_pos in range(3)]
        for i_pos in range(3)
    ]


def metric(deform, fdir):
    def cofactor(i_pos, j_pos):
        i_next, i_last = (i_pos + 1) % 3, (i_pos + 2) % 3
        j_next, j_last = (j_pos + 1) % 3, (j_pos + 2) % 3
        return deform[i_next][j_next] * deform[i_last][j_last] - deform[i_next][j_last] * deform[i_last][j_next]

    cof = [[cofactor(i_pos, j_pos) for j_pos in range(3)] for i_pos in range(3)]
    det = deform[0][0] * cof[0][0] + deform[0][1] * cof[0][1] + deform[0][2] * cof[0][2]
    scale = 1.0 / det
    inv = [[cof[i_pos][j_pos] * scale for i_pos in range(3)] for j_pos in range(3)]
    along = [sum(inv[a_pos][i_pos] * fdir[i_pos] for i_pos in range(3)) for a_pos in range(3)]
    comps = []
    for a_pos, b_pos in PAIRS:
        inner = sum(inv[a_pos][i_pos] * inv[b_pos][i_pos] for i_pos in range(3))
        comps.append(SIGMA_TRANS * inner + (SIGMA_LONG - SIGMA_TRANS) * along[a_pos] * along[b_pos])
    return comps


def inside(slab, slabs, offset):
    spot = slab + offset
    return jnp.where((spot >= 0) & (spot < slabs), 1.0, 0.0)


class Planes:
    def __init__(self, field, slabs, reach, order):
        self.slabs, self.reach, self.order = slabs, reach, order
        self.parts = [field[None]]
        self.doubling = slabs == 8
        self.rounds = 0

    def round(self):
        if self.doubling:
            held = jnp.concatenate(self.parts, axis=0) if len(self.parts) > 1 else self.parts[0]
            perm = [(i, i ^ self.order[self.rounds]) for i in range(self.slabs)]
            self.take(lax.ppermute(held, "slab", perm))
        elif self.rounds == 0:
            for shift in self.shifts()[1:]:
                perm = [((i + shift) % self.slabs, i) for i in range(self.slabs)]
                self.take(lax.ppermute(self.parts[0], "slab", perm))

    def take(self, part):
        self.parts.append(part)
        self.rounds += 1

    def shifts(self):
        return sorted({offset % self.slabs for offset in range(-self.reach, self.reach + 1)})

    def spot(self, slab, offset):
        if self.doubling:
            apart = slab ^ jnp.clip(slab + offset, 0, self.slabs - 1)
            bits = [(apart & step) // step for step in self.order]
            return bits[0] + 2 * bits[1] + 4 * bits[2]
        return self.shifts().index(offset % self.slabs)


def fiber_table():
    index = jnp.arange(128, dtype=jnp.float32)
    theta = -1.0 + 2.0 * index / (NFIB - 1)
    tilt = 0.3 * jnp.sin(3.0 * index)
    return jnp.stack([jnp.sin(tilt), jnp.cos(tilt) * jnp.sin(theta), jnp.cos(tilt) * jnp.cos(theta)])


def facing_fields_kernel(info_ref, *refs):
    out_ref = refs[-1]
    upper_side = info_ref[SIDE] == 0
    at = 0
    for ref in refs[:-1]:
        for pos in range(ref.shape[0]):
            for comp in range(ref.shape[1]):
                both = ref[pos, comp]
                half = both.shape[-1] // 2
                out_ref[at, comp] = jnp.where(upper_side, both[:, half:], both[:, :half])
            at += 1


def facing_rows(info, fields):
    _, comps, _, width = fields[0].shape
    count = sum(field.shape[0] for field in fields)
    vmem = pl.BlockSpec(memory_space=pltpu.VMEM)
    return pl.pallas_call(
        facing_fields_kernel,
        in_specs=[pl.BlockSpec(memory_space=pltpu.SMEM)] + [vmem] * len(fields),
        out_shape=shape_of(count, comps, 8, width // 2),
        compiler_params=params(),
        cost_estimate=cost(0, 600_000),
        name="facing",
    )(info, *fields)


def passive_kernel(planes, info_ref, table_ref, strip_ref, *refs):
    own_refs, (disp_out, stress_out, pull_out, disp_all, field) = refs[:-5], refs[-5:]
    slab, slabs = info_ref[SLAB], planes.slabs
    width = strip_ref.shape[-1]
    own = ROWS - 8
    k = Weights(info_ref[SIDE], own, width)
    reach = REACH + 1

    at = 0
    for ref in own_refs:
        for pos in range(ref.shape[0]):
            for comp in range(ref.shape[1]):
                both = ref[pos, comp]
                field[at, comp] = jnp.concatenate([both[:, :width], both[:, width:], strip_ref[at, comp]], axis=0)
            at += 1

    def plane(comp, offset):
        return field[planes.spot(slab, offset), comp]

    for offset in range(-reach, reach + 1):
        factor = inside(slab, slabs, offset)
        for comp in range(3):
            disp_all[comp, offset + reach] = plane(comp, offset) * factor

    tables = [jnp.broadcast_to(table_ref[comp : comp + 1], (8, 128)) for comp in range(3)]

    def direction(index, comp):
        index = index.astype(jnp.int32)
        rows = []
        for top in range(0, ROWS, 8):
            parts = [
                jnp.take_along_axis(tables[comp], index[top : top + 8, at : at + 128], axis=1, mode="promise_in_bounds")
                for at in range(0, width, 128)
            ]
            rows.append(jnp.concatenate(parts, axis=1))
        return jnp.concatenate(rows, axis=0)

    for step in range(2 * REACH + 1):
        offset = step - REACH
        below, mid, above = ([disp_all[comp, step + shift] for comp in range(3)] for shift in range(3))
        factor = inside(slab, slabs, offset)
        deform = deformation(below, mid, above, k)
        stress = times(deform, passive_stress(deform))
        index = plane(3, offset)
        fdir = [direction(index, comp) for comp in range(3)]
        for i_pos in range(3):
            pull = (ACTIVE_GAIN * factor) * sum(deform[i_pos][b_pos] * fdir[b_pos] for b_pos in range(3))
            for a_pos in range(3):
                stress_out[3 * i_pos + a_pos, step] = stress[i_pos][a_pos] * factor
                pull_out[3 * i_pos + a_pos, step] = pull * fdir[a_pos]
            disp_out[i_pos, step] = mid[i_pos]
            disp_out[3 + i_pos, step] = fdir[i_pos]


def passive_step(info, planes, strips):
    width = strips.shape[-1]
    count = 2 * REACH + 1
    shapes = [(6, count), (9, count), (9, count)]
    vmem = pl.BlockSpec(memory_space=pltpu.VMEM)
    return pl.pallas_call(
        functools.partial(passive_kernel, planes),
        in_specs=[pl.BlockSpec(memory_space=pltpu.SMEM)] + [vmem] * (2 + len(planes.parts)),
        out_shape=[jax.ShapeDtypeStruct((a, b, ROWS, width), jnp.float32) for a, b in shapes],
        scratch_shapes=[
            pltpu.VMEM((3, count + 2, ROWS, width), jnp.float32),
            pltpu.VMEM(strips.shape[:2] + (ROWS, width), jnp.float32),
        ],
        compiler_params=params(),
        cost_estimate=cost(400 * count * ROWS * width, 5_000_000),
        name="passive",
    )(info, fiber_table(), strips, *planes.parts)


def mechanics_kernel(planes, info_ref, disp_ref, stress_ref, pull_ref, *rest):
    active_refs, (disp_out, cond_out, d_one, p_two, active) = rest[:-5], rest[-5:]
    slab, side, slabs = info_ref[SLAB], info_ref[SIDE], planes.slabs
    own, width = disp_out.shape[-2:]
    k = Weights(side, own, width)

    at = 0
    for ref in active_refs:
        active[at : at + ref.shape[0]] = ref[...]
        at += ref.shape[0]

    def active_at(step):
        return active[planes.spot(slab, step - REACH)]

    for step in range(1, 2 * REACH):
        act = [active_at(step + shift) for shift in (-1, 0, 1)]
        factor = inside(slab, slabs, step - REACH)
        for i_pos in range(3):
            stress = [
                [stress_ref[3 * i_pos + a_pos, step + shift] + act[shift + 1] * pull_ref[3 * i_pos + a_pos, step + shift] for a_pos in range(3)]
                for shift in (-1, 0, 1)
            ]
            moved = disp_ref[i_pos, step] + MECH_RATE * force(stress[0], stress[1], stress[2], k)
            d_one[i_pos, step] = moved * factor

    for step in range(2, 2 * REACH - 1):
        disp = [[d_one[comp, step + shift] for comp in range(3)] for shift in (-1, 0, 1)]
        deform = deformation(disp[0], disp[1], disp[2], k)
        second = passive_stress(deform)
        fdir = [disp_ref[3 + comp, step] for comp in range(3)]
        gain = ACTIVE_GAIN * active_at(step)
        for a_pos, b_pos in PAIRS:
            entry = second[a_pos, b_pos] + gain * fdir[a_pos] * fdir[b_pos]
            second[a_pos, b_pos] = entry
            second[b_pos, a_pos] = entry
        stress = times(deform, second)
        factor = inside(slab, slabs, step - REACH)
        for i_pos in range(3):
            for a_pos in range(3):
                p_two[3 * i_pos + a_pos, step] = stress[i_pos][a_pos] * factor

    last = []
    for step in (REACH - 1, REACH, REACH + 1):
        factor = inside(slab, slabs, step - REACH)
        row = []
        for i_pos in range(3):
            stress = [[p_two[3 * i_pos + a_pos, step + shift] for a_pos in range(3)] for shift in (-1, 0, 1)]
            moved = d_one[i_pos, step] + MECH_RATE * force(stress[0], stress[1], stress[2], k)
            row.append(moved * factor)
        last.append(row)
    deform = deformation(last[0], last[1], last[2], k)
    comps = metric(deform, [disp_ref[3 + comp, REACH] for comp in range(3)])
    for i_pos in range(3):
        disp_out[i_pos, 0] = last[1][i_pos][:own]
    for pos, comp in enumerate(comps):
        cond_out[pos, 0] = comp[:own]


def mechanics_step(info, own, planes, window):
    width = planes.parts[0].shape[-1]
    count = 2 * REACH + 1
    held = sum(part.shape[0] for part in planes.parts)
    vmem = pl.BlockSpec(memory_space=pltpu.VMEM)
    return pl.pallas_call(
        functools.partial(mechanics_kernel, planes),
        in_specs=[pl.BlockSpec(memory_space=pltpu.SMEM)] + [vmem] * (3 + len(planes.parts)),
        out_shape=[
            jax.ShapeDtypeStruct((3, 1, own, width), jnp.float32),
            jax.ShapeDtypeStruct((6, 1, own, width), jnp.float32),
        ],
        scratch_shapes=[
            pltpu.VMEM((3, count, ROWS, width), jnp.float32),
            pltpu.VMEM((9, count, ROWS, width), jnp.float32),
            pltpu.VMEM((held, ROWS, width), jnp.float32),
        ],
        compiler_params=params(),
        cost_estimate=cost(400 * count * ROWS * width, 5_000_000),
        name="mechanics",
    )(info, *window, *planes.parts)


def tie(*arrays):
    return lax.optimization_barrier(arrays)


def on_device(states, cond, tension, fiber, disp):
    slabs = lax.axis_size("slab")
    slab, col = lax.axis_index("slab"), lax.axis_index("col")
    _, planes, rows, width = states.shape
    own = rows // 8
    flip = slab % 2
    far_exists = (slab > 0) & (slab < slabs - 1)
    info = jnp.stack([slab, col, flip, far_exists]).astype(jnp.int32)

    pairs = [(i, i ^ 1) for i in range(slabs)]
    others = [(i, i if i in (0, slabs - 1) else ((i + 1) ^ 1) - 1) for i in range(slabs)]
    swap = [(0, 1), (1, 0)]

    tiled = states.reshape(4, planes, own, 8, width)
    fields = Planes(own_field(disp, fiber), slabs, REACH + 1, (1, 4, 2))
    edges, facing = facing_parts(info, tiled)
    edges = lax.ppermute(edges, "col", swap)
    cond_strip = lax.ppermute(facing_cond(info, cond), "col", swap)
    strip = lax.ppermute(facing, "col", swap)
    far, near = first_sends(info, edges, tiled)
    far_halo = lax.ppermute(far, "slab", others)
    near_halo = lax.ppermute(near, "slab", pairs)
    coeffs = fine_coeffs(info, cond, cond_strip)
    whole = jnp.concatenate([tiled, strip[:, :, None]], axis=2)

    far_part, far_inner, far_gates = half_step("first", FAR_HALF, info, (whole,), coeffs)
    near_kind, near_arrays = "first", (whole,)
    for turn_index in range(1, SUB):
        last = turn_index == SUB - 1
        kind = "last" if last else "middle"
        far, far_send = halo_step(FAR_HALF, info, far_part, far_halo, coeffs)
        far_send, *near_arrays = tie(far_send, *near_arrays)
        near_part, near_inner, near_gates = half_step(near_kind, NEAR_HALF, info, near_arrays, coeffs)
        far_halo = lax.ppermute(far_send, "slab", others)
        far_part, far_next, far_gates = half_step(kind, FAR_HALF, info, (far, far_inner, near_inner, far_gates), coeffs)
        if last:
            near_part, far_part, *fields.parts = tie(near_part, far_part, *fields.parts)
        near, near_send = halo_step(NEAR_HALF, info, near_part, near_halo, coeffs)
        near_halo = lax.ppermute(near_send, "slab", pairs)
        fields.round()
        near_kind, near_arrays = kind, (near, near_inner, far_inner, near_gates)
        far_inner = far_next
    near_part, near_inner, near_gates = half_step(near_kind, NEAR_HALF, info, near_arrays, coeffs)
    strips = lax.ppermute(facing_rows(info, fields.parts), "col", swap)
    states_next, tension_next, active = finish_half(
        FAR_HALF, info, far_part, far_inner, far_halo, coeffs, tension, (far_gates, near_inner, near_gates)
    )
    window = passive_step(info, fields, strips)
    states_next, tension_next, active, facing = finish_half(
        NEAR_HALF, info, near_part, near_inner, near_halo, coeffs, tension, (active, states_next, tension_next)
    )
    active_strip = lax.ppermute(facing, "col", swap)
    actives = Planes(jnp.concatenate([active, active_strip], axis=0), slabs, REACH, (4, 1, 2))
    for _ in range(3):
        actives.round()
    disp_next, cond_next = mechanics_step(info, disp.shape[2], actives, window)
    return (states_next.reshape(states.shape), tension_next, disp_next, cond_next)


def solution(mesh):
    in_specs = (
        P(None, ("grp", "slab"), "col", None),
        P(None, ("grp", "slab"), "col", None),
        P(("grp", "slab"), "col", None),
        P(("grp", "slab"), "col", None),
        P(None, ("grp", "slab"), "col", None),
    )
    out_specs = (
        P(None, ("grp", "slab"), "col", None),
        P(("grp", "slab"), "col", None),
        P(None, ("grp", "slab"), "col", None),
        P(None, ("grp", "slab"), "col", None),
    )
    return jax.shard_map(
        on_device, mesh=mesh, in_specs=in_specs, out_specs=out_specs, check_vma=False
    )
```
